128 devices in a mesh: dir: 16 (over z_lo, y, core), freq: 8 (over z_hi, x).
Axes of the slice: x: 4, y: 4, z: 4 (z_hi: 2, z_lo: 2; z = z_hi * 2 + z_lo), core: 2. Of those that a mesh axis runs over, the one named last changes fastest.
Arguments:
- observed: float32 [512, 16, 2, 2, 512], P('dir', 'freq'), as said below
- flags: int32 [512, 2, 512], P('dir'), may hold values from 0 to 1, as said below
- screen: float32 [32, 512], P('dir'), may hold values from -6 to 6
- screen_kernel: float32 [512, 512], replicated
- station_uv: float32 [2, 2, 512], replicated, may hold values from -360 to 360
- source_lm: float32 [2, 6144], P(None, 'dir'), may hold values from -0.05 to 0.05
- source_flux: float32 [6144], P('dir')
- station_gain: bfloat16 [16, 2, 2, 512, 6144], P('freq', None, None, None, 'dir'), may hold values from -4.1875 to 4.1875
- source_direction: int32 [6144], P('dir'), may hold values from 0 to 1
- freq_ratio: float32 [16], P('freq')
Outputs:
- residual: float32 [512, 16, 2, 2, 512], P('dir', 'freq')
- updated_screen: float32 [32, 512], P('dir')
The draws below stay inside these ranges and needn't reach their ends.
Inputs may be any that keep to these rules, and one draw needn't show every extreme that they name: observed is Hermitian in its stations: observed[p, f, t, 0, q] equals observed[q, f, t, 0, p] and observed[p, f, t, 1, q] equals minus observed[q, f, t, 1, p]. flags[p, t, q] equals flags[q, t, p].
All inputs are finite; a program needn't handle non-finite values.
Results may differ from the reference program's by a relative error of at most 0.0037.
Values may be sent and summed in bfloat16 or wider, within the bound.
No kernel may reach another device: no remote copies, remote signals or barrier semaphores. Data moves between devices by JAX's collectives and lax.ppermute only.
A program may use at most 128 MiB of HBM per device.

```python
import math
import jax
import jax.numpy as jnp
from jax import lax

S = 512
DIR_DEV = 2
SRC_DEV = 384
TIMES = 2
DIRS = 32
SOURCES = 6144
FREQS = 16


def draw_observed(key, part):
    key_real, key_imag = jax.random.split(key, 2)
    first = jax.random.normal(key_real, (FREQS, TIMES, S, S), jnp.float32)
    second = jax.random.normal(key_imag, (FREQS, TIMES, S, S), jnp.float32)
    real_part = (first + jnp.swapaxes(first, 2, 3)) * 0.7071
    imag_part = (second - jnp.swapaxes(second, 2, 3)) * 0.7071
    stacked = jnp.stack([real_part, imag_part], axis=2)
    return jnp.transpose(stacked, (3, 0, 1, 2, 4))


def draw_flags(key, part):
    levels = jax.random.randint(key, (TIMES, S, S), 0, 10)
    kept = (levels >= 1).astype(jnp.int32)
    station_ids = jnp.arange(S, dtype=jnp.int32)
    upper = station_ids[:, None] < station_ids[None, :]
    symmetric = jnp.where(upper[None], kept, jnp.swapaxes(kept, 1, 2))
    return jnp.transpose(symmetric, (1, 0, 2))


def draw_screen_kernel(key, part):
    factor = jax.random.normal(key, (S, S), jnp.float32)
    product = jnp.dot(factor, factor.T, precision=lax.Precision.HIGHEST) / S
    return product + 0.5 * jnp.eye(S, dtype=jnp.float32)


def draw_source_flux(key, part):
    position = jnp.arange(SOURCES, dtype=jnp.float32) / (SOURCES - 1)
    slope = 1.0 + 2.0 * position
    base = jnp.exp(jax.random.uniform(key, (SOURCES,), jnp.float32, minval=math.log(0.3), maxval=0.0))
    return base * slope


def draw_freq_ratio(key, part):
    offset = jax.random.uniform(key, (FREQS,), jnp.float32)
    return 0.5 * 3.0 ** ((jnp.arange(FREQS, dtype=jnp.float32) + offset) / FREQS)


def set_ends(drawn, own_key, low, top_value):
    extent = drawn.shape
    place = [jax.random.randint(jax.random.fold_in(own_key, axis), (), 0, extent[axis]) for axis in range(len(extent))]
    drawn = drawn.at[tuple(place)].set(low)
    longest = extent.index(max(extent))
    place[longest] = (place[longest] + 1) % extent[longest]
    return drawn.at[tuple(place)].set(top_value)


def shard_levels(stream_key, extent, cuts, least, top_value):
    factor_of, own = 1.0, jax.random.fold_in(stream_key, 6)
    for dim, shards_of in cuts:
        steps = jnp.exp(jax.random.uniform(jax.random.fold_in(own, dim), (shards_of,), jnp.float32, least / len(cuts), top_value / len(cuts)))
        factor_of = factor_of * jnp.repeat(steps, extent[dim] // shards_of).reshape([-1 if axis == dim else 1 for axis in range(len(extent))])
    return factor_of


def scatter_about(stream_key, dims, deviation, reach, cuts=(), kind=jnp.bfloat16):
    drawn = deviation * jax.random.normal(stream_key, dims, jnp.float32)
    if cuts:
        drawn = drawn * shard_levels(stream_key, dims, cuts, -0.22, 0.18)
    return jnp.clip(drawn, -reach, reach).astype(kind)


def setup_inputs(seed: int = 0) -> dict:
    splits = jax.random.split(jax.random.key(seed), 11)
    observed = draw_observed(jax.random.fold_in(splits[10], 71), 0)
    flags = draw_flags(jax.random.fold_in(splits[10], 71), 0)
    screen = scatter_about(splits[2], (DIRS, S), 1.0, 6.0, ((0, 16),), jnp.float32)
    screen_kernel = draw_screen_kernel(jax.random.fold_in(splits[10], 71), 0)
    station_uv = scatter_about(splits[4], (TIMES, 2, S), 60.0, 360.0, (), jnp.float32)
    source_lm = jnp.clip(jax.random.uniform(splits[5], (2, SOURCES), jnp.float32, -0.05, 0.05) * shard_levels(splits[5], (2, SOURCES), ((1, 16),), -0.4, 0.0), -0.05, 0.05)
    source_flux = draw_source_flux(jax.random.fold_in(splits[10], 71), 0)
    station_gain = scatter_about(splits[7], (FREQS, TIMES, 2, S, SOURCES), 0.7, 4.1875, ((0, 8), (4, 16)))
    source_direction = set_ends(jax.random.randint(splits[8], (SOURCES,), 0, DIR_DEV), jax.random.fold_in(splits[8], 1), 0, DIR_DEV - 1).astype(jnp.int32)
    freq_ratio = draw_freq_ratio(jax.random.fold_in(splits[10], 71), 0)
    return dict(observed=observed, flags=flags, screen=screen, screen_kernel=screen_kernel, station_uv=station_uv, source_lm=source_lm, source_flux=source_flux, station_gain=station_gain, source_direction=source_direction, freq_ratio=freq_ratio)


step_size = 0.3
epsilon = 1e-06
highest = lax.Precision.HIGHEST

def reference(observed, flags, screen, screen_kernel, station_uv, source_lm, source_flux, station_gain, source_direction, freq_ratio):
    sources = source_flux.shape[0]
    scaling = 1.0 / math.sqrt(sources)
    owner_dir = jnp.arange(sources, dtype=jnp.int32) // SRC_DEV * DIR_DEV + source_direction
    onehot_dirs = (owner_dir[:, None] == jnp.arange(DIRS, dtype=jnp.int32)[None, :]).astype(jnp.float32)
    screen_src = jnp.dot(onehot_dirs, screen, precision=highest).T
    amplitude = jnp.sqrt(source_flux)
    station_ids = jnp.arange(S, dtype=jnp.int32)
    cross_baseline = (station_ids[:, None] != station_ids[None, :]).astype(jnp.float32)

    def per_matrix(matrix_index):
        channel = matrix_index // TIMES
        moment = matrix_index % TIMES
        frequency = freq_ratio[channel]
        uv_now = station_uv[moment]
        gain_now = station_gain[channel, moment].astype(jnp.float32)
        geometry = uv_now[0][:, None] * source_lm[0][None, :] + uv_now[1][:, None] * source_lm[1][None, :]
        phase_angle = screen_src / frequency + 2.0 * math.pi * frequency * geometry
        cosine = jnp.cos(phase_angle)
        sine = jnp.sin(phase_angle)
        phasor_re = (amplitude[None, :] * (gain_now[0] * cosine - gain_now[1] * sine)).astype(jnp.bfloat16)
        phasor_im = (amplitude[None, :] * (gain_now[0] * sine + gain_now[1] * cosine)).astype(jnp.bfloat16)
        left_mat = jnp.concatenate([phasor_re, phasor_im], axis=1)
        skew_mat = jnp.concatenate([phasor_im, -phasor_re], axis=1)
        real_part = jnp.dot(left_mat, left_mat.T, preferred_element_type=jnp.float32) * scaling
        imag_part = jnp.dot(skew_mat, left_mat.T, preferred_element_type=jnp.float32) * scaling
        model = jnp.stack([real_part, imag_part], axis=1)
        baseline_keep = flags[:, moment, :].astype(jnp.float32) * cross_baseline
        residual = baseline_keep[:, None, :] * (observed[:, channel, moment] - model)
        resid_half = residual.astype(jnp.bfloat16)
        row_prod = jnp.dot(resid_half[:, 0], left_mat, preferred_element_type=jnp.float32)
        row_prod = row_prod + jnp.dot(resid_half[:, 1], -skew_mat, preferred_element_type=jnp.float32)
        conj_mat = jnp.concatenate([phasor_re, -phasor_im], axis=1)
        dual_mat = jnp.concatenate([phasor_im, phasor_re], axis=1)
        col_prod = jnp.dot(resid_half[:, 0].T, conj_mat, preferred_element_type=jnp.float32)
        col_prod = col_prod + jnp.dot(resid_half[:, 1].T, dual_mat, preferred_element_type=jnp.float32)
        weight_re = row_prod[:, :sources] + col_prod[:, :sources]
        weight_im = row_prod[:, sources:] - col_prod[:, sources:]
        source_grad = phasor_im.astype(jnp.float32) * weight_re - phasor_re.astype(jnp.float32) * weight_im
        grad_now = jnp.dot(source_grad, onehot_dirs, precision=highest).T * (scaling / frequency)
        return (residual, grad_now)
    residuals, grads = lax.map(per_matrix, jnp.arange(FREQS * TIMES, dtype=jnp.int32))
    residual_all = jnp.transpose(residuals.reshape(FREQS, TIMES, S, 2, S), (2, 0, 1, 3, 4))
    gradient = lax.optimization_barrier(jnp.sum(grads, axis=0))
    smooth = jnp.dot(gradient, screen_kernel, precision=highest)
    mean_sq = jnp.mean(smooth * smooth)
    updated = screen - step_size * smooth / jnp.sqrt(mean_sq + epsilon)
    return (residual_all, updated)
```

```python
import functools
import math

import jax
import jax.numpy as jnp
from jax import lax
from jax.experimental import pallas as pl
from jax.experimental.pallas import tpu as pltpu
from jax.sharding import PartitionSpec as P

step_size = 0.3
epsilon = 1e-06
highest = lax.Precision.HIGHEST
bf16 = jnp.bfloat16
f32 = jnp.float32

SIN_COEF = (4.44288292, -7.3082457, 3.60635441, -0.84611289, 0.10982699)
COS_COEF = (1.4142135, -6.97885099, 5.73946117, -1.88356299, 0.31069819)
ROUNDER = 12582912.0
CHUNK = 16
VMEM = 60 * 1024 * 1024
NT = (((1,), (1,)), ((), ()))


def y_partner(rel, y):
    if rel == 0:
        return y
    if rel == 1:
        return y + 1 - 2 * (y % 2)
    if rel == 2:
        return 3 - y
    return (y + 2) % 4


def dir_perm(rel, flip_z=False, flip_core=False):
    pairs = []
    for index in range(16):
        z, y, core = index // 8, (index // 2) % 4, index % 2
        z = 1 - z if flip_z else z
        core = 1 - core if flip_core else core
        pairs.append((index, z * 8 + y_partner(rel, y) * 2 + core))
    return pairs


def phasor_kernel(send, ids, freq, gain, cols, lanes, out):
    moment = pl.program_id(0)
    channel = 1 - ids[0] if send else ids[0]
    ratio = freq[channel]
    along = lanes[0:1, :] * ratio
    across = lanes[1:2, :] * ratio
    amp = jnp.sqrt(lanes[2:3, :])
    second = lanes[3:4, :] > 0.5
    per_turn = 1.0 / (2.0 * math.pi * ratio)
    stations = gain.shape[3]
    sources = gain.shape[4]

    def rows_of(step, carry):
        rows = pl.ds(pl.multiple_of(step * CHUNK, CHUNK), CHUNK)
        col = cols[rows, :]
        u = jnp.where(moment == 0, col[:, 0:1], col[:, 2:3])
        v = jnp.where(moment == 0, col[:, 1:2], col[:, 3:4])
        low = col[:, 4:5] * per_turn
        high = col[:, 5:6] * per_turn
        turns = u * along + v * across + jnp.where(second, high, low)
        turns = turns - ((turns + ROUNDER) - ROUNDER)
        z = turns * turns
        sin_half = SIN_COEF[4]
        cos_half = COS_COEF[4]
        for power in (3, 2, 1, 0):
            sin_half = sin_half * z + SIN_COEF[power]
            cos_half = cos_half * z + COS_COEF[power]
        sin_half = sin_half * turns
        sine = (sin_half * cos_half) * amp
        cosine = (1.0 - sin_half * sin_half) * amp
        gain_re = gain[0, 0, 0, rows, :].astype(f32)
        gain_im = gain[0, 0, 1, rows, :].astype(f32)
        out[0, rows, 0:sources] = (gain_re * cosine - gain_im * sine).astype(bf16)
        out[0, rows, sources : 2 * sources] = (gain_re * sine + gain_im * cosine).astype(bf16)
        return carry

    lax.fori_loop(0, stations // CHUNK, rows_of, 0, unroll=2)
    mask = jnp.broadcast_to(lanes[3:4, :], (16, sources)).astype(bf16)
    out[0, stations : stations + 16, 0:sources] = mask
    out[0, stations : stations + 16, sources : 2 * sources] = mask


def phasor(send, ids, freq, gain, cols, lanes):
    stations, sources = gain.shape[3], gain.shape[4]

    def gain_block(t, ids_ref):
        channel = 1 - ids_ref[0] if send else ids_ref[0]
        return (channel, t, 0, 0, 0)

    return pl.pallas_call(
        functools.partial(phasor_kernel, send),
        grid_spec=pltpu.PrefetchScalarGridSpec(
            num_scalar_prefetch=1,
            grid=(2,),
            in_specs=[
                pl.BlockSpec(memory_space=pltpu.SMEM),
                pl.BlockSpec((1, 1, 2, stations, sources), gain_block),
                pl.BlockSpec(cols.shape, lambda t, ids_ref: (0, 0)),
                pl.BlockSpec(lanes.shape, lambda t, ids_ref: (0, 0)),
            ],
            out_specs=pl.BlockSpec((1, stations + 16, 2 * sources), lambda t, ids_ref: (t, 0, 0)),
        ),
        out_shape=jax.ShapeDtypeStruct((2, stations + 16, 2 * sources), bf16),
        compiler_params=pltpu.CompilerParams(vmem_limit_bytes=VMEM),
        cost_estimate=pl.CostEstimate(
            flops=40 * 2 * stations * sources, bytes_accessed=3200000, transcendentals=0
        ),
        name="phasor_send" if send else "phasor_own",
    )(ids, freq, gain, cols, lanes)


def upper_mask():
    row = lax.broadcasted_iota(jnp.int32, (64, 64), 0)
    col = lax.broadcasted_iota(jnp.int32, (64, 64), 1)
    return row < col, row > col


def pack(re, im, odd, keep_re):
    re = jnp.where(odd, re[:, 64:384], re[:, 0:320])
    im = jnp.where(odd, im[:, 64:384], im[:, 0:320])
    upper, _ = upper_mask()
    own = jnp.where(upper, re[:, 0:64], im[:, 0:64])
    far = jnp.where(keep_re, re[:, 256:320], im[:, 256:320])
    return jnp.concatenate([own, re[:, 64:256], far, im[:, 64:256]], axis=1)


def skewed(q):
    half = q.shape[1] // 2
    return jnp.concatenate([q[:, half:], -q[:, :half]], axis=1)


def mm(a, b):
    return lax.dot_general(a, b, NT, preferred_element_type=f32)


def spread_wide(wide, part, value):
    wide[part, :, 0:512] = value
    wide[part, :, 512:768] = value[:, 0:256]


def block_of(wide, part, chip):
    start = pl.multiple_of((chip // 2) * 128, 128)
    return wide[part, pl.ds(pl.multiple_of(chip * 64, 64), 64), pl.ds(start, 384)]


def model_kernel(scaling, ids, own, other, out0, out1, out2, out3, wide):
    y, z = ids[1], ids[2]
    q_own = own[0, 0:512, :]
    q_other = other[0, 0:512, :]
    spread_wide(wide, 0, (mm(q_own, q_own) + mm(q_other, q_other)) * scaling)
    spread_wide(wide, 1, (mm(skewed(q_own), q_own) + mm(skewed(q_other), q_other)) * scaling)
    for rel, out in enumerate((out0, out1, out2, out3)):
        for flip in range(2):
            zz = 1 - z if flip else z
            chip = zz * 4 + y_partner(rel, y)
            out[flip, 0] = pack(
                block_of(wide, 0, chip), block_of(wide, 1, chip), chip % 2 == 1, zz == 0
            ).astype(out.dtype)


def model_parts(scaling, ids, own, other):
    rows, lanes = own.shape[1], own.shape[2]
    block = pl.BlockSpec((1, rows, lanes), lambda t, ids_ref: (t, 0, 0))
    out = pl.BlockSpec((2, 1, 64, 512), lambda t, ids_ref: (0, t, 0, 0))
    return pl.pallas_call(
        functools.partial(model_kernel, scaling),
        grid_spec=pltpu.PrefetchScalarGridSpec(
            num_scalar_prefetch=1,
            grid=(2,),
            in_specs=[block, block],
            out_specs=[out] * 4,
            scratch_shapes=[pltpu.VMEM((2, 512, 768), f32)],
        ),
        out_shape=[jax.ShapeDtypeStruct((2, 2, 64, 512), f32)]
        + [jax.ShapeDtypeStruct((2, 2, 64, 512), bf16)] * 3,
        compiler_params=pltpu.CompilerParams(vmem_limit_bytes=VMEM),
        cost_estimate=pl.CostEstimate(
            flops=2 * 2 * 4 * 512 * 512 * 768, bytes_accessed=5000000, transcendentals=0
        ),
        name="model_parts",
    )(ids, own, other)


def direction_kernel(ids, own, other, out, whole, first):
    core, y, z = ids[0], ids[1], ids[2]
    for source, core_of in ((own, core), (other, 1 - core)):
        q = source[0, 0:512, :]
        in_first = source[0, 512:513, :] < 0.5
        q_first = jnp.where(in_first, q, jnp.zeros_like(q))
        spread_wide(whole, 0, mm(q, q))
        spread_wide(whole, 1, mm(skewed(q), q))
        spread_wide(first, 0, mm(q_first, q))
        spread_wide(first, 1, mm(skewed(q_first), q))
        for rel in range(4):
            for flip in range(2):
                zz = 1 - z if flip else z
                chip = zz * 4 + y_partner(rel, y)
                re_first, im_first = block_of(first, 0, chip), block_of(first, 1, chip)
                re_rest = block_of(whole, 0, chip) - re_first
                im_rest = block_of(whole, 1, chip) - im_first
                odd = chip % 2 == 1
                out[core_of * 2, rel, flip, 0] = pack(im_first, -re_first, odd, zz == 0).astype(bf16)
                out[core_of * 2 + 1, rel, flip, 0] = pack(im_rest, -re_rest, odd, zz == 0).astype(bf16)


def direction_parts(ids, own, other):
    rows, lanes = own.shape[1], own.shape[2]
    block = pl.BlockSpec((1, rows, lanes), lambda t, ids_ref: (t, 0, 0))
    return pl.pallas_call(
        direction_kernel,
        grid_spec=pltpu.PrefetchScalarGridSpec(
            num_scalar_prefetch=1,
            grid=(2,),
            in_specs=[block, block],
            out_specs=pl.BlockSpec((4, 4, 2, 1, 64, 512), lambda t, ids_ref: (0, 0, 0, t, 0, 0)),
            scratch_shapes=[pltpu.VMEM((2, 512, 768), f32)] * 2,
        ),
        out_shape=jax.ShapeDtypeStruct((4, 4, 2, 2, 64, 512), bf16),
        compiler_params=pltpu.CompilerParams(vmem_limit_bytes=VMEM),
        cost_estimate=pl.CostEstimate(
            flops=2 * 2 * 8 * 512 * 512 * 768, bytes_accessed=8000000, transcendentals=0
        ),
        name="direction_parts",
    )(ids, own, other)


def observed_kernel(ids, own, other, obs_out, keep_out, wide):
    core, y, z = ids[0], ids[1], ids[2]
    for moment in range(2):
        for part in range(3):
            index = moment * 3 + part
            for rows, source in ((core, own), (1 - core, other)):
                place = pl.ds(pl.multiple_of(rows * 32, 32), 32)
                wide[part, place, 0:512] = source[index]
                wide[part, place, 512:768] = source[index, :, 0:256]
        chip = z * 4 + y
        start = pl.ds(pl.multiple_of((chip // 2) * 128, 128), 384)
        odd = chip % 2 == 1
        obs_out[moment] = pack(wide[0, :, start], wide[1, :, start], odd, z == 0)
        keep = pack(wide[2, :, start], wide[2, :, start], odd, z == 0)
        row = lax.broadcasted_iota(jnp.int32, (64, 512), 0)
        col = lax.broadcasted_iota(jnp.int32, (64, 512), 1)
        keep_out[moment] = jnp.where(row == col, 0.0, keep)


def observed_parts(ids, own, other):
    return pl.pallas_call(
        observed_kernel,
        in_specs=[
            pl.BlockSpec(memory_space=pltpu.SMEM),
            pl.BlockSpec(memory_space=pltpu.VMEM),
            pl.BlockSpec(memory_space=pltpu.VMEM),
        ],
        out_specs=[pl.BlockSpec(memory_space=pltpu.VMEM)] * 2,
        out_shape=[jax.ShapeDtypeStruct((2, 64, 512), f32)] * 2,
        scratch_shapes=[pltpu.VMEM((3, 64, 768), f32)],
        cost_estimate=pl.CostEstimate(flops=1000000, bytes_accessed=1500000, transcendentals=0),
        name="observed_parts",
    )(ids, own, other)


def gradient_kernel(scaling, ids, freq, here, one, two, three, parts, out, rows_sum, cols_sum, total):
    core, y, z = ids[0], ids[1], ids[2]
    which = pl.program_id(0)
    for rel, source in enumerate((here, one, two, three)):
        for flip in range(2):
            zz = 1 - z if flip else z
            chip = zz * 4 + y_partner(rel, y)
            product = source[flip, 0].astype(f32) * parts[0, rel, flip, 0].astype(f32)
            product += source[flip, 1].astype(f32) * parts[0, rel, flip, 1].astype(f32)
            rows_sum[pl.ds(pl.multiple_of(chip * 64, 64), 64), :] = (
                product[:, 0:128] + product[:, 128:256] + product[:, 256:384] + product[:, 384:512]
            )
            cols_sum[pl.ds(chip, 1), :] = jnp.sum(product, axis=0, keepdims=True)
    along_rows = jnp.sum(jnp.transpose(rows_sum[...]), axis=0, keepdims=True)
    low = cols_sum[:, 0:256]
    high = cols_sum[:, 256:512]
    near = lax.broadcasted_iota(jnp.int32, (8, 256), 1) < 64
    placed = jnp.concatenate(
        [low + jnp.where(near, 0.0, high), jnp.where(near, high, 0.0)], axis=1
    )
    along_cols = placed[0:1]
    for chip in range(1, 8):
        along_cols += pltpu.roll(placed[chip : chip + 1], 64 * chip, 1)
    grad = (along_rows - along_cols) * (2.0 * scaling / freq[core])
    for piece in range(4):
        total[pl.ds(which * 4 + piece, 1), :] = grad[:, piece * 128 : (piece + 1) * 128]

    @pl.when(which == 3)
    def _():
        value = total[...].astype(bf16)

        def copy(index, carry):
            out[index] = value
            return carry

        lax.fori_loop(0, out.shape[0], copy, 0, unroll=8)


def gradient_parts(scaling, devices, ids, freq, here, one, two, three, parts):
    resid = pl.BlockSpec((2, 2, 64, 512), lambda d, ids_ref: (0, 0, 0, 0))
    return pl.pallas_call(
        functools.partial(gradient_kernel, scaling),
        grid_spec=pltpu.PrefetchScalarGridSpec(
            num_scalar_prefetch=1,
            grid=(4,),
            in_specs=[pl.BlockSpec(memory_space=pltpu.SMEM)]
            + [resid] * 4
            + [pl.BlockSpec((1, 4, 2, 2, 64, 512), lambda d, ids_ref: (d, 0, 0, 0, 0, 0))],
            out_specs=pl.BlockSpec((devices, 16, 128), lambda d, ids_ref: (0, 0, 0)),
            scratch_shapes=[
                pltpu.VMEM((512, 128), f32),
                pltpu.VMEM((8, 512), f32),
                pltpu.VMEM((16, 128), f32),
            ],
        ),
        out_shape=jax.ShapeDtypeStruct((devices, 16, 128), bf16),
        compiler_params=pltpu.CompilerParams(vmem_limit_bytes=VMEM),
        cost_estimate=pl.CostEstimate(flops=10000000, bytes_accessed=6000000, transcendentals=0),
        name="gradient_parts",
    )(ids, freq, here, one, two, three, parts)


def rows_kernel(ids, resid, here, one, two, three, own_out, other_out, rolled):
    core, y, z = ids[0], ids[1], ids[2]
    chip = z * 4 + y
    upper, lower = upper_mask()
    even = y % 2 == 0
    flip5 = jnp.where(y < 3, 1, 0)
    flip6 = jnp.where(y < 2, 1, 0)
    flip7 = jnp.where(y < 1, 1, 0)
    for moment in range(2):
        own = resid[moment]
        near = own[:, 0:64]
        near_t = jnp.transpose(near)
        zero = jnp.zeros_like(near)
        near_re = jnp.where(upper, near, jnp.where(lower, near_t, zero))
        near_im = jnp.where(lower, near, jnp.where(upper, -near_t, zero))
        far = own[:, 256:320]
        far_t = jnp.transpose(here[1, moment][:, 256:320].astype(f32))
        far_re = jnp.where(z == 0, far, far_t)
        far_im = jnp.where(z == 0, -far_t, far)
        block5 = jnp.where(even, one[flip5, moment].astype(f32), two[flip5, moment].astype(f32))
        block6 = three[flip6, moment].astype(f32)
        block7 = jnp.where(even, two[flip7, moment].astype(f32), one[flip7, moment].astype(f32))
        re = [near_re, own[:, 64:256], far_re]
        im = [near_im, own[:, 320:512], far_im]
        for block, offset in ((block5, 3), (block6, 2), (block7, 1)):
            re.append(jnp.transpose(block[:, 64 * offset : 64 * offset + 64]))
            im.append(-jnp.transpose(block[:, 256 + 64 * offset : 320 + 64 * offset]))
        for part, pieces in enumerate((re, im)):
            index = moment * 2 + part
            rolled[index] = pltpu.roll(jnp.concatenate(pieces, axis=1), chip * 64, 1)
            own_out[index] = rolled[index, pl.ds(pl.multiple_of(core * 32, 32), 32), :]
            other_out[index] = rolled[index, pl.ds(pl.multiple_of((1 - core) * 32, 32), 32), :]


def whole_rows(ids, resid, here, one, two, three):
    return pl.pallas_call(
        rows_kernel,
        in_specs=[pl.BlockSpec(memory_space=pltpu.SMEM)]
        + [pl.BlockSpec(memory_space=pltpu.VMEM)] * 5,
        out_specs=[pl.BlockSpec(memory_space=pltpu.VMEM)] * 2,
        out_shape=[jax.ShapeDtypeStruct((4, 32, 512), f32)] * 2,
        scratch_shapes=[pltpu.VMEM((4, 64, 512), f32)],
        cost_estimate=pl.CostEstimate(flops=2000000, bytes_accessed=1500000, transcendentals=0),
        name="whole_rows",
    )(ids, resid, here, one, two, three)


def update_kernel(ids, grads, kernel, screen, out, total, smooth):
    per_chip = grads.shape[0] // 8
    for chip in range(8):
        total[chip * 16 : chip * 16 + 16, :] = jnp.sum(
            grads[chip * per_chip : (chip + 1) * per_chip].astype(f32), axis=0
        )
    gradient = jnp.concatenate(
        [total[pl.ds(piece, 32, stride=4), :] for piece in range(4)], axis=1
    )
    value = jnp.dot(gradient, kernel[...], precision=highest, preferred_element_type=f32)
    mean_sq = jnp.sum(value * value) / value.size
    smooth[...] = value * (step_size * lax.rsqrt(mean_sq + epsilon))
    row = (ids[2] * 4 + ids[1]) * 4 + ids[0] * 2
    for step in range(2):
        out[step : step + 1, :] = screen[step : step + 1, :] - smooth[pl.ds(row + step, 1), :]


def updated_rows(ids, grads, kernel, screen):
    return pl.pallas_call(
        update_kernel,
        in_specs=[pl.BlockSpec(memory_space=pltpu.SMEM)]
        + [pl.BlockSpec(memory_space=pltpu.VMEM)] * 3,
        out_specs=pl.BlockSpec(memory_space=pltpu.VMEM),
        out_shape=jax.ShapeDtypeStruct(screen.shape, f32),
        scratch_shapes=[pltpu.VMEM((128, 128), f32), pltpu.VMEM((32, 512), f32)],
        cost_estimate=pl.CostEstimate(flops=200000000, bytes_accessed=1500000, transcendentals=0),
        name="updated_rows",
    )(ids, grads, kernel, screen)


def body(
    observed,
    flags,
    screen,
    screen_kernel,
    station_uv,
    source_lm,
    source_flux,
    station_gain,
    source_direction,
    freq_ratio,
):
    devices = lax.axis_size("dir") * lax.axis_size("freq")
    stations = screen.shape[1]
    scaling = 1.0 / math.sqrt(source_flux.shape[0] * lax.axis_size("dir"))
    index = lax.axis_index("dir")
    core = index % 2
    y = (index // 2) % 4
    z = index // 8
    ids = jnp.stack([core, y, z]).astype(jnp.int32)
    cols = jnp.concatenate(
        [station_uv.reshape(4, stations), screen, jnp.zeros((2, stations), f32)], axis=0
    ).T
    lanes = jnp.concatenate(
        [source_lm, source_flux[None], source_direction.astype(f32)[None], jnp.zeros((4, source_flux.shape[0]), f32)],
        axis=0,
    )
    swap = functools.partial(lax.ppermute, axis_name="dir", perm=dir_perm(0, flip_core=True))

    sent = phasor(True, ids, freq_ratio, station_gain, cols, lanes)
    other = swap(sent)
    own = phasor(False, ids, freq_ratio, station_gain, cols, lanes)

    keep = flags.astype(f32)[:, None, :, None, :]
    keep = jnp.broadcast_to(keep, (32, 2, 2, 1, stations))
    rows = jnp.concatenate([observed, keep], axis=3)
    rows = jnp.transpose(rows, (1, 2, 3, 0, 4)).reshape(2, 6, 32, stations)
    rows_own = lax.dynamic_index_in_dim(rows, core, 0, keepdims=False)
    rows_sent = lax.dynamic_index_in_dim(rows, 1 - core, 0, keepdims=False)
    rows_other = swap(rows_sent)
    obs, kept = observed_parts(ids, rows_own, rows_other)

    part0, part1, part2, part3 = model_parts(scaling, ids, own, other)
    got = [
        lax.ppermute(part, "dir", dir_perm(rel)) for rel, part in ((3, part3), (2, part2), (1, part1))
    ]
    directions = direction_parts(ids, own, other)
    summed = part0 + got[0].astype(f32) + got[1].astype(f32) + got[2].astype(f32)
    last = lax.ppermute(summed[1].astype(bf16), "dir", dir_perm(0, flip_z=True))
    resid = kept * (obs - (summed[0] + last.astype(f32)))
    half = resid.astype(bf16)
    here = jnp.stack([half, lax.ppermute(half, "dir", dir_perm(0, flip_z=True))])
    three = lax.ppermute(here, "dir", dir_perm(3))
    two = lax.ppermute(here, "dir", dir_perm(2))
    one = lax.ppermute(here, "dir", dir_perm(1))

    grads = gradient_parts(scaling, devices, ids, freq_ratio, here, one, two, three, directions)
    own_rows, sent_rows = whole_rows(ids, resid, here, one, two, three)
    other_rows = swap(sent_rows)
    grads = lax.all_to_all(grads, ("dir", "freq"), 0, 0, tiled=True)
    updated = updated_rows(ids, grads, screen_kernel, screen)

    first = jnp.where(core == 0, own_rows, other_rows)
    second = jnp.where(core == 0, other_rows, own_rows)
    residual = jnp.stack([first, second]).reshape(2, 2, 2, 32, stations)
    return jnp.transpose(residual, (3, 0, 1, 2, 4)), updated


def solution(mesh):
    placed = (
        P("dir", "freq", None, None, None),
        P("dir", None, None),
        P("dir", None),
        P(),
        P(),
        P(None, "dir"),
        P("dir"),
        P("freq", None, None, None, "dir"),
        P("dir"),
        P("freq"),
    )
    return jax.shard_map(
        body,
        mesh=mesh,
        in_specs=placed,
        out_specs=(P("dir", "freq", None, None, None), P("dir", None)),
        check_vma=False,
    )
```

```python
import functools
import math

import jax
import jax.numpy as jnp
from jax import lax
from jax.experimental import pallas as pl
from jax.experimental.pallas import tpu as pltpu
from jax.sharding import PartitionSpec as P

step_size = 0.3
epsilon = 1e-06
highest = lax.Precision.HIGHEST
bf16 = jnp.bfloat16
f32 = jnp.float32

SIN_COEF = (4.44288292, -7.3082457, 3.60635441, -0.84611289, 0.10982699)
COS_COEF = (1.4142135, -6.97885099, 5.73946117, -1.88356299, 0.31069819)
ROUNDER = 12582912.0
CHUNK = 32
MIB = 1024 * 1024
NT = (((1,), (1,)), ((), ()))


def y_partner(rel, y):
    if rel == 0:
        return y
    if rel == 1:
        return y + 1 - 2 * (y % 2)
    if rel == 2:
        return 3 - y
    return (y + 2) % 4


def dir_perm(rel, flip_z=False, flip_core=False):
    pairs = []
    for index in range(16):
        z, y, core = index // 8, (index // 2) % 4, index % 2
        z = 1 - z if flip_z else z
        core = 1 - core if flip_core else core
        pairs.append((index, z * 8 + y_partner(rel, y) * 2 + core))
    return pairs


ANY = pl.BlockSpec(memory_space=pl.ANY)
WHOLE = pl.BlockSpec(memory_space=pltpu.VMEM)
SCALARS = pl.BlockSpec(memory_space=pltpu.SMEM)


def position():
    index = lax.axis_index("dir")
    return index % 2, (index // 2) % 4, index // 8


def phasor_kernel(send, freq, gain, uv, screen, lm, flux, direction, out, held, sems):
    core, _, _ = position()
    channel = 1 - core if send else core
    stations, sources = gain.shape[3], gain.shape[4]
    half = stations // 2
    copies = []
    for moment in range(2):
        for part in range(2):
            rows = pl.ds(part * half, half)
            copies.append(
                pltpu.make_async_copy(
                    gain.at[channel, moment, :, rows, :],
                    held.at[moment, :, rows, :],
                    sems.at[moment * 2 + part],
                )
            )
    for copy in copies:
        copy.start()
    ratio = freq[channel]
    along = lm[0:1, :] * ratio
    across = lm[1:2, :] * ratio
    amp = jnp.sqrt(flux[...])
    second = direction[...] > 0
    per_turn = 1.0 / (2.0 * math.pi * ratio)
    by_station = jnp.concatenate(
        [uv[0], uv[1], screen[...] * per_turn, jnp.zeros((2, stations), f32)], axis=0
    )
    cols = jnp.transpose(by_station)
    mask = jnp.broadcast_to(jnp.where(second, 1.0, 0.0), (16, sources)).astype(bf16)
    for moment in range(2):
        for start in range(0, stations, CHUNK):
            if start % half == 0:
                copies[moment * 2 + start // half].wait()
            rows = slice(start, start + CHUNK)
            col = cols[rows]
            u = col[:, 2 * moment : 2 * moment + 1]
            v = col[:, 2 * moment + 1 : 2 * moment + 2]
            turns = u * along + v * across + jnp.where(second, col[:, 5:6], col[:, 4:5])
            turns = turns - ((turns + ROUNDER) - ROUNDER)
            z = turns * turns
            sin_half = SIN_COEF[4]
            cos_half = COS_COEF[4]
            for power in (3, 2, 1, 0):
                sin_half = sin_half * z + SIN_COEF[power]
                cos_half = cos_half * z + COS_COEF[power]
            sin_half = sin_half * turns
            sin_amp = sin_half * amp
            sine = sin_amp * cos_half
            cosine = amp - sin_amp * sin_half
            gain_re = held[moment, 0, rows, :].astype(f32)
            gain_im = held[moment, 1, rows, :].astype(f32)
            out[moment, rows, 0:sources] = (gain_re * cosine - gain_im * sine).astype(bf16)
            out[moment, rows, sources : 2 * sources] = (
                gain_re * sine + gain_im * cosine
            ).astype(bf16)
        out[moment, stations : stations + 16, 0:sources] = mask
        out[moment, stations : stations + 16, sources : 2 * sources] = mask


def phasor(send, freq, gain, uv, screen, lm, flux, direction):
    stations, sources = gain.shape[3], gain.shape[4]
    return pl.pallas_call(
        functools.partial(phasor_kernel, send),
        in_specs=[SCALARS, ANY] + [WHOLE] * 5,
        out_specs=WHOLE,
        out_shape=jax.ShapeDtypeStruct((2, stations + 16, 2 * sources), bf16),
        scratch_shapes=[
            pltpu.VMEM((2, 2, stations, sources), bf16),
            pltpu.SemaphoreType.DMA((4,)),
        ],
        compiler_params=pltpu.CompilerParams(vmem_limit_bytes=12 * MIB),
        cost_estimate=pl.CostEstimate(
            flops=40 * 2 * stations * sources, bytes_accessed=3200000, transcendentals=0
        ),
        name="phasor_send" if send else "phasor_own",
    )(freq, gain, uv, screen, lm, flux, direction)


def upper_mask():
    row = lax.broadcasted_iota(jnp.int32, (64, 64), 0)
    col = lax.broadcasted_iota(jnp.int32, (64, 64), 1)
    return row < col, row > col


def pack(re, im, odd, keep_re):
    re = jnp.where(odd, re[:, 64:384], re[:, 0:320])
    im = jnp.where(odd, im[:, 64:384], im[:, 0:320])
    upper, _ = upper_mask()
    own = jnp.where(upper, re[:, 0:64], im[:, 0:64])
    far = jnp.where(keep_re, re[:, 256:320], im[:, 256:320])
    return jnp.concatenate([own, re[:, 64:256], far, im[:, 64:256]], axis=1)


def skewed(q):
    half = q.shape[1] // 2
    return jnp.concatenate([q[:, half:], -q[:, :half]], axis=1)


def mm(a, b):
    return lax.dot_general(a, b, NT, preferred_element_type=f32)


def spread_wide(wide, part, value):
    wide[part, :, 0:512] = value
    wide[part, :, 512:768] = value[:, 0:256]


def block_of(wide, part, chip):
    start = pl.multiple_of((chip // 2) * 128, 128)
    return wide[part, pl.ds(pl.multiple_of(chip * 64, 64), 64), pl.ds(start, 384)]


def model_kernel(scaling, own, other, out0, out1, out2, out3, wide):
    _, y, z = position()
    for moment in range(2):
        q_own = own[moment, 0:512, :]
        q_other = other[moment, 0:512, :]
        spread_wide(wide, 0, (mm(q_own, q_own) + mm(q_other, q_other)) * scaling)
        spread_wide(wide, 1, (mm(skewed(q_own), q_own) + mm(skewed(q_other), q_other)) * scaling)
        for rel, out in enumerate((out0, out1, out2, out3)):
            for flip in range(2):
                zz = 1 - z if flip else z
                chip = zz * 4 + y_partner(rel, y)
                out[flip, moment] = pack(
                    block_of(wide, 0, chip), block_of(wide, 1, chip), chip % 2 == 1, zz == 0
                ).astype(out.dtype)


def model_parts(scaling, own, other):
    return pl.pallas_call(
        functools.partial(model_kernel, scaling),
        in_specs=[WHOLE] * 2,
        out_specs=[WHOLE] * 4,
        scratch_shapes=[pltpu.VMEM((2, 512, 768), f32)],
        out_shape=[jax.ShapeDtypeStruct((2, 2, 64, 512), f32)]
        + [jax.ShapeDtypeStruct((2, 2, 64, 512), bf16)] * 3,
        compiler_params=pltpu.CompilerParams(vmem_limit_bytes=16 * MIB),
        cost_estimate=pl.CostEstimate(
            flops=2 * 2 * 4 * 512 * 512 * 768, bytes_accessed=5000000, transcendentals=0
        ),
        name="model_parts",
    )(own, other)


def direction_kernel(moment, own, other, out, whole, first):
    core, y, z = position()
    for source, core_of in ((own, core), (other, 1 - core)):
        q = source[moment, 0:512, :]
        in_first = source[moment, 512:513, :] < 0.5
        q_first = jnp.where(in_first, q, jnp.zeros_like(q))
        spread_wide(whole, 0, mm(q, q))
        spread_wide(whole, 1, mm(skewed(q), q))
        spread_wide(first, 0, mm(q_first, q))
        spread_wide(first, 1, mm(skewed(q_first), q))
        for rel in range(4):
            for flip in range(2):
                zz = 1 - z if flip else z
                chip = zz * 4 + y_partner(rel, y)
                odd = chip % 2 == 1
                keep_im = zz == 0
                all_of = pack(block_of(whole, 1, chip), -block_of(whole, 0, chip), odd, keep_im)
                first_of = pack(block_of(first, 1, chip), -block_of(first, 0, chip), odd, keep_im)
                out[core_of * 2, rel, flip] = first_of.astype(bf16)
                out[core_of * 2 + 1, rel, flip] = (all_of - first_of).astype(bf16)


def direction_parts(moment, own, other):
    return pl.pallas_call(
        functools.partial(direction_kernel, moment),
        in_specs=[WHOLE] * 2,
        out_specs=WHOLE,
        scratch_shapes=[pltpu.VMEM((2, 512, 768), f32)] * 2,
        out_shape=jax.ShapeDtypeStruct((4, 4, 2, 64, 512), bf16),
        compiler_params=pltpu.CompilerParams(vmem_limit_bytes=18 * MIB),
        cost_estimate=pl.CostEstimate(
            flops=2 * 8 * 512 * 512 * 768, bytes_accessed=5000000, transcendentals=0
        ),
        name="direction_parts%d" % moment,
    )(own, other)


def sum_kernel(own, one, two, three, _, stay, send):
    for flip, out in ((0, stay), (1, send)):
        out[...] = (
            own[flip] + one[flip].astype(f32) + two[flip].astype(f32) + three[flip].astype(f32)
        ).astype(out.dtype)


def sum_parts(own, one, two, three, after):
    return pl.pallas_call(
        sum_kernel,
        in_specs=[WHOLE] * 4 + [ANY],
        out_specs=[WHOLE] * 2,
        out_shape=[
            jax.ShapeDtypeStruct(own.shape[1:], f32),
            jax.ShapeDtypeStruct(own.shape[1:], bf16),
        ],
        compiler_params=pltpu.CompilerParams(vmem_limit_bytes=4 * MIB),
        cost_estimate=pl.CostEstimate(flops=500000, bytes_accessed=2500000, transcendentals=0),
        name="sum_parts",
    )(own, one, two, three, after)


def observed_kernel(own, other, obs_out, keep_out, wide):
    core, y, z = position()
    for moment in range(2):
        for part in range(3):
            index = moment * 3 + part
            for rows, source in ((core, own), (1 - core, other)):
                place = pl.ds(pl.multiple_of(rows * 32, 32), 32)
                wide[part, place, 0:512] = source[index]
                wide[part, place, 512:768] = source[index, :, 0:256]
        chip = z * 4 + y
        start = pl.ds(pl.multiple_of((chip // 2) * 128, 128), 384)
        odd = chip % 2 == 1
        obs_out[moment] = pack(wide[0, :, start], wide[1, :, start], odd, z == 0)
        keep = pack(wide[2, :, start], wide[2, :, start], odd, z == 0)
        row = lax.broadcasted_iota(jnp.int32, (64, 512), 0)
        col = lax.broadcasted_iota(jnp.int32, (64, 512), 1)
        keep_out[moment] = jnp.where(row == col, 0.0, keep)


def observed_parts(own, other):
    return pl.pallas_call(
        observed_kernel,
        in_specs=[WHOLE] * 2,
        out_specs=[WHOLE] * 2,
        out_shape=[jax.ShapeDtypeStruct((2, 64, 512), f32)] * 2,
        scratch_shapes=[pltpu.VMEM((3, 64, 768), f32)],
        cost_estimate=pl.CostEstimate(flops=1000000, bytes_accessed=1500000, transcendentals=0),
        compiler_params=pltpu.CompilerParams(vmem_limit_bytes=4 * MIB),
        name="observed_parts",
    )(own, other)


def gradient_kernel(scaling, freq, here, one, two, three, parts0, parts1, out, rows_sum, cols_sum):
    core, y, z = position()
    for rel, source in enumerate((here, one, two, three)):
        for flip in range(2):
            zz = 1 - z if flip else z
            chip = zz * 4 + y_partner(rel, y)
            for start in range(0, 64, 32):
                rows = slice(start, start + 32)
                resid0 = source[flip, 0, rows, :].astype(f32)
                resid1 = source[flip, 1, rows, :].astype(f32)
                for which in range(4):
                    product = resid0 * parts0[which, rel, flip, rows, :].astype(f32)
                    product += resid1 * parts1[which, rel, flip, rows, :].astype(f32)
                    rows_sum[which, pl.ds(pl.multiple_of(chip * 64 + start, 32), 32), :] = (
                        product[:, 0:128] + product[:, 128:256]
                    ) + (product[:, 256:384] + product[:, 384:512])
                    column = (product[0:8] + product[8:16]) + (product[16:24] + product[24:32])
                    if start == 0:
                        cols_sum[which, chip] = column
                    else:
                        cols_sum[which, chip] += column
    near = lax.broadcasted_iota(jnp.int32, (8, 256), 1) < 64
    factor = 2.0 * scaling / freq[core]
    pieces = []
    for which in range(4):
        placed = []
        for odd in range(2):
            total = None
            for chip in range(odd, 8, 2):
                low = cols_sum[which, chip, :, 0:256]
                high = cols_sum[which, chip, :, 256:512]
                folded = [low + jnp.where(near, 0.0, high), jnp.where(near, high, 0.0)]
                quarters = [part[:, at : at + 128] for part in folded for at in (0, 128)]
                turn = (4 - chip // 2) % 4
                quarters = quarters[turn:] + quarters[:turn]
                total = quarters if total is None else [a + b for a, b in zip(total, quarters)]
            placed.append(jnp.concatenate(total, axis=1))
        columns = placed[0] + pltpu.roll(placed[1], 64, 1)
        along_rows = jnp.sum(jnp.transpose(rows_sum[which]), axis=0, keepdims=True)
        grad = (along_rows - jnp.sum(columns, axis=0, keepdims=True)) * factor
        pieces.extend(grad[:, at : at + 128] for at in range(0, 512, 128))
    value = jnp.concatenate(pieces, axis=0).astype(bf16)

    def copy(index, carry):
        out[index] = value
        return carry

    lax.fori_loop(0, out.shape[0], copy, 0, unroll=8)


def gradient_parts(scaling, devices, freq, here, one, two, three, parts0, parts1):
    return pl.pallas_call(
        functools.partial(gradient_kernel, scaling),
        in_specs=[SCALARS] + [WHOLE] * 6,
        out_specs=WHOLE,
        scratch_shapes=[pltpu.VMEM((4, 512, 128), f32), pltpu.VMEM((4, 8, 8, 512), f32)],
        out_shape=jax.ShapeDtypeStruct((devices, 16, 128), bf16),
        compiler_params=pltpu.CompilerParams(vmem_limit_bytes=12 * MIB),
        cost_estimate=pl.CostEstimate(flops=10000000, bytes_accessed=6000000, transcendentals=0),
        name="gradient_parts",
    )(freq, here, one, two, three, parts0, parts1)


def rows_kernel(resid, here, one, two, three, _, own_out, other_out, rolled):
    core, y, z = position()
    chip = z * 4 + y
    upper, lower = upper_mask()
    even = y % 2 == 0
    flip5 = jnp.where(y < 3, 1, 0)
    flip6 = jnp.where(y < 2, 1, 0)
    flip7 = jnp.where(y < 1, 1, 0)
    for moment in range(2):
        own = resid[moment]
        near = own[:, 0:64]
        near_t = jnp.transpose(near)
        zero = jnp.zeros_like(near)
        near_re = jnp.where(upper, near, jnp.where(lower, near_t, zero))
        near_im = jnp.where(lower, near, jnp.where(upper, -near_t, zero))
        far = own[:, 256:320]
        far_t = jnp.transpose(here[1, moment][:, 256:320].astype(f32))
        far_re = jnp.where(z == 0, far, far_t)
        far_im = jnp.where(z == 0, -far_t, far)
        block5 = jnp.where(even, one[flip5, moment].astype(f32), two[flip5, moment].astype(f32))
        block6 = three[flip6, moment].astype(f32)
        block7 = jnp.where(even, two[flip7, moment].astype(f32), one[flip7, moment].astype(f32))
        re = [near_re, own[:, 64:256], far_re]
        im = [near_im, own[:, 320:512], far_im]
        for block, offset in ((block5, 3), (block6, 2), (block7, 1)):
            re.append(jnp.transpose(block[:, 64 * offset : 64 * offset + 64]))
            im.append(-jnp.transpose(block[:, 256 + 64 * offset : 320 + 64 * offset]))
        for part, pieces in enumerate((re, im)):
            index = moment * 2 + part
            rolled[index] = pltpu.roll(jnp.concatenate(pieces, axis=1), chip * 64, 1)
            own_out[index] = rolled[index, pl.ds(pl.multiple_of(core * 32, 32), 32), :]
            other_out[index] = rolled[index, pl.ds(pl.multiple_of((1 - core) * 32, 32), 32), :]


def whole_rows(resid, here, one, two, three, after):
    return pl.pallas_call(
        rows_kernel,
        in_specs=[WHOLE] * 5 + [ANY],
        out_specs=[WHOLE] * 2,
        out_shape=[jax.ShapeDtypeStruct((4, 32, 512), f32)] * 2,
        scratch_shapes=[pltpu.VMEM((4, 64, 512), f32)],
        cost_estimate=pl.CostEstimate(flops=2000000, bytes_accessed=1500000, transcendentals=0),
        compiler_params=pltpu.CompilerParams(vmem_limit_bytes=6 * MIB),
        name="whole_rows",
    )(resid, here, one, two, three, after)


def halves(value):
    high = value.astype(bf16)
    return high, (value - high.astype(f32)).astype(bf16)


def update_kernel(grads, kernel, screen, out, total, smooth):
    core, y, z = position()
    per_chip = grads.shape[0] // 8
    for chip in range(8):
        total[chip * 16 : chip * 16 + 16, :] = jnp.sum(
            grads[chip * per_chip : (chip + 1) * per_chip].astype(f32), axis=0
        )
    gradient = jnp.concatenate(
        [total[pl.ds(piece, 32, stride=4), :] for piece in range(4)], axis=1
    )
    grad_high, grad_low = halves(gradient)
    kern_high, kern_low = halves(kernel[...])
    both = jnp.dot(
        jnp.concatenate([grad_high, grad_low], axis=0), kern_high, preferred_element_type=f32
    )
    value = both[0:32] + (
        both[32:64] + jnp.dot(grad_high, kern_low, preferred_element_type=f32)
    )
    mean_sq = jnp.sum(value * value) / value.size
    smooth[...] = value * (step_size * lax.rsqrt(mean_sq + epsilon))
    row = (z * 4 + y) * 4 + core * 2
    for step in range(2):
        out[step : step + 1, :] = screen[step : step + 1, :] - smooth[pl.ds(row + step, 1), :]


def updated_rows(grads, kernel, screen):
    return pl.pallas_call(
        update_kernel,
        in_specs=[WHOLE] * 3,
        out_specs=WHOLE,
        out_shape=jax.ShapeDtypeStruct(screen.shape, f32),
        scratch_shapes=[pltpu.VMEM((128, 128), f32), pltpu.VMEM((32, 512), f32)],
        compiler_params=pltpu.CompilerParams(vmem_limit_bytes=8 * MIB),
        cost_estimate=pl.CostEstimate(flops=200000000, bytes_accessed=1500000, transcendentals=0),
        name="updated_rows",
    )(grads, kernel, screen)


def body(
    observed,
    flags,
    screen,
    screen_kernel,
    station_uv,
    source_lm,
    source_flux,
    station_gain,
    source_direction,
    freq_ratio,
):
    devices = lax.axis_size("dir") * lax.axis_size("freq")
    stations = screen.shape[1]
    scaling = 1.0 / math.sqrt(source_flux.shape[0] * lax.axis_size("dir"))
    core = position()[0]
    swap = functools.partial(lax.ppermute, axis_name="dir", perm=dir_perm(0, flip_core=True))

    inputs = (
        freq_ratio,
        station_gain,
        station_uv,
        screen,
        source_lm,
        source_flux[None],
        source_direction[None],
    )
    sent = phasor(True, *inputs)
    other = swap(sent)
    own = phasor(False, *inputs)

    keep = flags.astype(f32)[:, None, :, None, :]
    keep = jnp.broadcast_to(keep, (32, 2, 2, 1, stations))
    rows = jnp.concatenate([observed, keep], axis=3)
    rows = jnp.transpose(rows, (1, 2, 3, 0, 4)).reshape(2, 6, 32, stations)
    rows_own = lax.dynamic_index_in_dim(rows, core, 0, keepdims=False)
    rows_sent = lax.dynamic_index_in_dim(rows, 1 - core, 0, keepdims=False)
    rows_other = swap(rows_sent)
    obs, kept = observed_parts(rows_own, rows_other)

    part0, part1, part2, part3 = model_parts(scaling, own, other)
    got = [
        lax.ppermute(part, "dir", dir_perm(rel)) for rel, part in ((1, part1), (2, part2), (3, part3))
    ]
    directions0 = direction_parts(0, own, other)
    stay, send = sum_parts(part0, *got, directions0)
    last = lax.ppermute(send, "dir", dir_perm(0, flip_z=True))
    resid = kept * (obs - (stay + last.astype(f32)))
    half = resid.astype(bf16)
    here = jnp.stack([half, lax.ppermute(half, "dir", dir_perm(0, flip_z=True))])
    three = lax.ppermute(here, "dir", dir_perm(3))
    two = lax.ppermute(here, "dir", dir_perm(2))
    one = lax.ppermute(here, "dir", dir_perm(1))
    directions1 = direction_parts(1, own, other)

    grads = gradient_parts(
        scaling, devices, freq_ratio, here, one, two, three, directions0, directions1
    )
    own_rows, sent_rows = whole_rows(resid, here, one, two, three, grads)
    other_rows = swap(sent_rows)
    grads = lax.all_to_all(grads, ("dir", "freq"), 0, 0, tiled=True)
    updated = updated_rows(grads, screen_kernel, screen)

    first = jnp.where(core == 0, own_rows, other_rows)
    second = jnp.where(core == 0, other_rows, own_rows)
    residual = jnp.stack([first, second]).reshape(2, 2, 2, 32, stations)
    return jnp.transpose(residual, (3, 0, 1, 2, 4)), updated


def solution(mesh):
    placed = (
        P("dir", "freq", None, None, None),
        P("dir", None, None),
        P("dir", None),
        P(),
        P(),
        P(None, "dir"),
        P("dir"),
        P("freq", None, None, None, "dir"),
        P("dir"),
        P("freq"),
    )
    return jax.shard_map(
        body,
        mesh=mesh,
        in_specs=placed,
        out_specs=(P("dir", "freq", None, None, None), P("dir", None)),
        check_vma=False,
    )
```

```python
import functools
import math

import jax
import jax.numpy as jnp
from jax import lax
from jax.experimental import pallas as pl
from jax.experimental.pallas import tpu as pltpu
from jax.sharding import PartitionSpec as P

step_size = 0.3
epsilon = 1e-06
highest = lax.Precision.HIGHEST
bf16 = jnp.bfloat16
f32 = jnp.float32

SIN_COEF = (4.44288292, -7.3082457, 3.60635441, -0.84611289, 0.10982699)
COS_COEF = (1.4142135, -6.97885099, 5.73946117, -1.88356299, 0.31069819)
ROUNDER = 12582912.0
CHUNK = 32
MIB = 1024 * 1024
NT = (((1,), (1,)), ((), ()))


def y_partner(rel, y):
    if rel == 0:
        return y
    if rel == 1:
        return y + 1 - 2 * (y % 2)
    if rel == 2:
        return 3 - y
    return (y + 2) % 4


def dir_perm(rel, flip_z=False, flip_core=False):
    pairs = []
    for index in range(16):
        z, y, core = index // 8, (index // 2) % 4, index % 2
        z = 1 - z if flip_z else z
        core = 1 - core if flip_core else core
        pairs.append((index, z * 8 + y_partner(rel, y) * 2 + core))
    return pairs


ANY = pl.BlockSpec(memory_space=pl.ANY)
HBM = pl.BlockSpec(memory_space=pltpu.HBM)
WHOLE = pl.BlockSpec(memory_space=pltpu.VMEM)
SCALARS = pl.BlockSpec(memory_space=pltpu.SMEM)


def position():
    index = lax.axis_index("dir")
    return index % 2, (index // 2) % 4, index // 8


def phasor_rows(channel, freq, gain_of, uv, screen, lm, flux, direction, out, ready):
    stations, sources = screen.shape[1], lm.shape[1]
    ratio = freq[channel]
    along = lm[0:1, :] * ratio
    across = lm[1:2, :] * ratio
    amp = jnp.sqrt(flux[...])
    second = direction[...] > 0
    per_turn = 1.0 / (2.0 * math.pi * ratio)
    by_station = jnp.concatenate(
        [uv[0], uv[1], screen[...] * per_turn, jnp.zeros((2, stations), f32)], axis=0
    )
    cols = jnp.transpose(by_station)
    mask = jnp.broadcast_to(jnp.where(second, 1.0, 0.0), (16, sources)).astype(bf16)
    for moment in range(2):
        for start in range(0, stations, CHUNK):
            ready(moment, start)
            rows = slice(start, start + CHUNK)
            col = cols[rows]
            u = col[:, 2 * moment : 2 * moment + 1]
            v = col[:, 2 * moment + 1 : 2 * moment + 2]
            turns = u * along + v * across + jnp.where(second, col[:, 5:6], col[:, 4:5])
            turns = turns - ((turns + ROUNDER) - ROUNDER)
            z = turns * turns
            sin_half = SIN_COEF[4]
            cos_half = COS_COEF[4]
            for power in (3, 2, 1, 0):
                sin_half = sin_half * z + SIN_COEF[power]
                cos_half = cos_half * z + COS_COEF[power]
            sin_half = sin_half * turns
            sin_amp = sin_half * amp
            sine = sin_amp * cos_half
            cosine = amp - sin_amp * sin_half
            gain_re = gain_of(moment, 0, rows).astype(f32)
            gain_im = gain_of(moment, 1, rows).astype(f32)
            out[moment, rows, 0:sources] = (gain_re * cosine - gain_im * sine).astype(bf16)
            out[moment, rows, sources : 2 * sources] = (
                gain_re * sine + gain_im * cosine
            ).astype(bf16)
        out[moment, stations : stations + 16, 0:sources] = mask
        out[moment, stations : stations + 16, sources : 2 * sources] = mask


def phasor_send_kernel(
    freq, gain, uv, screen, lm, flux, direction, out, flux_held, direction_held, *rest
):
    held, freq_held, uv_held, screen_held, lm_held, sems = rest
    core, _, _ = position()
    channel = 1 - core
    quarter = gain.shape[3] // 4
    loads = [
        pltpu.make_async_copy(source, target, sems.at[8 + index])
        for index, (source, target) in enumerate(
            (
                (freq, freq_held),
                (uv, uv_held),
                (screen, screen_held),
                (lm, lm_held),
                (flux, flux_held.at[0]),
                (direction, direction_held.at[0]),
            )
        )
    ]
    copies = []
    for moment in range(2):
        for part in range(4):
            rows = pl.ds(part * quarter, quarter)
            copies.append(
                pltpu.make_async_copy(
                    gain.at[channel, moment, :, rows, :],
                    held.at[moment, :, rows, :],
                    sems.at[moment * 4 + part],
                )
            )
    for copy in loads + copies:
        copy.start()
    for load in loads:
        load.wait()

    def ready(moment, start):
        if start % quarter == 0:
            copies[moment * 4 + start // quarter].wait()

    def gain_of(moment, part, rows):
        return held[moment, part, rows, :]

    phasor_rows(
        channel, freq_held, gain_of, uv_held, screen_held, lm_held, flux_held, direction_held, out, ready
    )


def phasor_own_kernel(freq, gain, uv, screen, lm, flux, direction, out):
    channel = position()[0]

    def gain_of(moment, part, rows):
        return gain[channel, moment, part, rows, :]

    phasor_rows(
        channel, freq, gain_of, uv, screen, lm, flux, direction, out, lambda moment, start: None
    )


def phasor_send(*inputs):
    gain = inputs[1]
    stations, sources = gain.shape[3], gain.shape[4]
    return pl.pallas_call(
        phasor_send_kernel,
        in_specs=[HBM] * 7,
        out_specs=[WHOLE] * 3,
        out_shape=[
            jax.ShapeDtypeStruct((2, stations + 16, 2 * sources), bf16),
            jax.ShapeDtypeStruct((1, sources), f32),
            jax.ShapeDtypeStruct((1, sources), jnp.int32),
        ],
        scratch_shapes=[
            pltpu.VMEM((2, 2, stations, sources), bf16),
            pltpu.SMEM(inputs[0].shape, f32),
        ]
        + [pltpu.VMEM(array.shape, f32) for array in inputs[2:5]]
        + [pltpu.SemaphoreType.DMA((14,))],
        compiler_params=pltpu.CompilerParams(vmem_limit_bytes=60 * MIB),
        cost_estimate=pl.CostEstimate(
            flops=40 * 2 * stations * sources, bytes_accessed=3200000, transcendentals=0
        ),
        name="phasor_send",
    )(*inputs)


def phasor_own(*inputs):
    gain = inputs[1]
    stations, sources = gain.shape[3], gain.shape[4]
    return pl.pallas_call(
        phasor_own_kernel,
        in_specs=[SCALARS] + [WHOLE] * 6,
        out_specs=WHOLE,
        out_shape=jax.ShapeDtypeStruct((2, stations + 16, 2 * sources), bf16),
        compiler_params=pltpu.CompilerParams(vmem_limit_bytes=16 * MIB),
        cost_estimate=pl.CostEstimate(
            flops=40 * 2 * stations * sources, bytes_accessed=3200000, transcendentals=0
        ),
        name="phasor_own",
    )(*inputs)


def upper_mask():
    row = lax.broadcasted_iota(jnp.int32, (64, 64), 0)
    col = lax.broadcasted_iota(jnp.int32, (64, 64), 1)
    return row < col, row > col


def pack(re, im, odd, keep_re):
    re = jnp.where(odd, re[:, 64:384], re[:, 0:320])
    im = jnp.where(odd, im[:, 64:384], im[:, 0:320])
    upper, _ = upper_mask()
    own = jnp.where(upper, re[:, 0:64], im[:, 0:64])
    far = jnp.where(keep_re, re[:, 256:320], im[:, 256:320])
    return jnp.concatenate([own, re[:, 64:256], far, im[:, 64:256]], axis=1)


def skewed(q):
    half = q.shape[1] // 2
    return jnp.concatenate([q[:, half:], -q[:, :half]], axis=1)


def mm(a, b):
    return lax.dot_general(a, b, NT, preferred_element_type=f32)


def fill_wide(wide, part, top, bottom):
    wide[part, 0:256, 0:512] = top
    wide[part, 256:512, 256:512] = bottom
    corner = jnp.transpose(top[:, 256:512])
    wide[part, 256:512, 512:768] = corner if part == 0 else -corner


def fill_gram(wide, left, right):
    for part, rows in ((0, left), (1, skewed(left))):
        value = mm(rows, right)
        wide[part, :, 0:512] = value
        wide[part, :, 512:768] = value[:, 0:256]


def block_of(wide, part, chip):
    start = pl.multiple_of((chip // 2) * 128, 128)
    return wide[part, pl.ds(pl.multiple_of(chip * 64, 64), 64), pl.ds(start, 384)]


def model_kernel(scaling, own, other_hbm, out0, out1, out2, out3, wide, other, top, bottom, sems):
    _, y, z = position()
    copies = [
        pltpu.make_async_copy(other_hbm.at[moment], other.at[moment], sems.at[moment])
        for moment in range(2)
    ]
    for copy in copies:
        copy.start()
    for moment in range(2):
        q = own[moment, 0:512, :]
        for part, rows in ((0, q), (1, skewed(q))):
            top[part] = mm(rows[0:256], q)
            bottom[part] = mm(rows[256:512], q[256:512])
        copies[moment].wait()
        q = other[moment, 0:512, :]
        for part, rows in ((0, q), (1, skewed(q))):
            fill_wide(
                wide,
                part,
                (top[part] + mm(rows[0:256], q)) * scaling,
                (bottom[part] + mm(rows[256:512], q[256:512])) * scaling,
            )
        for rel, out in enumerate((out0, out1, out2, out3)):
            for flip in range(2):
                zz = 1 - z if flip else z
                chip = zz * 4 + y_partner(rel, y)
                out[flip, moment] = pack(
                    block_of(wide, 0, chip), block_of(wide, 1, chip), chip % 2 == 1, zz == 0
                ).astype(out.dtype)


def model_parts(scaling, own, other):
    return pl.pallas_call(
        functools.partial(model_kernel, scaling),
        in_specs=[WHOLE, HBM],
        out_specs=[WHOLE] * 4,
        scratch_shapes=[
            pltpu.VMEM((2, 512, 768), f32),
            pltpu.VMEM(other.shape, bf16),
            pltpu.VMEM((2, 256, 512), f32),
            pltpu.VMEM((2, 256, 256), f32),
            pltpu.SemaphoreType.DMA((2,)),
        ],
        out_shape=[jax.ShapeDtypeStruct((2, 2, 64, 512), f32)]
        + [jax.ShapeDtypeStruct((2, 2, 64, 512), bf16)] * 3,
        compiler_params=pltpu.CompilerParams(vmem_limit_bytes=16 * MIB),
        cost_estimate=pl.CostEstimate(
            flops=2 * 2 * 4 * 512 * 512 * 768, bytes_accessed=5000000, transcendentals=0
        ),
        name="model_parts",
    )(own, other)


def direction_kernel(moment, own, other, out, whole, first):
    core, y, z = position()
    for source, core_of in ((own, core), (other, 1 - core)):
        q = source[moment, 0:512, :]
        in_first = source[moment, 512:513, :] < 0.5
        q_first = jnp.where(in_first, q, jnp.zeros_like(q))
        fill_gram(whole, q, q)
        fill_gram(first, q_first, q)
        for rel in range(4):
            for flip in range(2):
                zz = 1 - z if flip else z
                chip = zz * 4 + y_partner(rel, y)
                odd = chip % 2 == 1
                keep_im = zz == 0
                all_of = pack(block_of(whole, 1, chip), -block_of(whole, 0, chip), odd, keep_im)
                first_of = pack(block_of(first, 1, chip), -block_of(first, 0, chip), odd, keep_im)
                out[core_of * 2, rel, flip] = first_of.astype(bf16)
                out[core_of * 2 + 1, rel, flip] = (all_of - first_of).astype(bf16)


def direction_parts(moment, own, other):
    return pl.pallas_call(
        functools.partial(direction_kernel, moment),
        in_specs=[WHOLE] * 2,
        out_specs=WHOLE,
        scratch_shapes=[pltpu.VMEM((2, 512, 768), f32)] * 2,
        out_shape=jax.ShapeDtypeStruct((4, 4, 2, 64, 512), bf16),
        compiler_params=pltpu.CompilerParams(vmem_limit_bytes=18 * MIB),
        cost_estimate=pl.CostEstimate(
            flops=2 * 8 * 512 * 512 * 768, bytes_accessed=5000000, transcendentals=0
        ),
        name="direction_parts%d" % moment,
    )(own, other)


def sum_kernel(own, one, two, three, _, stay, send):
    for flip, out in ((0, stay), (1, send)):
        out[...] = (
            own[flip] + one[flip].astype(f32) + two[flip].astype(f32) + three[flip].astype(f32)
        ).astype(out.dtype)


def sum_parts(own, one, two, three, after):
    return pl.pallas_call(
        sum_kernel,
        in_specs=[WHOLE] * 4 + [ANY],
        out_specs=[WHOLE] * 2,
        out_shape=[
            jax.ShapeDtypeStruct(own.shape[1:], f32),
            jax.ShapeDtypeStruct(own.shape[1:], bf16),
        ],
        compiler_params=pltpu.CompilerParams(vmem_limit_bytes=4 * MIB),
        cost_estimate=pl.CostEstimate(flops=500000, bytes_accessed=2500000, transcendentals=0),
        name="sum_parts",
    )(own, one, two, three, after)


def observed_kernel(observed, flags, other, other_flags, obs_out, keep_out, own, wide, sem):
    core, y, z = position()
    copy = pltpu.make_async_copy(observed.at[:, core], own, sem)
    copy.start()
    copy.wait()
    chip = z * 4 + y
    start = pl.ds(pl.multiple_of((chip // 2) * 128, 128), 384)
    odd = chip % 2 == 1
    row = lax.broadcasted_iota(jnp.int32, (64, 512), 0)
    col = lax.broadcasted_iota(jnp.int32, (64, 512), 1)
    for moment in range(2):
        for rows, source, kept in ((core, own, flags), (1 - core, other, other_flags)):
            there = pl.ds(pl.multiple_of(rows * 32, 32), 32)
            for part in range(3):
                value = kept[:, moment, :].astype(f32) if part == 2 else source[:, moment, part, :]
                wide[part, there, 0:512] = value
                wide[part, there, 512:768] = value[:, 0:256]
        obs_out[moment] = pack(wide[0, :, start], wide[1, :, start], odd, z == 0)
        keep = pack(wide[2, :, start], wide[2, :, start], odd, z == 0)
        keep_out[moment] = jnp.where(row == col, 0.0, keep)


def observed_parts(observed, flags, other, other_flags):
    return pl.pallas_call(
        observed_kernel,
        in_specs=[HBM] + [WHOLE] * 3,
        out_specs=[WHOLE] * 2,
        out_shape=[jax.ShapeDtypeStruct((2, 64, 512), f32)] * 2,
        scratch_shapes=[
            pltpu.VMEM(other.shape, f32),
            pltpu.VMEM((3, 64, 768), f32),
            pltpu.SemaphoreType.DMA,
        ],
        cost_estimate=pl.CostEstimate(flops=1000000, bytes_accessed=1500000, transcendentals=0),
        compiler_params=pltpu.CompilerParams(vmem_limit_bytes=6 * MIB),
        name="observed_parts",
    )(observed, flags, other, other_flags)


def gradient_kernel(scaling, freq, here, one, two, three, parts0, parts1, out, rows_sum, cols_sum):
    core, y, z = position()
    for rel, source in enumerate((here, one, two, three)):
        for flip in range(2):
            zz = 1 - z if flip else z
            chip = zz * 4 + y_partner(rel, y)
            for start in range(0, 64, 32):
                rows = slice(start, start + 32)
                resid0 = source[flip, 0, rows, :].astype(f32)
                resid1 = source[flip, 1, rows, :].astype(f32)
                for which in range(4):
                    product = resid0 * parts0[which, rel, flip, rows, :].astype(f32)
                    product += resid1 * parts1[which, rel, flip, rows, :].astype(f32)
                    rows_sum[which, pl.ds(pl.multiple_of(chip * 64 + start, 32), 32), :] = (
                        product[:, 0:128] + product[:, 128:256]
                    ) + (product[:, 256:384] + product[:, 384:512])
                    column = (product[0:8] + product[8:16]) + (product[16:24] + product[24:32])
                    if start == 0:
                        cols_sum[which, chip] = column
                    else:
                        cols_sum[which, chip] += column
    near = lax.broadcasted_iota(jnp.int32, (8, 256), 1) < 64
    factor = 2.0 * scaling / freq[core]
    pieces = []
    for which in range(4):
        placed = []
        for odd in range(2):
            total = None
            for chip in range(odd, 8, 2):
                low = cols_sum[which, chip, :, 0:256]
                high = cols_sum[which, chip, :, 256:512]
                folded = [low + jnp.where(near, 0.0, high), jnp.where(near, high, 0.0)]
                quarters = [part[:, at : at + 128] for part in folded for at in (0, 128)]
                turn = (4 - chip // 2) % 4
                quarters = quarters[turn:] + quarters[:turn]
                total = quarters if total is None else [a + b for a, b in zip(total, quarters)]
            placed.append(jnp.concatenate(total, axis=1))
        columns = placed[0] + pltpu.roll(placed[1], 64, 1)
        along_rows = jnp.sum(jnp.transpose(rows_sum[which]), axis=0, keepdims=True)
        grad = (along_rows - jnp.sum(columns, axis=0, keepdims=True)) * factor
        pieces.extend(grad[:, at : at + 128] for at in range(0, 512, 128))
    value = jnp.concatenate(pieces, axis=0).astype(bf16)

    def copy(index, carry):
        out[index] = value
        return carry

    lax.fori_loop(0, out.shape[0], copy, 0, unroll=8)


def gradient_parts(scaling, devices, freq, here, one, two, three, parts0, parts1):
    return pl.pallas_call(
        functools.partial(gradient_kernel, scaling),
        in_specs=[SCALARS] + [WHOLE] * 6,
        out_specs=WHOLE,
        scratch_shapes=[pltpu.VMEM((4, 512, 128), f32), pltpu.VMEM((4, 8, 8, 512), f32)],
        out_shape=jax.ShapeDtypeStruct((devices, 16, 128), bf16),
        compiler_params=pltpu.CompilerParams(vmem_limit_bytes=12 * MIB),
        cost_estimate=pl.CostEstimate(flops=10000000, bytes_accessed=6000000, transcendentals=0),
        name="gradient_parts",
    )(freq, here, one, two, three, parts0, parts1)


def rows_kernel(resid, here, one, two, three, _, own_out, other_out, rolled):
    core, y, z = position()
    chip = z * 4 + y
    upper, lower = upper_mask()
    even = y % 2 == 0
    flip5 = jnp.where(y < 3, 1, 0)
    flip6 = jnp.where(y < 2, 1, 0)
    flip7 = jnp.where(y < 1, 1, 0)
    for moment in range(2):
        own = resid[moment]
        near = own[:, 0:64]
        near_t = jnp.transpose(near)
        zero = jnp.zeros_like(near)
        near_re = jnp.where(upper, near, jnp.where(lower, near_t, zero))
        near_im = jnp.where(lower, near, jnp.where(upper, -near_t, zero))
        far = own[:, 256:320]
        far_t = jnp.transpose(here[1, moment][:, 256:320].astype(f32))
        far_re = jnp.where(z == 0, far, far_t)
        far_im = jnp.where(z == 0, -far_t, far)
        block5 = jnp.where(even, one[flip5, moment].astype(f32), two[flip5, moment].astype(f32))
        block6 = three[flip6, moment].astype(f32)
        block7 = jnp.where(even, two[flip7, moment].astype(f32), one[flip7, moment].astype(f32))
        re = [near_re, own[:, 64:256], far_re]
        im = [near_im, own[:, 320:512], far_im]
        for block, offset in ((block5, 3), (block6, 2), (block7, 1)):
            re.append(jnp.transpose(block[:, 64 * offset : 64 * offset + 64]))
            im.append(-jnp.transpose(block[:, 256 + 64 * offset : 320 + 64 * offset]))
        for part, pieces in enumerate((re, im)):
            index = moment * 2 + part
            rolled[index] = pltpu.roll(jnp.concatenate(pieces, axis=1), chip * 64, 1)
            own_out[index] = rolled[index, pl.ds(pl.multiple_of(core * 32, 32), 32), :]
            other_out[index] = rolled[index, pl.ds(pl.multiple_of((1 - core) * 32, 32), 32), :]


def whole_rows(resid, here, one, two, three, after):
    return pl.pallas_call(
        rows_kernel,
        in_specs=[WHOLE] * 5 + [ANY],
        out_specs=[WHOLE] * 2,
        out_shape=[jax.ShapeDtypeStruct((4, 32, 512), f32)] * 2,
        scratch_shapes=[pltpu.VMEM((4, 64, 512), f32)],
        cost_estimate=pl.CostEstimate(flops=2000000, bytes_accessed=1500000, transcendentals=0),
        compiler_params=pltpu.CompilerParams(vmem_limit_bytes=6 * MIB),
        name="whole_rows",
    )(resid, here, one, two, three, after)


def halves(value):
    high = value.astype(bf16)
    return high, (value - high.astype(f32)).astype(bf16)


def update_kernel(grads, kernel, screen, out, total, smooth):
    core, y, z = position()
    per_chip = grads.shape[0] // 8
    for chip in range(8):
        total[chip * 16 : chip * 16 + 16, :] = jnp.sum(
            grads[chip * per_chip : (chip + 1) * per_chip].astype(f32), axis=0
        )
    gradient = jnp.concatenate(
        [total[pl.ds(piece, 32, stride=4), :] for piece in range(4)], axis=1
    )
    grad_high, grad_low = halves(gradient)
    kern_high, kern_low = halves(kernel[...])
    both = jnp.dot(
        jnp.concatenate([grad_high, grad_low], axis=0), kern_high, preferred_element_type=f32
    )
    value = both[0:32] + (
        both[32:64] + jnp.dot(grad_high, kern_low, preferred_element_type=f32)
    )
    mean_sq = jnp.sum(value * value) / value.size
    smooth[...] = value * (step_size * lax.rsqrt(mean_sq + epsilon))
    row = (z * 4 + y) * 4 + core * 2
    for step in range(2):
        out[step : step + 1, :] = screen[step : step + 1, :] - smooth[pl.ds(row + step, 1), :]


def updated_rows(grads, kernel, screen):
    return pl.pallas_call(
        update_kernel,
        in_specs=[WHOLE] * 3,
        out_specs=WHOLE,
        out_shape=jax.ShapeDtypeStruct(screen.shape, f32),
        scratch_shapes=[pltpu.VMEM((128, 128), f32), pltpu.VMEM((32, 512), f32)],
        compiler_params=pltpu.CompilerParams(vmem_limit_bytes=8 * MIB),
        cost_estimate=pl.CostEstimate(flops=200000000, bytes_accessed=1500000, transcendentals=0),
        name="updated_rows",
    )(grads, kernel, screen)


def body(
    observed,
    flags,
    screen,
    screen_kernel,
    station_uv,
    source_lm,
    source_flux,
    station_gain,
    source_direction,
    freq_ratio,
):
    devices = lax.axis_size("dir") * lax.axis_size("freq")
    stations = screen.shape[1]
    scaling = 1.0 / math.sqrt(source_flux.shape[0] * lax.axis_size("dir"))
    core = position()[0]
    swap = functools.partial(lax.ppermute, axis_name="dir", perm=dir_perm(0, flip_core=True))

    inputs = (freq_ratio, station_gain, station_uv, screen, source_lm)
    sent, flux_row, direction_row = phasor_send(*inputs, source_flux, source_direction)
    other = swap(sent)
    own = phasor_own(*inputs, flux_row, direction_row)

    other_flags = swap(flags)
    other_observed = swap(lax.dynamic_index_in_dim(observed, 1 - core, 1, keepdims=False))
    obs, kept = observed_parts(observed, flags, other_observed, other_flags)

    part0, part1, part2, part3 = model_parts(scaling, own, other)
    got = [
        lax.ppermute(part, "dir", dir_perm(rel)) for rel, part in ((3, part3), (2, part2), (1, part1))
    ]
    directions0 = direction_parts(0, own, other)
    stay, send = sum_parts(part0, *got, directions0)
    last = lax.ppermute(send, "dir", dir_perm(0, flip_z=True))
    resid = kept * (obs - (stay + last.astype(f32)))
    half = resid.astype(bf16)
    here = jnp.stack([half, lax.ppermute(half, "dir", dir_perm(0, flip_z=True))])
    three = lax.ppermute(here, "dir", dir_perm(3))
    two = lax.ppermute(here, "dir", dir_perm(2))
    one = lax.ppermute(here, "dir", dir_perm(1))
    directions1 = direction_parts(1, own, other)

    grads = gradient_parts(
        scaling, devices, freq_ratio, here, one, two, three, directions0, directions1
    )
    own_rows, sent_rows = whole_rows(resid, here, one, two, three, grads)
    other_rows = swap(sent_rows)
    grads = lax.all_to_all(grads, ("dir", "freq"), 0, 0, tiled=True)
    updated = updated_rows(grads, screen_kernel, screen)

    first = jnp.where(core == 0, own_rows, other_rows)
    second = jnp.where(core == 0, other_rows, own_rows)
    residual = jnp.stack([first, second]).reshape(2, 2, 2, 32, stations)
    return jnp.transpose(residual, (3, 0, 1, 2, 4)), updated


def solution(mesh):
    placed = (
        P("dir", "freq", None, None, None),
        P("dir", None, None),
        P("dir", None),
        P(),
        P(),
        P(None, "dir"),
        P("dir"),
        P("freq", None, None, None, "dir"),
        P("dir"),
        P("freq"),
    )
    return jax.shard_map(
        body,
        mesh=mesh,
        in_specs=placed,
        out_specs=(P("dir", "freq", None, None, None), P("dir", None)),
        check_vma=False,
    )
```

```python
import functools
import math

import jax
import jax.numpy as jnp
from jax import lax
from jax.experimental import pallas as pl
from jax.experimental.pallas import tpu as pltpu
from jax.sharding import PartitionSpec as P

step_size = 0.3
epsilon = 1e-06
highest = lax.Precision.HIGHEST
bf16 = jnp.bfloat16
f32 = jnp.float32

SIN_COEF = (4.44288292, -7.3082457, 3.60635441, -0.84611289, 0.10982699)
COS_COEF = (1.4142135, -6.97885099, 5.73946117, -1.88356299, 0.31069819)
ROUNDER = 12582912.0
CHUNK = 32
MIB = 1024 * 1024
NT = (((1,), (1,)), ((), ()))


def y_partner(rel, y):
    if rel == 0:
        return y
    if rel == 1:
        return y + 1 - 2 * (y % 2)
    if rel == 2:
        return 3 - y
    return (y + 2) % 4


def dir_perm(rel, flip_z=False, flip_core=False):
    pairs = []
    for index in range(16):
        z, y, core = index // 8, (index // 2) % 4, index % 2
        z = 1 - z if flip_z else z
        core = 1 - core if flip_core else core
        pairs.append((index, z * 8 + y_partner(rel, y) * 2 + core))
    return pairs


STEPS = ((1, 2), (2, 1))
ANY = pl.BlockSpec(memory_space=pl.ANY)
HBM = pl.BlockSpec(memory_space=pltpu.HBM)
WHOLE = pl.BlockSpec(memory_space=pltpu.VMEM)
SCALARS = pl.BlockSpec(memory_space=pltpu.SMEM)


def position():
    index = lax.axis_index("dir")
    return index % 2, (index // 2) % 4, index // 8


def phasor_rows(channel, freq, gain_of, uv, screen, lm, flux, direction, out, ready):
    stations, sources = screen.shape[1], lm.shape[1]
    ratio = freq[channel]
    along = lm[0:1, :] * ratio
    across = lm[1:2, :] * ratio
    amp = jnp.sqrt(flux[...])
    second = direction[...] > 0
    per_turn = 1.0 / (2.0 * math.pi * ratio)
    by_station = jnp.concatenate(
        [uv[0], uv[1], screen[...] * per_turn, jnp.zeros((2, stations), f32)], axis=0
    )
    cols = jnp.transpose(by_station)
    mask = jnp.broadcast_to(jnp.where(second, 1.0, 0.0), (16, sources)).astype(bf16)
    for moment in range(2):
        for start in range(0, stations, CHUNK):
            ready(moment, start)
            rows = slice(start, start + CHUNK)
            col = cols[rows]
            u = col[:, 2 * moment : 2 * moment + 1]
            v = col[:, 2 * moment + 1 : 2 * moment + 2]
            turns = u * along + v * across + jnp.where(second, col[:, 5:6], col[:, 4:5])
            turns = turns - ((turns + ROUNDER) - ROUNDER)
            z = turns * turns
            sin_half = SIN_COEF[4]
            cos_half = COS_COEF[4]
            for power in (3, 2, 1, 0):
                sin_half = sin_half * z + SIN_COEF[power]
                cos_half = cos_half * z + COS_COEF[power]
            sin_half = sin_half * turns
            sin_amp = sin_half * amp
            sine = sin_amp * cos_half
            cosine = amp - sin_amp * sin_half
            gain_re = gain_of(moment, 0, rows).astype(f32)
            gain_im = gain_of(moment, 1, rows).astype(f32)
            out[moment, rows, 0:sources] = (gain_re * cosine - gain_im * sine).astype(bf16)
            out[moment, rows, sources : 2 * sources] = (
                gain_re * sine + gain_im * cosine
            ).astype(bf16)
        out[moment, stations : stations + 16, 0:sources] = mask
        out[moment, stations : stations + 16, sources : 2 * sources] = mask


def phasor_send_kernel(
    freq, gain, uv, screen, lm, flux, direction, out, *rest
):
    held, freq_held, uv_held, screen_held, lm_held, flux_held, direction_held, sems = rest
    core, _, _ = position()
    channel = 1 - core
    quarter = gain.shape[3] // 4
    loads = [
        pltpu.make_async_copy(source, target, sems.at[8 + index])
        for index, (source, target) in enumerate(
            (
                (freq, freq_held),
                (uv, uv_held),
                (screen, screen_held),
                (lm, lm_held),
                (flux, flux_held.at[0]),
                (direction, direction_held.at[0]),
            )
        )
    ]
    copies = []
    for moment in range(2):
        for part in range(4):
            rows = pl.ds(part * quarter, quarter)
            copies.append(
                pltpu.make_async_copy(
                    gain.at[channel, moment, :, rows, :],
                    held.at[moment, :, rows, :],
                    sems.at[moment * 4 + part],
                )
            )
    for copy in loads + copies:
        copy.start()
    for load in loads:
        load.wait()

    def ready(moment, start):
        if start % quarter == 0:
            copies[moment * 4 + start // quarter].wait()

    def gain_of(moment, part, rows):
        return held[moment, part, rows, :]

    phasor_rows(
        channel, freq_held, gain_of, uv_held, screen_held, lm_held, flux_held, direction_held, out, ready
    )


def phasor_own_kernel(freq, gain, uv, screen, lm, flux, direction, out, flux_held, direction_held, sems):
    channel = position()[0]
    loads = [
        pltpu.make_async_copy(flux, flux_held.at[0], sems.at[0]),
        pltpu.make_async_copy(direction, direction_held.at[0], sems.at[1]),
    ]
    for load in loads:
        load.start()
    for load in loads:
        load.wait()

    def gain_of(moment, part, rows):
        return gain[channel, moment, part, rows, :]

    phasor_rows(
        channel, freq, gain_of, uv, screen, lm, flux_held, direction_held, out, lambda moment, start: None
    )


def phasor_send(*inputs):
    gain = inputs[1]
    stations, sources = gain.shape[3], gain.shape[4]
    return pl.pallas_call(
        phasor_send_kernel,
        in_specs=[HBM] * 7,
        out_specs=WHOLE,
        out_shape=jax.ShapeDtypeStruct((2, stations + 16, 2 * sources), bf16),
        scratch_shapes=[
            pltpu.VMEM((2, 2, stations, sources), bf16),
            pltpu.SMEM(inputs[0].shape, f32),
        ]
        + [pltpu.VMEM(array.shape, f32) for array in inputs[2:5]]
        + [pltpu.VMEM((1, sources), f32), pltpu.VMEM((1, sources), jnp.int32)]
        + [pltpu.SemaphoreType.DMA((14,))],
        compiler_params=pltpu.CompilerParams(vmem_limit_bytes=60 * MIB),
        cost_estimate=pl.CostEstimate(
            flops=40 * 2 * stations * sources, bytes_accessed=3200000, transcendentals=0
        ),
        name="phasor_send",
    )(*inputs)


def phasor_own(*inputs):
    gain = inputs[1]
    stations, sources = gain.shape[3], gain.shape[4]
    return pl.pallas_call(
        phasor_own_kernel,
        in_specs=[SCALARS] + [WHOLE] * 4 + [ANY] * 2,
        out_specs=WHOLE,
        out_shape=jax.ShapeDtypeStruct((2, stations + 16, 2 * sources), bf16),
        scratch_shapes=[
            pltpu.VMEM((1, sources), f32),
            pltpu.VMEM((1, sources), jnp.int32),
            pltpu.SemaphoreType.DMA((2,)),
        ],
        compiler_params=pltpu.CompilerParams(vmem_limit_bytes=16 * MIB),
        cost_estimate=pl.CostEstimate(
            flops=40 * 2 * stations * sources, bytes_accessed=3200000, transcendentals=0
        ),
        name="phasor_own",
    )(*inputs)


def resid_block(resids, moment, rel, flip):
    here, near, far = resids[moment]
    first, second = STEPS[moment]
    if rel == 0:
        return here.at[flip]
    if rel == second:
        return near.at[flip]
    return far.at[0 if rel == first else 1, flip]


def upper_mask():
    row = lax.broadcasted_iota(jnp.int32, (64, 64), 0)
    col = lax.broadcasted_iota(jnp.int32, (64, 64), 1)
    return row < col, row > col


def pack(re, im, odd, keep_re):
    re = jnp.where(odd, re[:, 64:384], re[:, 0:320])
    im = jnp.where(odd, im[:, 64:384], im[:, 0:320])
    upper, _ = upper_mask()
    own = jnp.where(upper, re[:, 0:64], im[:, 0:64])
    far = jnp.where(keep_re, re[:, 256:320], im[:, 256:320])
    return jnp.concatenate([own, re[:, 64:256], far, im[:, 64:256]], axis=1)


def skewed(q):
    half = q.shape[1] // 2
    return jnp.concatenate([q[:, half:], -q[:, :half]], axis=1)


def mm(a, b):
    return lax.dot_general(a, b, NT, preferred_element_type=f32)


def fill_wide(wide, part, top, bottom):
    wide[part, 0:256, 0:512] = top
    wide[part, 256:512, 256:512] = bottom
    corner = jnp.transpose(top[:, 256:512])
    wide[part, 256:512, 512:768] = corner if part == 0 else -corner


def fill_gram(wide, left, right):
    for part, rows in ((0, left), (1, skewed(left))):
        value = mm(rows, right)
        wide[part, :, 0:512] = value
        wide[part, :, 512:768] = value[:, 0:256]


def block_of(wide, part, chip):
    start = pl.multiple_of((chip // 2) * 128, 128)
    return wide[part, pl.ds(pl.multiple_of(chip * 64, 64), 64), pl.ds(start, 384)]


def model_kernel(scaling, own, other_hbm, stay, keep, send0, send1, wide, other, top, bottom, sems):
    _, y, z = position()
    copies = [
        pltpu.make_async_copy(other_hbm.at[moment], other.at[moment], sems.at[moment])
        for moment in range(2)
    ]
    for copy in copies:
        copy.start()
    for moment in range(2):
        q = own[moment, 0:512, :]
        for part, rows in ((0, q), (1, skewed(q))):
            top[part] = mm(rows[0:256], q)
            bottom[part] = mm(rows[256:512], q[256:512])
        copies[moment].wait()
        q = other[moment, 0:512, :]
        for part, rows in ((0, q), (1, skewed(q))):
            fill_wide(
                wide,
                part,
                (top[part] + mm(rows[0:256], q)) * scaling,
                (bottom[part] + mm(rows[256:512], q[256:512])) * scaling,
            )
        first, second = STEPS[moment]
        for rel in range(4):
            for flip in range(2):
                zz = 1 - z if flip else z
                chip = zz * 4 + y_partner(rel, y)
                value = pack(
                    block_of(wide, 0, chip), block_of(wide, 1, chip), chip % 2 == 1, zz == 0
                )
                if rel == 0:
                    stay[flip, moment] = value
                elif rel == second:
                    keep[moment, flip] = value
                else:
                    send = (send0, send1)[moment]
                    send[0 if rel == first else 1, flip] = value.astype(bf16)


def model_parts(scaling, own, other):
    four = jax.ShapeDtypeStruct((2, 2, 64, 512), f32)
    return pl.pallas_call(
        functools.partial(model_kernel, scaling),
        in_specs=[WHOLE, HBM],
        out_specs=[WHOLE] * 4,
        scratch_shapes=[
            pltpu.VMEM((2, 512, 768), f32),
            pltpu.VMEM(own.shape, bf16),
            pltpu.VMEM((2, 256, 512), f32),
            pltpu.VMEM((2, 256, 256), f32),
            pltpu.SemaphoreType.DMA((2,)),
        ],
        out_shape=[four, four] + [jax.ShapeDtypeStruct((2, 2, 64, 512), bf16)] * 2,
        compiler_params=pltpu.CompilerParams(vmem_limit_bytes=16 * MIB),
        cost_estimate=pl.CostEstimate(
            flops=2 * 2 * 4 * 512 * 512 * 768, bytes_accessed=5000000, transcendentals=0
        ),
        name="model_parts",
    )(own, other)


def direction_kernel(moment, own, other, out, whole, first):
    core, y, z = position()
    for source, core_of in ((own, core), (other, 1 - core)):
        q = source[moment, 0:512, :]
        in_first = source[moment, 512:513, :] < 0.5
        q_first = jnp.where(in_first, q, jnp.zeros_like(q))
        fill_gram(whole, q, q)
        fill_gram(first, q_first, q)
        for rel in range(4):
            for flip in range(2):
                zz = 1 - z if flip else z
                chip = zz * 4 + y_partner(rel, y)
                odd = chip % 2 == 1
                keep_im = zz == 0
                all_of = pack(block_of(whole, 1, chip), -block_of(whole, 0, chip), odd, keep_im)
                first_of = pack(block_of(first, 1, chip), -block_of(first, 0, chip), odd, keep_im)
                out[core_of * 2, rel, flip] = first_of.astype(bf16)
                out[core_of * 2 + 1, rel, flip] = (all_of - first_of).astype(bf16)


def direction_parts(moment, own, other):
    return pl.pallas_call(
        functools.partial(direction_kernel, moment),
        in_specs=[WHOLE] * 2,
        out_specs=WHOLE,
        scratch_shapes=[pltpu.VMEM((2, 512, 768), f32)] * 2,
        out_shape=jax.ShapeDtypeStruct((4, 4, 2, 64, 512), bf16),
        compiler_params=pltpu.CompilerParams(vmem_limit_bytes=18 * MIB),
        cost_estimate=pl.CostEstimate(
            flops=2 * 8 * 512 * 512 * 768, bytes_accessed=5000000, transcendentals=0
        ),
        name="direction_parts%d" % moment,
    )(own, other)


def relay_kernel(keep, got0, got1, _, out0, out1):
    for moment, (got, out) in enumerate(((got0, out0), (got1, out1))):
        out[...] = (keep[moment] + got[1].astype(f32)).astype(bf16)


def relay_parts(keep, got0, got1, after):
    return pl.pallas_call(
        relay_kernel,
        in_specs=[WHOLE] * 3 + [ANY],
        out_specs=[WHOLE] * 2,
        out_shape=[jax.ShapeDtypeStruct(keep.shape[1:], bf16)] * 2,
        compiler_params=pltpu.CompilerParams(vmem_limit_bytes=4 * MIB),
        cost_estimate=pl.CostEstimate(flops=300000, bytes_accessed=1500000, transcendentals=0),
        name="relay_parts",
    )(keep, got0, got1, after)


def sum_kernel(own, got0, got1, last0, last1, stay, send):
    for moment, (got, last) in enumerate(((got0, last0), (got1, last1))):
        for flip, out in ((0, stay), (1, send)):
            out[moment] = (
                own[flip, moment] + got[0, flip].astype(f32) + last[flip].astype(f32)
            ).astype(out.dtype)


def sum_parts(own, *parts):
    return pl.pallas_call(
        sum_kernel,
        in_specs=[WHOLE] * 5,
        out_specs=[WHOLE] * 2,
        out_shape=[
            jax.ShapeDtypeStruct(own.shape[1:], f32),
            jax.ShapeDtypeStruct(own.shape[1:], bf16),
        ],
        compiler_params=pltpu.CompilerParams(vmem_limit_bytes=4 * MIB),
        cost_estimate=pl.CostEstimate(flops=500000, bytes_accessed=2500000, transcendentals=0),
        name="sum_parts",
    )(own, *parts)


def observed_send_kernel(observed, flags, _, out, sem):
    core, _, _ = position()
    copy = pltpu.make_async_copy(observed.at[:, 1 - core], out.at[:, :, 0:2, :], sem)
    copy.start()
    for moment in range(2):
        keep = flags[:, moment, :].astype(f32)
        out[:, moment, 2, :] = keep
        out[:, moment, 3, :] = keep
    copy.wait()


def observed_send(observed, flags, after):
    rows, _, _, _, stations = observed.shape
    return pl.pallas_call(
        observed_send_kernel,
        in_specs=[HBM, WHOLE, ANY],
        out_specs=WHOLE,
        out_shape=jax.ShapeDtypeStruct((rows, 2, 4, stations), f32),
        scratch_shapes=[pltpu.SemaphoreType.DMA],
        cost_estimate=pl.CostEstimate(flops=100000, bytes_accessed=700000, transcendentals=0),
        compiler_params=pltpu.CompilerParams(vmem_limit_bytes=4 * MIB),
        name="observed_send",
    )(observed, flags, after)


def observed_kernel(observed, flags, other, obs_out, keep_out, own, wide, sem):
    core, y, z = position()
    copy = pltpu.make_async_copy(observed.at[:, core], own, sem)
    copy.start()
    copy.wait()
    chip = z * 4 + y
    start = pl.ds(pl.multiple_of((chip // 2) * 128, 128), 384)
    odd = chip % 2 == 1
    row = lax.broadcasted_iota(jnp.int32, (64, 512), 0)
    col = lax.broadcasted_iota(jnp.int32, (64, 512), 1)
    for moment in range(2):
        for rows, mine in ((core, True), (1 - core, False)):
            there = pl.ds(pl.multiple_of(rows * 32, 32), 32)
            for part in range(3):
                if not mine:
                    value = other[:, moment, part, :]
                elif part == 2:
                    value = flags[:, moment, :].astype(f32)
                else:
                    value = own[:, moment, part, :]
                wide[part, there, 0:512] = value
                wide[part, there, 512:768] = value[:, 0:256]
        obs_out[moment] = pack(wide[0, :, start], wide[1, :, start], odd, z == 0)
        keep = pack(wide[2, :, start], wide[2, :, start], odd, z == 0)
        keep_out[moment] = jnp.where(row == col, 0.0, keep)


def observed_parts(observed, flags, other):
    rows, _, _, _, stations = observed.shape
    return pl.pallas_call(
        observed_kernel,
        in_specs=[HBM] + [WHOLE] * 2,
        out_specs=[WHOLE] * 2,
        out_shape=[jax.ShapeDtypeStruct((2, 64, 512), f32)] * 2,
        scratch_shapes=[
            pltpu.VMEM((rows, 2, 2, stations), f32),
            pltpu.VMEM((3, 64, 768), f32),
            pltpu.SemaphoreType.DMA,
        ],
        cost_estimate=pl.CostEstimate(flops=1000000, bytes_accessed=1500000, transcendentals=0),
        compiler_params=pltpu.CompilerParams(vmem_limit_bytes=6 * MIB),
        name="observed_parts",
    )(observed, flags, other)


def gradient_kernel(scaling, freq, *refs):
    resids = refs[0:3], refs[3:6]
    parts0, parts1, out, rows_sum, cols_sum = refs[6:]
    core, y, z = position()
    for rel in range(4):
        for flip in range(2):
            zz = 1 - z if flip else z
            chip = zz * 4 + y_partner(rel, y)
            first = resid_block(resids, 0, rel, flip)
            second = resid_block(resids, 1, rel, flip)
            for start in range(0, 64, 32):
                rows = slice(start, start + 32)
                resid0 = first[rows, :].astype(f32)
                resid1 = second[rows, :].astype(f32)
                for which in range(4):
                    product = resid0 * parts0[which, rel, flip, rows, :].astype(f32)
                    product += resid1 * parts1[which, rel, flip, rows, :].astype(f32)
                    rows_sum[which, pl.ds(pl.multiple_of(chip * 64 + start, 32), 32), :] = (
                        product[:, 0:128] + product[:, 128:256]
                    ) + (product[:, 256:384] + product[:, 384:512])
                    column = (product[0:8] + product[8:16]) + (product[16:24] + product[24:32])
                    if start == 0:
                        cols_sum[which, chip] = column
                    else:
                        cols_sum[which, chip] += column
    near = lax.broadcasted_iota(jnp.int32, (8, 256), 1) < 64
    factor = 2.0 * scaling / freq[core]
    pieces = []
    for which in range(4):
        placed = []
        for odd in range(2):
            total = None
            for chip in range(odd, 8, 2):
                low = cols_sum[which, chip, :, 0:256]
                high = cols_sum[which, chip, :, 256:512]
                folded = [low + jnp.where(near, 0.0, high), jnp.where(near, high, 0.0)]
                quarters = [part[:, at : at + 128] for part in folded for at in (0, 128)]
                turn = (4 - chip // 2) % 4
                quarters = quarters[turn:] + quarters[:turn]
                total = quarters if total is None else [a + b for a, b in zip(total, quarters)]
            placed.append(jnp.concatenate(total, axis=1))
        columns = placed[0] + pltpu.roll(placed[1], 64, 1)
        along_rows = jnp.sum(jnp.transpose(rows_sum[which]), axis=0, keepdims=True)
        grad = (along_rows - jnp.sum(columns, axis=0, keepdims=True)) * factor
        pieces.extend(grad[:, at : at + 128] for at in range(0, 512, 128))
    value = jnp.concatenate(pieces, axis=0).astype(bf16)

    def copy(index, carry):
        out[index] = value
        return carry

    lax.fori_loop(0, out.shape[0], copy, 0, unroll=8)


def gradient_parts(scaling, devices, freq, resids, parts0, parts1):
    return pl.pallas_call(
        functools.partial(gradient_kernel, scaling),
        in_specs=[SCALARS] + [WHOLE] * 8,
        out_specs=WHOLE,
        scratch_shapes=[pltpu.VMEM((4, 512, 128), f32), pltpu.VMEM((4, 8, 8, 512), f32)],
        out_shape=jax.ShapeDtypeStruct((devices, 16, 128), bf16),
        compiler_params=pltpu.CompilerParams(vmem_limit_bytes=12 * MIB),
        cost_estimate=pl.CostEstimate(flops=10000000, bytes_accessed=6000000, transcendentals=0),
        name="gradient_parts",
    )(freq, *resids, parts0, parts1)


def rows_kernel(resid, *refs):
    resids = refs[0:3], refs[3:6]
    _, own_out, other_out, rolled = refs[6:]
    core, y, z = position()
    chip = z * 4 + y
    upper, lower = upper_mask()
    even = y % 2 == 0
    flip5 = jnp.where(y < 3, 1, 0)
    flip6 = jnp.where(y < 2, 1, 0)
    flip7 = jnp.where(y < 1, 1, 0)
    for moment in range(2):
        own = resid[moment]
        near = own[:, 0:64]
        near_t = jnp.transpose(near)
        zero = jnp.zeros_like(near)
        near_re = jnp.where(upper, near, jnp.where(lower, near_t, zero))
        near_im = jnp.where(lower, near, jnp.where(upper, -near_t, zero))
        far = own[:, 256:320]
        far_t = jnp.transpose(resid_block(resids, moment, 0, 1)[:, 256:320].astype(f32))
        far_re = jnp.where(z == 0, far, far_t)
        far_im = jnp.where(z == 0, -far_t, far)
        one5, two5, block6, one7, two7 = (
            resid_block(resids, moment, rel, flip)[...].astype(f32)
            for rel, flip in ((1, flip5), (2, flip5), (3, flip6), (1, flip7), (2, flip7))
        )
        block5 = jnp.where(even, one5, two5)
        block7 = jnp.where(even, two7, one7)
        re = [near_re, own[:, 64:256], far_re]
        im = [near_im, own[:, 320:512], far_im]
        for block, offset in ((block5, 3), (block6, 2), (block7, 1)):
            re.append(jnp.transpose(block[:, 64 * offset : 64 * offset + 64]))
            im.append(-jnp.transpose(block[:, 256 + 64 * offset : 320 + 64 * offset]))
        for part, pieces in enumerate((re, im)):
            index = moment * 2 + part
            rolled[index] = pltpu.roll(jnp.concatenate(pieces, axis=1), chip * 64, 1)
            own_out[index] = rolled[index, pl.ds(pl.multiple_of(core * 32, 32), 32), :]
            other_out[index] = rolled[index, pl.ds(pl.multiple_of((1 - core) * 32, 32), 32), :]


def whole_rows(resid, resids, after):
    return pl.pallas_call(
        rows_kernel,
        in_specs=[WHOLE] * 7 + [ANY],
        out_specs=[WHOLE] * 2,
        out_shape=[jax.ShapeDtypeStruct((4, 32, 512), f32)] * 2,
        scratch_shapes=[pltpu.VMEM((4, 64, 512), f32)],
        cost_estimate=pl.CostEstimate(flops=0, bytes_accessed=0, transcendentals=0),
        compiler_params=pltpu.CompilerParams(vmem_limit_bytes=6 * MIB),
        name="whole_rows",
    )(resid, *resids, after)


def halves(value):
    high = value.astype(bf16)
    return high, (value - high.astype(f32)).astype(bf16)


def update_kernel(grads, kernel, screen, out, total, smooth):
    core, y, z = position()
    per_chip = grads.shape[0] // 8
    for chip in range(8):
        total[chip * 16 : chip * 16 + 16, :] = jnp.sum(
            grads[chip * per_chip : (chip + 1) * per_chip].astype(f32), axis=0
        )
    gradient = jnp.concatenate(
        [total[pl.ds(piece, 32, stride=4), :] for piece in range(4)], axis=1
    )
    grad_high, grad_low = halves(gradient)
    kern_high, kern_low = halves(kernel[...])
    both = jnp.dot(
        jnp.concatenate([grad_high, grad_low], axis=0), kern_high, preferred_element_type=f32
    )
    value = both[0:32] + (
        both[32:64] + jnp.dot(grad_high, kern_low, preferred_element_type=f32)
    )
    mean_sq = jnp.sum(value * value) / value.size
    smooth[...] = value * (step_size * lax.rsqrt(mean_sq + epsilon))
    row = (z * 4 + y) * 4 + core * 2
    for step in range(2):
        out[step : step + 1, :] = screen[step : step + 1, :] - smooth[pl.ds(row + step, 1), :]


def updated_rows(grads, kernel, screen):
    return pl.pallas_call(
        update_kernel,
        in_specs=[WHOLE] * 3,
        out_specs=WHOLE,
        out_shape=jax.ShapeDtypeStruct(screen.shape, f32),
        scratch_shapes=[pltpu.VMEM((128, 128), f32), pltpu.VMEM((32, 512), f32)],
        compiler_params=pltpu.CompilerParams(vmem_limit_bytes=8 * MIB),
        cost_estimate=pl.CostEstimate(flops=200000000, bytes_accessed=1500000, transcendentals=0),
        name="updated_rows",
    )(grads, kernel, screen)


def body(
    observed,
    flags,
    screen,
    screen_kernel,
    station_uv,
    source_lm,
    source_flux,
    station_gain,
    source_direction,
    freq_ratio,
):
    devices = lax.axis_size("dir") * lax.axis_size("freq")
    stations = screen.shape[1]
    scaling = 1.0 / math.sqrt(source_flux.shape[0] * lax.axis_size("dir"))
    core = position()[0]
    swap = functools.partial(lax.ppermute, axis_name="dir", perm=dir_perm(0, flip_core=True))

    inputs = (freq_ratio, station_gain, station_uv, screen, source_lm, source_flux, source_direction)
    other = swap(phasor_send(*inputs))
    own = phasor_own(*inputs)

    def across(rel, array):
        return lax.ppermute(array, "dir", dir_perm(rel))

    def across_z(array):
        return lax.ppermute(array, "dir", dir_perm(0, flip_z=True))

    kept0, keep, send0, send1 = model_parts(scaling, own, other)
    other_observed = swap(observed_send(observed, flags, send0))
    obs, kept = observed_parts(observed, flags, other_observed)
    got0, got1 = across(1, send0), across(2, send1)
    directions0 = direction_parts(0, own, other)
    relay0, relay1 = relay_parts(keep, got0, got1, directions0)
    last0, last1 = across(2, relay0), across(1, relay1)
    stay, send = sum_parts(kept0, got0, got1, last0, last1)
    resid = kept * (obs - (stay + across_z(send).astype(f32)))
    half = resid.astype(bf16)
    half_z = across_z(half)
    directions1 = direction_parts(1, own, other)
    resids = []
    for moment, (first, second) in enumerate(STEPS):
        here = jnp.stack([half[moment], half_z[moment]])
        near = across(second, here)
        resids.extend([here, near, across(first, jnp.stack([here, near]))])

    grads = gradient_parts(scaling, devices, freq_ratio, resids, directions0, directions1)
    own_rows, sent_rows = whole_rows(resid, resids, grads)
    other_rows = swap(sent_rows)
    grads = lax.all_to_all(grads, ("dir", "freq"), 0, 0, tiled=True)
    updated = updated_rows(grads, screen_kernel, screen)

    first = jnp.where(core == 0, own_rows, other_rows)
    second = jnp.where(core == 0, other_rows, own_rows)
    residual = jnp.stack([first, second]).reshape(2, 2, 2, 32, stations)
    return jnp.transpose(residual, (3, 0, 1, 2, 4)), updated


def solution(mesh):
    placed = (
        P("dir", "freq", None, None, None),
        P("dir", None, None),
        P("dir", None),
        P(),
        P(),
        P(None, "dir"),
        P("dir"),
        P("freq", None, None, None, "dir"),
        P("dir"),
        P("freq"),
    )
    return jax.shard_map(
        body,
        mesh=mesh,
        in_specs=placed,
        out_specs=(P("dir", "freq", None, None, None), P("dir", None)),
        check_vma=False,
    )
```

```python
import functools
import math

import jax
import jax.numpy as jnp
from jax import lax
from jax.experimental import pallas as pl
from jax.experimental.pallas import tpu as pltpu
from jax.sharding import PartitionSpec as P

step_size = 0.3
epsilon = 1e-06
highest = lax.Precision.HIGHEST
bf16 = jnp.bfloat16
f32 = jnp.float32

SIN_COEF = (4.44288292, -7.3082457, 3.60635441, -0.84611289, 0.10982699)
COS_COEF = (1.4142135, -6.97885099, 5.73946117, -1.88356299, 0.31069819)
ROUNDER = 12582912.0
CHUNK = 32
MIB = 1024 * 1024
NT = (((1,), (1,)), ((), ()))


def y_partner(rel, y):
    if rel == 0:
        return y
    if rel == 1:
        return y + 1 - 2 * (y % 2)
    if rel == 2:
        return 3 - y
    return (y + 2) % 4


def dir_perm(rel, flip_z=False, flip_core=False):
    pairs = []
    for index in range(16):
        z, y, core = index // 8, (index // 2) % 4, index % 2
        z = 1 - z if flip_z else z
        core = 1 - core if flip_core else core
        pairs.append((index, z * 8 + y_partner(rel, y) * 2 + core))
    return pairs


ANY = pl.BlockSpec(memory_space=pl.ANY)
HBM = pl.BlockSpec(memory_space=pltpu.HBM)
WHOLE = pl.BlockSpec(memory_space=pltpu.VMEM)
SCALARS = pl.BlockSpec(memory_space=pltpu.SMEM)


def position():
    index = lax.axis_index("dir")
    return index % 2, (index // 2) % 4, index // 8


def phasor_rows(channel, freq, gain_of, uv, screen, lm, flux, direction, out, ready):
    stations, sources = screen.shape[1], lm.shape[1]
    ratio = freq[channel]
    along = lm[0:1, :] * ratio
    across = lm[1:2, :] * ratio
    amp = jnp.sqrt(flux[...])
    second = direction[...] > 0
    per_turn = 1.0 / (2.0 * math.pi * ratio)
    by_station = jnp.concatenate(
        [uv[0], uv[1], screen[...] * per_turn, jnp.zeros((2, stations), f32)], axis=0
    )
    cols = jnp.transpose(by_station)
    mask = jnp.broadcast_to(jnp.where(second, 1.0, 0.0), (16, sources)).astype(bf16)
    for moment in range(2):
        for start in range(0, stations, CHUNK):
            ready(moment, start)
            rows = slice(start, start + CHUNK)
            col = cols[rows]
            u = col[:, 2 * moment : 2 * moment + 1]
            v = col[:, 2 * moment + 1 : 2 * moment + 2]
            turns = u * along + v * across + jnp.where(second, col[:, 5:6], col[:, 4:5])
            turns = turns - ((turns + ROUNDER) - ROUNDER)
            z = turns * turns
            sin_half = SIN_COEF[4]
            cos_half = COS_COEF[4]
            for power in (3, 2, 1, 0):
                sin_half = sin_half * z + SIN_COEF[power]
                cos_half = cos_half * z + COS_COEF[power]
            sin_half = sin_half * turns
            sin_amp = sin_half * amp
            sine = sin_amp * cos_half
            cosine = amp - sin_amp * sin_half
            gain_re = gain_of(moment, 0, rows).astype(f32)
            gain_im = gain_of(moment, 1, rows).astype(f32)
            out[moment, rows, 0:sources] = (gain_re * cosine - gain_im * sine).astype(bf16)
            out[moment, rows, sources : 2 * sources] = (
                gain_re * sine + gain_im * cosine
            ).astype(bf16)
        out[moment, stations : stations + 16, 0:sources] = mask
        out[moment, stations : stations + 16, sources : 2 * sources] = mask


def phasor_send_kernel(
    freq, gain, uv, screen, lm, flux, direction, out, *rest
):
    held, freq_held, uv_held, screen_held, lm_held, flux_held, direction_held, sems = rest
    core, _, _ = position()
    channel = 1 - core
    quarter = gain.shape[3] // 4
    loads = [
        pltpu.make_async_copy(source, target, sems.at[8 + index])
        for index, (source, target) in enumerate(
            (
                (freq, freq_held),
                (uv, uv_held),
                (screen, screen_held),
                (lm, lm_held),
                (flux, flux_held.at[0]),
                (direction, direction_held.at[0]),
            )
        )
    ]
    copies = []
    for moment in range(2):
        for part in range(4):
            rows = pl.ds(part * quarter, quarter)
            copies.append(
                pltpu.make_async_copy(
                    gain.at[channel, moment, :, rows, :],
                    held.at[moment, :, rows, :],
                    sems.at[moment * 4 + part],
                )
            )
    for copy in loads + copies:
        copy.start()
    for load in loads:
        load.wait()

    def ready(moment, start):
        if start % quarter == 0:
            copies[moment * 4 + start // quarter].wait()

    def gain_of(moment, part, rows):
        return held[moment, part, rows, :]

    phasor_rows(
        channel, freq_held, gain_of, uv_held, screen_held, lm_held, flux_held, direction_held, out, ready
    )


def phasor_own_kernel(freq, gain, uv, screen, lm, flux, direction, out, flux_held, direction_held, sems):
    channel = position()[0]
    loads = [
        pltpu.make_async_copy(flux, flux_held.at[0], sems.at[0]),
        pltpu.make_async_copy(direction, direction_held.at[0], sems.at[1]),
    ]
    for load in loads:
        load.start()
    for load in loads:
        load.wait()

    def gain_of(moment, part, rows):
        return gain[channel, moment, part, rows, :]

    phasor_rows(
        channel, freq, gain_of, uv, screen, lm, flux_held, direction_held, out, lambda moment, start: None
    )


def phasor_send(*inputs):
    gain = inputs[1]
    stations, sources = gain.shape[3], gain.shape[4]
    return pl.pallas_call(
        phasor_send_kernel,
        in_specs=[HBM] * 7,
        out_specs=WHOLE,
        out_shape=jax.ShapeDtypeStruct((2, stations + 16, 2 * sources), bf16),
        scratch_shapes=[
            pltpu.VMEM((2, 2, stations, sources), bf16),
            pltpu.SMEM(inputs[0].shape, f32),
        ]
        + [pltpu.VMEM(array.shape, f32) for array in inputs[2:5]]
        + [pltpu.VMEM((1, sources), f32), pltpu.VMEM((1, sources), jnp.int32)]
        + [pltpu.SemaphoreType.DMA((14,))],
        compiler_params=pltpu.CompilerParams(vmem_limit_bytes=60 * MIB),
        cost_estimate=pl.CostEstimate(
            flops=40 * 2 * stations * sources, bytes_accessed=3200000, transcendentals=0
        ),
        name="phasor_send",
    )(*inputs)


def phasor_own(*inputs):
    gain = inputs[1]
    stations, sources = gain.shape[3], gain.shape[4]
    return pl.pallas_call(
        phasor_own_kernel,
        in_specs=[SCALARS] + [WHOLE] * 4 + [ANY] * 2,
        out_specs=WHOLE,
        out_shape=jax.ShapeDtypeStruct((2, stations + 16, 2 * sources), bf16),
        scratch_shapes=[
            pltpu.VMEM((1, sources), f32),
            pltpu.VMEM((1, sources), jnp.int32),
            pltpu.SemaphoreType.DMA((2,)),
        ],
        compiler_params=pltpu.CompilerParams(vmem_limit_bytes=16 * MIB),
        cost_estimate=pl.CostEstimate(
            flops=40 * 2 * stations * sources, bytes_accessed=3200000, transcendentals=0
        ),
        name="phasor_own",
    )(*inputs)


def upper_mask():
    row = lax.broadcasted_iota(jnp.int32, (64, 64), 0)
    col = lax.broadcasted_iota(jnp.int32, (64, 64), 1)
    return row < col, row > col


def pack(re, im, odd, keep_re):
    re = jnp.where(odd, re[:, 64:384], re[:, 0:320])
    im = jnp.where(odd, im[:, 64:384], im[:, 0:320])
    upper, _ = upper_mask()
    own = jnp.where(upper, re[:, 0:64], im[:, 0:64])
    far = jnp.where(keep_re, re[:, 256:320], im[:, 256:320])
    return jnp.concatenate([own, re[:, 64:256], far, im[:, 64:256]], axis=1)


def skewed(q):
    half = q.shape[1] // 2
    return jnp.concatenate([q[:, half:], -q[:, :half]], axis=1)


def mm(a, b):
    return lax.dot_general(a, b, NT, preferred_element_type=f32)


def fill_wide(wide, part, top, bottom):
    wide[part, 0:256, 0:512] = top
    wide[part, 256:512, 256:512] = bottom
    corner = jnp.transpose(top[:, 256:512])
    wide[part, 256:512, 512:768] = corner if part == 0 else -corner


def fill_gram(wide, left, right):
    for part, rows in ((0, left), (1, skewed(left))):
        value = mm(rows, right)
        wide[part, :, 0:512] = value
        wide[part, :, 512:768] = value[:, 0:256]


def block_of(wide, part, chip):
    start = pl.multiple_of((chip // 2) * 128, 128)
    return wide[part, pl.ds(pl.multiple_of(chip * 64, 64), 64), pl.ds(start, 384)]


def model_kernel(scaling, own, other_hbm, stay, out11, out21, out31, out10, out20, out30, wide, other, top, bottom, sems):
    _, y, z = position()
    copies = [
        pltpu.make_async_copy(other_hbm.at[moment], other.at[moment], sems.at[moment])
        for moment in range(2)
    ]
    for copy in copies:
        copy.start()
    for moment in range(2):
        q = own[moment, 0:512, :]
        for part, rows in ((0, q), (1, skewed(q))):
            top[part] = mm(rows[0:256], q)
            bottom[part] = mm(rows[256:512], q[256:512])
        copies[moment].wait()
        q = other[moment, 0:512, :]
        for part, rows in ((0, q), (1, skewed(q))):
            fill_wide(
                wide,
                part,
                (top[part] + mm(rows[0:256], q)) * scaling,
                (bottom[part] + mm(rows[256:512], q[256:512])) * scaling,
            )
        for flip, outs in ((1, (out11, out21, out31)), (0, (out10, out20, out30))):
            for rel in range(4):
                zz = 1 - z if flip else z
                chip = zz * 4 + y_partner(rel, y)
                value = pack(
                    block_of(wide, 0, chip), block_of(wide, 1, chip), chip % 2 == 1, zz == 0
                )
                if rel == 0:
                    stay[flip, moment] = value
                else:
                    outs[rel - 1][moment] = value.astype(bf16)


def model_parts(scaling, own, other):
    return pl.pallas_call(
        functools.partial(model_kernel, scaling),
        in_specs=[WHOLE, HBM],
        out_specs=[WHOLE] * 7,
        scratch_shapes=[
            pltpu.VMEM((2, 512, 768), f32),
            pltpu.VMEM(own.shape, bf16),
            pltpu.VMEM((2, 256, 512), f32),
            pltpu.VMEM((2, 256, 256), f32),
            pltpu.SemaphoreType.DMA((2,)),
        ],
        out_shape=[jax.ShapeDtypeStruct((2, 2, 64, 512), f32)]
        + [jax.ShapeDtypeStruct((2, 64, 512), bf16)] * 6,
        compiler_params=pltpu.CompilerParams(vmem_limit_bytes=16 * MIB),
        cost_estimate=pl.CostEstimate(
            flops=2 * 2 * 4 * 512 * 512 * 768, bytes_accessed=5000000, transcendentals=0
        ),
        name="model_parts",
    )(own, other)


def direction_kernel(moment, own, other, out, whole, first):
    core, y, z = position()
    for source, core_of in ((own, core), (other, 1 - core)):
        q = source[moment, 0:512, :]
        in_first = source[moment, 512:513, :] < 0.5
        q_first = jnp.where(in_first, q, jnp.zeros_like(q))
        fill_gram(whole, q, q)
        fill_gram(first, q_first, q)
        for rel in range(4):
            for flip in range(2):
                zz = 1 - z if flip else z
                chip = zz * 4 + y_partner(rel, y)
                odd = chip % 2 == 1
                keep_im = zz == 0
                all_of = pack(block_of(whole, 1, chip), -block_of(whole, 0, chip), odd, keep_im)
                first_of = pack(block_of(first, 1, chip), -block_of(first, 0, chip), odd, keep_im)
                out[core_of * 2, rel, flip] = first_of.astype(bf16)
                out[core_of * 2 + 1, rel, flip] = (all_of - first_of).astype(bf16)


def direction_parts(moment, own, other):
    return pl.pallas_call(
        functools.partial(direction_kernel, moment),
        in_specs=[WHOLE] * 2,
        out_specs=WHOLE,
        scratch_shapes=[pltpu.VMEM((2, 512, 768), f32)] * 2,
        out_shape=jax.ShapeDtypeStruct((4, 4, 2, 64, 512), bf16),
        compiler_params=pltpu.CompilerParams(vmem_limit_bytes=18 * MIB),
        cost_estimate=pl.CostEstimate(
            flops=2 * 8 * 512 * 512 * 768, bytes_accessed=5000000, transcendentals=0
        ),
        name="direction_parts%d" % moment,
    )(own, other)


def send_kernel(own, one, two, three, send):
    send[...] = (
        own[1] + one[...].astype(f32) + two[...].astype(f32) + three[...].astype(f32)
    ).astype(bf16)


def send_parts(own, *parts):
    return pl.pallas_call(
        send_kernel,
        in_specs=[WHOLE] * 4,
        out_specs=WHOLE,
        out_shape=jax.ShapeDtypeStruct(own.shape[1:], bf16),
        compiler_params=pltpu.CompilerParams(vmem_limit_bytes=4 * MIB),
        cost_estimate=pl.CostEstimate(flops=300000, bytes_accessed=1500000, transcendentals=0),
        name="send_parts",
    )(own, *parts)


def residual_kernel(own, one, two, three, last, obs, kept, _, resid, half):
    total = own[0] + one[...].astype(f32) + two[...].astype(f32) + three[...].astype(f32)
    value = kept[...] * (obs[...] - (total + last[...].astype(f32)))
    resid[...] = value
    half[...] = value.astype(bf16)


def residual_parts(own, *parts):
    return pl.pallas_call(
        residual_kernel,
        in_specs=[WHOLE] * 7 + [ANY],
        out_specs=[WHOLE] * 2,
        out_shape=[
            jax.ShapeDtypeStruct(own.shape[1:], f32),
            jax.ShapeDtypeStruct(own.shape[1:], bf16),
        ],
        compiler_params=pltpu.CompilerParams(vmem_limit_bytes=4 * MIB),
        cost_estimate=pl.CostEstimate(flops=500000, bytes_accessed=2500000, transcendentals=0),
        name="residual_parts",
    )(own, *parts)


def observed_send_kernel(observed, flags, _, out, sem):
    core, _, _ = position()
    copy = pltpu.make_async_copy(observed.at[:, 1 - core], out.at[:, :, 0:2, :], sem)
    copy.start()
    for moment in range(2):
        keep = flags[:, moment, :].astype(f32)
        out[:, moment, 2, :] = keep
        out[:, moment, 3, :] = keep
    copy.wait()


def observed_send(observed, flags, after):
    rows, _, _, _, stations = observed.shape
    return pl.pallas_call(
        observed_send_kernel,
        in_specs=[HBM, WHOLE, ANY],
        out_specs=WHOLE,
        out_shape=jax.ShapeDtypeStruct((rows, 2, 4, stations), f32),
        scratch_shapes=[pltpu.SemaphoreType.DMA],
        cost_estimate=pl.CostEstimate(flops=100000, bytes_accessed=700000, transcendentals=0),
        compiler_params=pltpu.CompilerParams(vmem_limit_bytes=4 * MIB),
        name="observed_send",
    )(observed, flags, after)


def observed_kernel(observed, flags, other, obs_out, keep_out, own, wide, sem):
    core, y, z = position()
    copy = pltpu.make_async_copy(observed.at[:, core], own, sem)
    copy.start()
    copy.wait()
    chip = z * 4 + y
    start = pl.ds(pl.multiple_of((chip // 2) * 128, 128), 384)
    odd = chip % 2 == 1
    row = lax.broadcasted_iota(jnp.int32, (64, 512), 0)
    col = lax.broadcasted_iota(jnp.int32, (64, 512), 1)
    for moment in range(2):
        for rows, mine in ((core, True), (1 - core, False)):
            there = pl.ds(pl.multiple_of(rows * 32, 32), 32)
            for part in range(3):
                if not mine:
                    value = other[:, moment, part, :]
                elif part == 2:
                    value = flags[:, moment, :].astype(f32)
                else:
                    value = own[:, moment, part, :]
                wide[part, there, 0:512] = value
                wide[part, there, 512:768] = value[:, 0:256]
        obs_out[moment] = pack(wide[0, :, start], wide[1, :, start], odd, z == 0)
        keep = pack(wide[2, :, start], wide[2, :, start], odd, z == 0)
        keep_out[moment] = jnp.where(row == col, 0.0, keep)


def observed_parts(observed, flags, other):
    rows, _, _, _, stations = observed.shape
    return pl.pallas_call(
        observed_kernel,
        in_specs=[HBM] + [WHOLE] * 2,
        out_specs=[WHOLE] * 2,
        out_shape=[jax.ShapeDtypeStruct((2, 64, 512), f32)] * 2,
        scratch_shapes=[
            pltpu.VMEM((rows, 2, 2, stations), f32),
            pltpu.VMEM((3, 64, 768), f32),
            pltpu.SemaphoreType.DMA,
        ],
        cost_estimate=pl.CostEstimate(flops=1000000, bytes_accessed=1500000, transcendentals=0),
        compiler_params=pltpu.CompilerParams(vmem_limit_bytes=6 * MIB),
        name="observed_parts",
    )(observed, flags, other)


def gradient_kernel(scaling, freq, *refs):
    resids = refs[0:8]
    parts0, parts1, out, rows_sum, cols_sum = refs[8:]
    core, y, z = position()
    for rel in range(4):
        for flip in range(2):
            zz = 1 - z if flip else z
            chip = zz * 4 + y_partner(rel, y)
            source = resids[flip * 4 + rel]
            for start in range(0, 64, 32):
                rows = slice(start, start + 32)
                resid0 = source[0, rows, :].astype(f32)
                resid1 = source[1, rows, :].astype(f32)
                for which in range(4):
                    product = resid0 * parts0[which, rel, flip, rows, :].astype(f32)
                    product += resid1 * parts1[which, rel, flip, rows, :].astype(f32)
                    rows_sum[which, pl.ds(pl.multiple_of(chip * 64 + start, 32), 32), :] = (
                        product[:, 0:128] + product[:, 128:256]
                    ) + (product[:, 256:384] + product[:, 384:512])
                    column = (product[0:8] + product[8:16]) + (product[16:24] + product[24:32])
                    if start == 0:
                        cols_sum[which, chip] = column
                    else:
                        cols_sum[which, chip] += column
    near = lax.broadcasted_iota(jnp.int32, (8, 256), 1) < 64
    factor = 2.0 * scaling / freq[core]
    pieces = []
    for which in range(4):
        placed = []
        for odd in range(2):
            total = None
            for chip in range(odd, 8, 2):
                low = cols_sum[which, chip, :, 0:256]
                high = cols_sum[which, chip, :, 256:512]
                folded = [low + jnp.where(near, 0.0, high), jnp.where(near, high, 0.0)]
                quarters = [part[:, at : at + 128] for part in folded for at in (0, 128)]
                turn = (4 - chip // 2) % 4
                quarters = quarters[turn:] + quarters[:turn]
                total = quarters if total is None else [a + b for a, b in zip(total, quarters)]
            placed.append(jnp.concatenate(total, axis=1))
        columns = placed[0] + pltpu.roll(placed[1], 64, 1)
        along_rows = jnp.sum(jnp.transpose(rows_sum[which]), axis=0, keepdims=True)
        grad = (along_rows - jnp.sum(columns, axis=0, keepdims=True)) * factor
        pieces.extend(grad[:, at : at + 128] for at in range(0, 512, 128))
    value = jnp.concatenate(pieces, axis=0).astype(bf16)

    def copy(index, carry):
        out[index] = value
        return carry

    lax.fori_loop(0, out.shape[0], copy, 0, unroll=8)


def gradient_parts(scaling, devices, freq, resids, parts0, parts1):
    return pl.pallas_call(
        functools.partial(gradient_kernel, scaling),
        in_specs=[SCALARS] + [WHOLE] * 10,
        out_specs=WHOLE,
        scratch_shapes=[pltpu.VMEM((4, 512, 128), f32), pltpu.VMEM((4, 8, 8, 512), f32)],
        out_shape=jax.ShapeDtypeStruct((devices, 16, 128), bf16),
        compiler_params=pltpu.CompilerParams(vmem_limit_bytes=12 * MIB),
        cost_estimate=pl.CostEstimate(flops=10000000, bytes_accessed=6000000, transcendentals=0),
        name="gradient_parts",
    )(freq, *resids, parts0, parts1)


def rows_kernel(resid, *refs):
    resids = refs[0:8]
    _, own_out, other_out, rolled = refs[8:]
    core, y, z = position()
    chip = z * 4 + y
    upper, lower = upper_mask()
    even = y % 2 == 0
    flip5 = jnp.where(y < 3, 1, 0)
    flip6 = jnp.where(y < 2, 1, 0)
    flip7 = jnp.where(y < 1, 1, 0)
    for moment in range(2):
        own = resid[moment]
        near = own[:, 0:64]
        near_t = jnp.transpose(near)
        zero = jnp.zeros_like(near)
        near_re = jnp.where(upper, near, jnp.where(lower, near_t, zero))
        near_im = jnp.where(lower, near, jnp.where(upper, -near_t, zero))
        far = own[:, 256:320]
        far_t = jnp.transpose(resids[4][moment][:, 256:320].astype(f32))
        far_re = jnp.where(z == 0, far, far_t)
        far_im = jnp.where(z == 0, -far_t, far)
        one5, two5, block6, one7, two7 = (
            jnp.where(flip == 1, resids[4 + rel][moment], resids[rel][moment]).astype(f32)
            for rel, flip in ((1, flip5), (2, flip5), (3, flip6), (1, flip7), (2, flip7))
        )
        block5 = jnp.where(even, one5, two5)
        block7 = jnp.where(even, two7, one7)
        re = [near_re, own[:, 64:256], far_re]
        im = [near_im, own[:, 320:512], far_im]
        for block, offset in ((block5, 3), (block6, 2), (block7, 1)):
            re.append(jnp.transpose(block[:, 64 * offset : 64 * offset + 64]))
            im.append(-jnp.transpose(block[:, 256 + 64 * offset : 320 + 64 * offset]))
        for part, pieces in enumerate((re, im)):
            index = moment * 2 + part
            rolled[index] = pltpu.roll(jnp.concatenate(pieces, axis=1), chip * 64, 1)
            own_out[index] = rolled[index, pl.ds(pl.multiple_of(core * 32, 32), 32), :]
            other_out[index] = rolled[index, pl.ds(pl.multiple_of((1 - core) * 32, 32), 32), :]


def whole_rows(resid, resids, after):
    return pl.pallas_call(
        rows_kernel,
        in_specs=[WHOLE] * 9 + [ANY],
        out_specs=[WHOLE] * 2,
        out_shape=[jax.ShapeDtypeStruct((4, 32, 512), f32)] * 2,
        scratch_shapes=[pltpu.VMEM((4, 64, 512), f32)],
        cost_estimate=pl.CostEstimate(flops=0, bytes_accessed=0, transcendentals=0),
        compiler_params=pltpu.CompilerParams(vmem_limit_bytes=6 * MIB),
        name="whole_rows",
    )(resid, *resids, after)


def halves(value):
    high = value.astype(bf16)
    return high, (value - high.astype(f32)).astype(bf16)


def update_kernel(grads, kernel, screen, out, total, smooth):
    core, y, z = position()
    per_chip = grads.shape[0] // 8
    for chip in range(8):
        total[chip * 16 : chip * 16 + 16, :] = jnp.sum(
            grads[chip * per_chip : (chip + 1) * per_chip].astype(f32), axis=0
        )
    gradient = jnp.concatenate(
        [total[pl.ds(piece, 32, stride=4), :] for piece in range(4)], axis=1
    )
    grad_high, grad_low = halves(gradient)
    kern_high, kern_low = halves(kernel[...])
    both = jnp.dot(
        jnp.concatenate([grad_high, grad_low], axis=0), kern_high, preferred_element_type=f32
    )
    value = both[0:32] + (
        both[32:64] + jnp.dot(grad_high, kern_low, preferred_element_type=f32)
    )
    mean_sq = jnp.sum(value * value) / value.size
    smooth[...] = value * (step_size * lax.rsqrt(mean_sq + epsilon))
    row = (z * 4 + y) * 4 + core * 2
    for step in range(2):
        out[step : step + 1, :] = screen[step : step + 1, :] - smooth[pl.ds(row + step, 1), :]


def updated_rows(grads, kernel, screen):
    return pl.pallas_call(
        update_kernel,
        in_specs=[WHOLE] * 3,
        out_specs=WHOLE,
        out_shape=jax.ShapeDtypeStruct(screen.shape, f32),
        scratch_shapes=[pltpu.VMEM((128, 128), f32), pltpu.VMEM((32, 512), f32)],
        compiler_params=pltpu.CompilerParams(vmem_limit_bytes=8 * MIB),
        cost_estimate=pl.CostEstimate(flops=200000000, bytes_accessed=1500000, transcendentals=0),
        name="updated_rows",
    )(grads, kernel, screen)


def body(
    observed,
    flags,
    screen,
    screen_kernel,
    station_uv,
    source_lm,
    source_flux,
    station_gain,
    source_direction,
    freq_ratio,
):
    devices = lax.axis_size("dir") * lax.axis_size("freq")
    stations = screen.shape[1]
    scaling = 1.0 / math.sqrt(source_flux.shape[0] * lax.axis_size("dir"))
    core = position()[0]
    swap = functools.partial(lax.ppermute, axis_name="dir", perm=dir_perm(0, flip_core=True))

    inputs = (freq_ratio, station_gain, station_uv, screen, source_lm, source_flux, source_direction)
    other = swap(phasor_send(*inputs))
    own = phasor_own(*inputs)

    def across(rel, array):
        return lax.ppermute(array, "dir", dir_perm(rel))

    def across_z(array):
        return lax.ppermute(array, "dir", dir_perm(0, flip_z=True))

    parts = model_parts(scaling, own, other)
    far = [across(rel, parts[rel]) for rel in (3, 2, 1)]
    near = [across(rel, parts[rel + 3]) for rel in (3, 2, 1)]
    other_observed = swap(observed_send(observed, flags, parts[6]))
    obs, kept = observed_parts(observed, flags, other_observed)
    directions0 = direction_parts(0, own, other)
    last = across_z(send_parts(parts[0], *far))
    resid, half = residual_parts(parts[0], *near, last, obs, kept, directions0)
    half_z = across_z(half)
    directions1 = direction_parts(1, own, other)
    resids = [
        array if rel == 0 else across(rel, array) for array in (half, half_z) for rel in range(4)
    ]

    grads = gradient_parts(scaling, devices, freq_ratio, resids, directions0, directions1)
    own_rows, sent_rows = whole_rows(resid, resids, grads)
    other_rows = swap(sent_rows)
    grads = lax.all_to_all(grads, ("dir", "freq"), 0, 0, tiled=True)
    updated = updated_rows(grads, screen_kernel, screen)

    first = jnp.where(core == 0, own_rows, other_rows)
    second = jnp.where(core == 0, other_rows, own_rows)
    residual = jnp.stack([first, second]).reshape(2, 2, 2, 32, stations)
    return jnp.transpose(residual, (3, 0, 1, 2, 4)), updated


def solution(mesh):
    placed = (
        P("dir", "freq", None, None, None),
        P("dir", None, None),
        P("dir", None),
        P(),
        P(),
        P(None, "dir"),
        P("dir"),
        P("freq", None, None, None, "dir"),
        P("dir"),
        P("freq"),
    )
    return jax.shard_map(
        body,
        mesh=mesh,
        in_specs=placed,
        out_specs=(P("dir", "freq", None, None, None), P("dir", None)),
        check_vma=False,
    )
```

```python
import functools
import math

import jax
import jax.numpy as jnp
from jax import lax
from jax.experimental import pallas as pl
from jax.experimental.pallas import tpu as pltpu
from jax.sharding import PartitionSpec as P

step_size = 0.3
epsilon = 1e-06
highest = lax.Precision.HIGHEST
bf16 = jnp.bfloat16
f32 = jnp.float32

SIN_COEF = (4.44288292, -7.3082457, 3.60635441, -0.84611289, 0.10982699)
COS_COEF = (1.4142135, -6.97885099, 5.73946117, -1.88356299, 0.31069819)
ROUNDER = 12582912.0
CHUNK = 32
MIB = 1024 * 1024
NT = (((1,), (1,)), ((), ()))


def y_partner(rel, y):
    if rel == 0:
        return y
    if rel == 1:
        return y + 1 - 2 * (y % 2)
    if rel == 2:
        return 3 - y
    return (y + 2) % 4


def dir_perm(rel, flip_z=False, flip_core=False):
    pairs = []
    for index in range(16):
        z, y, core = index // 8, (index // 2) % 4, index % 2
        z = 1 - z if flip_z else z
        core = 1 - core if flip_core else core
        pairs.append((index, z * 8 + y_partner(rel, y) * 2 + core))
    return pairs


ANY = pl.BlockSpec(memory_space=pl.ANY)
HBM = pl.BlockSpec(memory_space=pltpu.HBM)
WHOLE = pl.BlockSpec(memory_space=pltpu.VMEM)
SCALARS = pl.BlockSpec(memory_space=pltpu.SMEM)


def position():
    index = lax.axis_index("dir")
    return index % 2, (index // 2) % 4, index // 8


def phasor_rows(channel, freq, gain_of, uv, screen, lm, flux, direction, out, ready):
    stations, sources = screen.shape[1], lm.shape[1]
    ratio = freq[channel]
    along = lm[0:1, :] * ratio
    across = lm[1:2, :] * ratio
    amp = jnp.sqrt(flux[...])
    second = direction[...] > 0
    per_turn = 1.0 / (2.0 * math.pi * ratio)
    by_station = jnp.concatenate(
        [uv[0], uv[1], screen[...] * per_turn, jnp.zeros((2, stations), f32)], axis=0
    )
    cols = jnp.transpose(by_station)
    mask = jnp.broadcast_to(jnp.where(second, 1.0, 0.0), (16, sources)).astype(bf16)
    for moment in range(2):
        for start in range(0, stations, CHUNK):
            ready(moment, start)
            rows = slice(start, start + CHUNK)
            col = cols[rows]
            u = col[:, 2 * moment : 2 * moment + 1]
            v = col[:, 2 * moment + 1 : 2 * moment + 2]
            turns = u * along + v * across + jnp.where(second, col[:, 5:6], col[:, 4:5])
            turns = turns - ((turns + ROUNDER) - ROUNDER)
            z = turns * turns
            sin_half = SIN_COEF[4]
            cos_half = COS_COEF[4]
            for power in (3, 2, 1, 0):
                sin_half = sin_half * z + SIN_COEF[power]
                cos_half = cos_half * z + COS_COEF[power]
            sin_half = sin_half * turns
            sin_amp = sin_half * amp
            sine = sin_amp * cos_half
            cosine = amp - sin_amp * sin_half
            gain_re = gain_of(moment, 0, rows).astype(f32)
            gain_im = gain_of(moment, 1, rows).astype(f32)
            out[moment, rows, 0:sources] = (gain_re * cosine - gain_im * sine).astype(bf16)
            out[moment, rows, sources : 2 * sources] = (
                gain_re * sine + gain_im * cosine
            ).astype(bf16)
        out[moment, stations : stations + 16, 0:sources] = mask
        out[moment, stations : stations + 16, sources : 2 * sources] = mask


def phasor_send_kernel(
    freq, gain, uv, screen, lm, flux, direction, out_hbm, *rest
):
    out, out_sems, held, freq_held, uv_held, screen_held, lm_held, flux_held, direction_held, sems = rest
    core, _, _ = position()
    channel = 1 - core
    quarter = gain.shape[3] // 4
    loads = [
        pltpu.make_async_copy(source, target, sems.at[8 + index])
        for index, (source, target) in enumerate(
            (
                (freq, freq_held),
                (uv, uv_held),
                (screen, screen_held),
                (lm, lm_held),
                (flux, flux_held.at[0]),
                (direction, direction_held.at[0]),
            )
        )
    ]
    copies = []
    for moment in range(2):
        for part in range(4):
            rows = pl.ds(part * quarter, quarter)
            copies.append(
                pltpu.make_async_copy(
                    gain.at[channel, moment, :, rows, :],
                    held.at[moment, :, rows, :],
                    sems.at[moment * 4 + part],
                )
            )
    for copy in loads + copies:
        copy.start()
    for load in loads:
        load.wait()

    half = gain.shape[3] // 2
    writes = []

    def write(moment, start, size):
        rows = pl.ds(start, size)
        writes.append(
            pltpu.make_async_copy(
                out.at[moment, rows, :], out_hbm.at[moment, rows, :], out_sems.at[len(writes)]
            )
        )
        writes[-1].start()

    def ready(moment, start):
        if start % quarter == 0:
            copies[moment * 4 + start // quarter].wait()
        if start == half:
            write(moment, 0, half)
        if start == 0 and moment == 1:
            write(0, half, half + 16)

    def gain_of(moment, part, rows):
        return held[moment, part, rows, :]

    phasor_rows(
        channel, freq_held, gain_of, uv_held, screen_held, lm_held, flux_held, direction_held, out, ready
    )
    write(1, half, half + 16)
    for copy in writes:
        copy.wait()


def phasor_own_kernel(freq, gain, uv, screen, lm, flux, direction, out, flux_held, direction_held, sems):
    channel = position()[0]
    loads = [
        pltpu.make_async_copy(flux, flux_held.at[0], sems.at[0]),
        pltpu.make_async_copy(direction, direction_held.at[0], sems.at[1]),
    ]
    for load in loads:
        load.start()
    for load in loads:
        load.wait()

    def gain_of(moment, part, rows):
        return gain[channel, moment, part, rows, :]

    phasor_rows(
        channel, freq, gain_of, uv, screen, lm, flux_held, direction_held, out, lambda moment, start: None
    )


def phasor_send(*inputs):
    gain = inputs[1]
    stations, sources = gain.shape[3], gain.shape[4]
    return pl.pallas_call(
        phasor_send_kernel,
        in_specs=[HBM] * 7,
        out_specs=HBM,
        out_shape=jax.ShapeDtypeStruct((2, stations + 16, 2 * sources), bf16),
        scratch_shapes=[
            pltpu.VMEM((2, stations + 16, 2 * sources), bf16),
            pltpu.SemaphoreType.DMA((4,)),
            pltpu.VMEM((2, 2, stations, sources), bf16),
            pltpu.SMEM(inputs[0].shape, f32),
        ]
        + [pltpu.VMEM(array.shape, f32) for array in inputs[2:5]]
        + [pltpu.VMEM((1, sources), f32), pltpu.VMEM((1, sources), jnp.int32)]
        + [pltpu.SemaphoreType.DMA((14,))],
        compiler_params=pltpu.CompilerParams(vmem_limit_bytes=60 * MIB),
        cost_estimate=pl.CostEstimate(
            flops=40 * 2 * stations * sources, bytes_accessed=3200000, transcendentals=0
        ),
        name="phasor_send",
    )(*inputs)


def phasor_own(*inputs):
    gain = inputs[1]
    stations, sources = gain.shape[3], gain.shape[4]
    return pl.pallas_call(
        phasor_own_kernel,
        in_specs=[SCALARS] + [WHOLE] * 4 + [ANY] * 2,
        out_specs=WHOLE,
        out_shape=jax.ShapeDtypeStruct((2, stations + 16, 2 * sources), bf16),
        scratch_shapes=[
            pltpu.VMEM((1, sources), f32),
            pltpu.VMEM((1, sources), jnp.int32),
            pltpu.SemaphoreType.DMA((2,)),
        ],
        compiler_params=pltpu.CompilerParams(vmem_limit_bytes=16 * MIB),
        cost_estimate=pl.CostEstimate(
            flops=40 * 2 * stations * sources, bytes_accessed=3200000, transcendentals=0
        ),
        name="phasor_own",
    )(*inputs)


def upper_mask():
    row = lax.broadcasted_iota(jnp.int32, (64, 64), 0)
    col = lax.broadcasted_iota(jnp.int32, (64, 64), 1)
    return row < col, row > col


def pack(re, im, odd, keep_re):
    re = jnp.where(odd, pltpu.roll(re, 320, 1), re)
    im = jnp.where(odd, pltpu.roll(im, 320, 1), im)
    row = lax.broadcasted_iota(jnp.int32, (64, 128), 0)
    col = lax.broadcasted_iota(jnp.int32, (64, 128), 1)
    near = col < 64
    far = jnp.where(keep_re, re[:, 256:384], im[:, 256:384])
    return jnp.concatenate(
        [
            jnp.where(near & (row >= col), im[:, 0:128], re[:, 0:128]),
            re[:, 128:256],
            jnp.where(near, far, im[:, 0:128]),
            im[:, 128:256],
        ],
        axis=1,
    )


def skewed(q):
    half = q.shape[1] // 2
    return jnp.concatenate([q[:, half:], -q[:, :half]], axis=1)


def mm(a, b):
    return lax.dot_general(a, b, NT, preferred_element_type=f32)


def fill_wide(wide, part, top, bottom):
    wide[part, 0:256, 0:512] = top
    wide[part, 256:512, 256:512] = bottom
    corner = jnp.transpose(top[:, 256:512])
    wide[part, 256:512, 512:768] = corner if part == 0 else -corner


def fill_gram(wide, left, right, scaling):
    for part, rows in ((0, left), (1, skewed(left))):
        value = mm(rows, right) * scaling
        wide[part, :, 0:512] = value
        wide[part, :, 512:768] = value[:, 0:256]


def block_of(wide, part, chip):
    start = pl.multiple_of((chip // 2) * 128, 128)
    return wide[part, pl.ds(pl.multiple_of(chip * 64, 64), 64), pl.ds(start, 384)]


def model_kernel(scaling, own, other_hbm, stay, out11, out21, out31, out10, out20, out30, wides, tops, bottoms, other, sems):
    _, y, z = position()
    copies = [
        pltpu.make_async_copy(other_hbm.at[moment], other.at[moment], sems.at[moment])
        for moment in range(2)
    ]
    for copy in copies:
        copy.start()
    for moment in range(2):
        wide, top, bottom = wides.at[moment], tops.at[moment], bottoms.at[moment]
        q = own[moment, 0:512, :]
        for part, rows in ((0, q), (1, skewed(q))):
            top[part] = mm(rows[0:256], q) * scaling
            bottom[part] = mm(rows[256:512], q[256:512]) * scaling
        copies[moment].wait()
        q = other[moment, 0:512, :]
        for part, rows in ((0, q), (1, skewed(q))):
            fill_wide(
                wide,
                part,
                top[part] + mm(rows[0:256], q) * scaling,
                bottom[part] + mm(rows[256:512], q[256:512]) * scaling,
            )
        for flip, outs in ((1, (out11, out21, out31)), (0, (out10, out20, out30))):
            for rel in range(4):
                zz = 1 - z if flip else z
                chip = zz * 4 + y_partner(rel, y)
                value = pack(
                    block_of(wide, 0, chip), block_of(wide, 1, chip), chip % 2 == 1, zz == 0
                )
                if rel == 0:
                    stay[flip, moment] = value
                else:
                    outs[rel - 1][moment] = value.astype(bf16)


def model_parts(scaling, own, other):
    return pl.pallas_call(
        functools.partial(model_kernel, scaling),
        in_specs=[WHOLE, HBM],
        out_specs=[WHOLE] * 10,
        scratch_shapes=[pltpu.VMEM(own.shape, bf16), pltpu.SemaphoreType.DMA((2,))],
        out_shape=[jax.ShapeDtypeStruct((2, 2, 64, 512), f32)]
        + [jax.ShapeDtypeStruct((2, 64, 512), bf16)] * 6
        + [
            jax.ShapeDtypeStruct((2, 2, 512, 768), f32),
            jax.ShapeDtypeStruct((2, 2, 256, 512), f32),
            jax.ShapeDtypeStruct((2, 2, 256, 256), f32),
        ],
        compiler_params=pltpu.CompilerParams(vmem_limit_bytes=20 * MIB),
        cost_estimate=pl.CostEstimate(
            flops=2 * 2 * 4 * 512 * 512 * 768, bytes_accessed=5000000, transcendentals=0
        ),
        name="model_parts",
    )(own, other)


def direction_kernel(moment, scaling, own, other, totals, tops, bottoms, out, mine, first_own, first_other):
    core, y, z = position()
    total = totals.at[moment]
    for part in range(2):
        fill_wide(mine, part, tops[moment, part], bottoms[moment, part])
    for source, first in ((own, first_own), (other, first_other)):
        q = source[moment, 0:512, :]
        in_first = source[moment, 512:513, :] < 0.5
        fill_gram(first, jnp.where(in_first, q, jnp.zeros_like(q)), q, scaling)
    for rel in range(4):
        for flip in range(2):
            zz = 1 - z if flip else z
            chip = zz * 4 + y_partner(rel, y)
            whole, own_all, own_first, other_first = (
                pack(block_of(wide, 1, chip), -block_of(wide, 0, chip), chip % 2 == 1, zz == 0)
                for wide in (total, mine, first_own, first_other)
            )
            out[core * 2, rel, flip] = own_first.astype(bf16)
            out[core * 2 + 1, rel, flip] = (own_all - own_first).astype(bf16)
            out[2 - core * 2, rel, flip] = other_first.astype(bf16)
            out[3 - core * 2, rel, flip] = ((whole - own_all) - other_first).astype(bf16)


def direction_parts(moment, scaling, *arrays):
    return pl.pallas_call(
        functools.partial(direction_kernel, moment, scaling),
        in_specs=[WHOLE] * 5,
        out_specs=WHOLE,
        scratch_shapes=[pltpu.VMEM((2, 512, 768), f32)] * 3,
        out_shape=jax.ShapeDtypeStruct((4, 4, 2, 64, 512), bf16),
        compiler_params=pltpu.CompilerParams(vmem_limit_bytes=18 * MIB),
        cost_estimate=pl.CostEstimate(
            flops=2 * 4 * 512 * 512 * 768, bytes_accessed=5000000, transcendentals=0
        ),
        name="direction_parts%d" % moment,
    )(*arrays)


def send_kernel(own, one, two, three, send):
    send[...] = (
        own[1] + one[...].astype(f32) + two[...].astype(f32) + three[...].astype(f32)
    ).astype(bf16)


def send_parts(own, *parts):
    return pl.pallas_call(
        send_kernel,
        in_specs=[WHOLE] * 4,
        out_specs=WHOLE,
        out_shape=jax.ShapeDtypeStruct(own.shape[1:], bf16),
        compiler_params=pltpu.CompilerParams(vmem_limit_bytes=4 * MIB),
        cost_estimate=pl.CostEstimate(flops=300000, bytes_accessed=1500000, transcendentals=0),
        name="send_parts",
    )(own, *parts)


def residual_kernel(own, one, two, three, last, obs, kept, _, resid, half):
    total = own[0] + one[...].astype(f32) + two[...].astype(f32) + three[...].astype(f32)
    value = kept[...] * (obs[...] - (total + last[...].astype(f32)))
    resid[...] = value
    half[...] = value.astype(bf16)


def residual_parts(own, *parts):
    return pl.pallas_call(
        residual_kernel,
        in_specs=[WHOLE] * 7 + [ANY],
        out_specs=[WHOLE] * 2,
        out_shape=[
            jax.ShapeDtypeStruct(own.shape[1:], f32),
            jax.ShapeDtypeStruct(own.shape[1:], bf16),
        ],
        compiler_params=pltpu.CompilerParams(vmem_limit_bytes=4 * MIB),
        cost_estimate=pl.CostEstimate(flops=500000, bytes_accessed=2500000, transcendentals=0),
        name="residual_parts",
    )(own, *parts)


def observed_send_kernel(observed, flags, _, out, sem):
    core, _, _ = position()
    copy = pltpu.make_async_copy(observed.at[:, 1 - core], out.at[:, :, 0:2, :], sem)
    copy.start()
    for moment in range(2):
        keep = flags[:, moment, :].astype(f32)
        out[:, moment, 2, :] = keep
        out[:, moment, 3, :] = keep
    copy.wait()


def observed_send(observed, flags, after):
    rows, _, _, _, stations = observed.shape
    return pl.pallas_call(
        observed_send_kernel,
        in_specs=[HBM, WHOLE, ANY],
        out_specs=WHOLE,
        out_shape=jax.ShapeDtypeStruct((rows, 2, 4, stations), f32),
        scratch_shapes=[pltpu.SemaphoreType.DMA],
        cost_estimate=pl.CostEstimate(flops=100000, bytes_accessed=700000, transcendentals=0),
        compiler_params=pltpu.CompilerParams(vmem_limit_bytes=4 * MIB),
        name="observed_send",
    )(observed, flags, after)


def observed_kernel(observed, flags, other, obs_out, keep_out, own, wide, sem):
    core, y, z = position()
    copy = pltpu.make_async_copy(observed.at[:, core], own, sem)
    copy.start()
    copy.wait()
    chip = z * 4 + y
    start = pl.ds(pl.multiple_of((chip // 2) * 128, 128), 384)
    odd = chip % 2 == 1
    row = lax.broadcasted_iota(jnp.int32, (64, 512), 0)
    col = lax.broadcasted_iota(jnp.int32, (64, 512), 1)
    for moment in range(2):
        for rows, mine in ((core, True), (1 - core, False)):
            there = pl.ds(pl.multiple_of(rows * 32, 32), 32)
            for part in range(3):
                if not mine:
                    value = other[:, moment, part, :]
                elif part == 2:
                    value = flags[:, moment, :].astype(f32)
                else:
                    value = own[:, moment, part, :]
                wide[part, there, 0:512] = value
                wide[part, there, 512:768] = value[:, 0:256]
        obs_out[moment] = pack(wide[0, :, start], wide[1, :, start], odd, z == 0)
        keep = pack(wide[2, :, start], wide[2, :, start], odd, z == 0)
        keep_out[moment] = jnp.where(row == col, 0.0, keep)


def observed_parts(observed, flags, other):
    rows, _, _, _, stations = observed.shape
    return pl.pallas_call(
        observed_kernel,
        in_specs=[HBM] + [WHOLE] * 2,
        out_specs=[WHOLE] * 2,
        out_shape=[jax.ShapeDtypeStruct((2, 64, 512), f32)] * 2,
        scratch_shapes=[
            pltpu.VMEM((rows, 2, 2, stations), f32),
            pltpu.VMEM((3, 64, 768), f32),
            pltpu.SemaphoreType.DMA,
        ],
        cost_estimate=pl.CostEstimate(flops=1000000, bytes_accessed=1500000, transcendentals=0),
        compiler_params=pltpu.CompilerParams(vmem_limit_bytes=6 * MIB),
        name="observed_parts",
    )(observed, flags, other)


def gradient_kernel(freq, *refs):
    resids = refs[0:8]
    parts0, parts1, out, rows_sum, cols_sum = refs[8:]
    core, y, z = position()
    for rel in range(4):
        for flip in range(2):
            zz = 1 - z if flip else z
            chip = zz * 4 + y_partner(rel, y)
            source = resids[flip * 4 + rel]
            for start in range(0, 64, 32):
                rows = slice(start, start + 32)
                resid0 = source[0, rows, :]
                resid1 = source[1, rows, :]
                for which in range(4):
                    product = (resid0 * parts0[which, rel, flip, rows, :]).astype(f32)
                    product += (resid1 * parts1[which, rel, flip, rows, :]).astype(f32)
                    rows_sum[which, pl.ds(pl.multiple_of(chip * 64 + start, 32), 32), :] = (
                        product[:, 0:128] + product[:, 128:256]
                    ) + (product[:, 256:384] + product[:, 384:512])
                    column = (product[0:8] + product[8:16]) + (product[16:24] + product[24:32])
                    if start == 0:
                        cols_sum[which, chip] = column
                    else:
                        cols_sum[which, chip] += column
    near = lax.broadcasted_iota(jnp.int32, (8, 256), 1) < 64
    factor = 2.0 / freq[core]
    pieces = []
    for which in range(4):
        placed = []
        for odd in range(2):
            total = None
            for chip in range(odd, 8, 2):
                low = cols_sum[which, chip, :, 0:256]
                high = cols_sum[which, chip, :, 256:512]
                folded = [low + jnp.where(near, 0.0, high), jnp.where(near, high, 0.0)]
                quarters = [part[:, at : at + 128] for part in folded for at in (0, 128)]
                turn = (4 - chip // 2) % 4
                quarters = quarters[turn:] + quarters[:turn]
                total = quarters if total is None else [a + b for a, b in zip(total, quarters)]
            placed.append(jnp.concatenate(total, axis=1))
        columns = placed[0] + pltpu.roll(placed[1], 64, 1)
        along_rows = jnp.sum(jnp.transpose(rows_sum[which]), axis=0, keepdims=True)
        grad = (along_rows - jnp.sum(columns, axis=0, keepdims=True)) * factor
        pieces.extend(grad[:, at : at + 128] for at in range(0, 512, 128))
    value = jnp.concatenate(pieces, axis=0).astype(bf16)

    def copy(index, carry):
        out[index] = value
        return carry

    lax.fori_loop(0, out.shape[0], copy, 0, unroll=8)


def gradient_parts(devices, freq, resids, parts0, parts1):
    return pl.pallas_call(
        gradient_kernel,
        in_specs=[SCALARS] + [WHOLE] * 10,
        out_specs=WHOLE,
        scratch_shapes=[pltpu.VMEM((4, 512, 128), f32), pltpu.VMEM((4, 8, 8, 512), f32)],
        out_shape=jax.ShapeDtypeStruct((devices, 16, 128), bf16),
        compiler_params=pltpu.CompilerParams(vmem_limit_bytes=12 * MIB),
        cost_estimate=pl.CostEstimate(flops=10000000, bytes_accessed=6000000, transcendentals=0),
        name="gradient_parts",
    )(freq, *resids, parts0, parts1)


def rows_kernel(resid, *refs):
    resids = refs[0:8]
    _, own_out, other_out, rolled = refs[8:]
    core, y, z = position()
    chip = z * 4 + y
    upper, lower = upper_mask()
    even = y % 2 == 0
    flip5 = jnp.where(y < 3, 1, 0)
    flip6 = jnp.where(y < 2, 1, 0)
    flip7 = jnp.where(y < 1, 1, 0)
    for moment in range(2):
        own = resid[moment]
        near = own[:, 0:64]
        near_t = jnp.transpose(near)
        zero = jnp.zeros_like(near)
        near_re = jnp.where(upper, near, jnp.where(lower, near_t, zero))
        near_im = jnp.where(lower, near, jnp.where(upper, -near_t, zero))
        far = own[:, 256:320]
        far_t = jnp.transpose(resids[4][moment][:, 256:320].astype(f32))
        far_re = jnp.where(z == 0, far, far_t)
        far_im = jnp.where(z == 0, -far_t, far)
        one5, two5, block6, one7, two7 = (
            jnp.where(flip == 1, resids[4 + rel][moment], resids[rel][moment]).astype(f32)
            for rel, flip in ((1, flip5), (2, flip5), (3, flip6), (1, flip7), (2, flip7))
        )
        block5 = jnp.where(even, one5, two5)
        block7 = jnp.where(even, two7, one7)
        re = [near_re, own[:, 64:256], far_re]
        im = [near_im, own[:, 320:512], far_im]
        for block, offset in ((block5, 3), (block6, 2), (block7, 1)):
            re.append(jnp.transpose(block[:, 64 * offset : 64 * offset + 64]))
            im.append(-jnp.transpose(block[:, 256 + 64 * offset : 320 + 64 * offset]))
        for part, pieces in enumerate((re, im)):
            index = moment * 2 + part
            rolled[index] = pltpu.roll(jnp.concatenate(pieces, axis=1), chip * 64, 1)
            own_out[index] = rolled[index, pl.ds(pl.multiple_of(core * 32, 32), 32), :]
            other_out[index] = rolled[index, pl.ds(pl.multiple_of((1 - core) * 32, 32), 32), :]


def whole_rows(resid, resids, after):
    return pl.pallas_call(
        rows_kernel,
        in_specs=[WHOLE] * 9 + [ANY],
        out_specs=[WHOLE] * 2,
        out_shape=[jax.ShapeDtypeStruct((4, 32, 512), f32)] * 2,
        scratch_shapes=[pltpu.VMEM((4, 64, 512), f32)],
        cost_estimate=pl.CostEstimate(flops=0, bytes_accessed=0, transcendentals=0),
        compiler_params=pltpu.CompilerParams(vmem_limit_bytes=6 * MIB),
        name="whole_rows",
    )(resid, *resids, after)


def halves(value):
    high = value.astype(bf16)
    return high, (value - high.astype(f32)).astype(bf16)


def update_kernel(grads, kernel, screen, out, total, smooth):
    core, y, z = position()
    per_chip = grads.shape[0] // 8
    for chip in range(8):
        total[chip * 16 : chip * 16 + 16, :] = jnp.sum(
            grads[chip * per_chip : (chip + 1) * per_chip].astype(f32), axis=0
        )
    gradient = jnp.concatenate(
        [total[pl.ds(piece, 32, stride=4), :] for piece in range(4)], axis=1
    )
    grad_high, grad_low = halves(gradient)
    kern_high, kern_low = halves(kernel[...])
    both = jnp.dot(
        jnp.concatenate([grad_high, grad_low], axis=0), kern_high, preferred_element_type=f32
    )
    value = both[0:32] + (
        both[32:64] + jnp.dot(grad_high, kern_low, preferred_element_type=f32)
    )
    mean_sq = jnp.sum(value * value) / value.size
    smooth[...] = value * (step_size * lax.rsqrt(mean_sq + epsilon))
    row = (z * 4 + y) * 4 + core * 2
    for step in range(2):
        out[step : step + 1, :] = screen[step : step + 1, :] - smooth[pl.ds(row + step, 1), :]


def updated_rows(grads, kernel, screen):
    return pl.pallas_call(
        update_kernel,
        in_specs=[WHOLE] * 3,
        out_specs=WHOLE,
        out_shape=jax.ShapeDtypeStruct(screen.shape, f32),
        scratch_shapes=[pltpu.VMEM((128, 128), f32), pltpu.VMEM((32, 512), f32)],
        compiler_params=pltpu.CompilerParams(vmem_limit_bytes=8 * MIB),
        cost_estimate=pl.CostEstimate(flops=200000000, bytes_accessed=1500000, transcendentals=0),
        name="updated_rows",
    )(grads, kernel, screen)


def body(
    observed,
    flags,
    screen,
    screen_kernel,
    station_uv,
    source_lm,
    source_flux,
    station_gain,
    source_direction,
    freq_ratio,
):
    devices = lax.axis_size("dir") * lax.axis_size("freq")
    stations = screen.shape[1]
    scaling = 1.0 / math.sqrt(source_flux.shape[0] * lax.axis_size("dir"))
    core = position()[0]
    swap = functools.partial(lax.ppermute, axis_name="dir", perm=dir_perm(0, flip_core=True))

    inputs = (freq_ratio, station_gain, station_uv, screen, source_lm, source_flux, source_direction)
    other = swap(phasor_send(*inputs))
    own = phasor_own(*inputs)

    def across(rel, array):
        return lax.ppermute(array, "dir", dir_perm(rel))

    def across_z(array):
        return lax.ppermute(array, "dir", dir_perm(0, flip_z=True))

    parts = model_parts(scaling, own, other)
    far = [across(rel, parts[rel]) for rel in (3, 2, 1)]
    near = [across(rel, parts[rel + 3]) for rel in (3, 2, 1)]
    other_observed = swap(observed_send(observed, flags, parts[6]))
    obs, kept = observed_parts(observed, flags, other_observed)
    directions0 = direction_parts(0, scaling, own, other, *parts[7:])
    last = across_z(send_parts(parts[0], *far))
    resid, half = residual_parts(parts[0], *near, last, obs, kept, directions0)
    half_z = across_z(half)
    directions1 = direction_parts(1, scaling, own, other, *parts[7:])
    resids = [
        array if rel == 0 else across(rel, array) for array in (half, half_z) for rel in range(4)
    ]

    grads = gradient_parts(devices, freq_ratio, resids, directions0, directions1)
    own_rows, sent_rows = whole_rows(resid, resids, grads)
    other_rows = swap(sent_rows)
    grads = lax.all_to_all(grads, ("dir", "freq"), 0, 0, tiled=True)
    updated = updated_rows(grads, screen_kernel, screen)

    first = jnp.where(core == 0, own_rows, other_rows)
    second = jnp.where(core == 0, other_rows, own_rows)
    residual = jnp.stack([first, second]).reshape(2, 2, 2, 32, stations)
    return jnp.transpose(residual, (3, 0, 1, 2, 4)), updated


def solution(mesh):
    placed = (
        P("dir", "freq", None, None, None),
        P("dir", None, None),
        P("dir", None),
        P(),
        P(),
        P(None, "dir"),
        P("dir"),
        P("freq", None, None, None, "dir"),
        P("dir"),
        P("freq"),
    )
    return jax.shard_map(
        body,
        mesh=mesh,
        in_specs=placed,
        out_specs=(P("dir", "freq", None, None, None), P("dir", None)),
        check_vma=False,
    )
```

```python
import functools
import math

import jax
import jax.numpy as jnp
from jax import lax
from jax.experimental import pallas as pl
from jax.experimental.pallas import tpu as pltpu
from jax.sharding import PartitionSpec as P

step_size = 0.3
epsilon = 1e-06
highest = lax.Precision.HIGHEST
bf16 = jnp.bfloat16
f32 = jnp.float32

SIN_COEF = (4.44288292, -7.3082457, 3.60635441, -0.84611289, 0.10982699)
COS_COEF = (1.4142135, -6.97885099, 5.73946117, -1.88356299, 0.31069819)
ROUNDER = 12582912.0
CHUNK = 32
MIB = 1024 * 1024
NT = (((1,), (1,)), ((), ()))


def y_partner(rel, y):
    if rel == 0:
        return y
    if rel == 1:
        return y + 1 - 2 * (y % 2)
    if rel == 2:
        return 3 - y
    return (y + 2) % 4


def dir_perm(rel, flip_z=False, flip_core=False):
    pairs = []
    for index in range(16):
        z, y, core = index // 8, (index // 2) % 4, index % 2
        z = 1 - z if flip_z else z
        core = 1 - core if flip_core else core
        pairs.append((index, z * 8 + y_partner(rel, y) * 2 + core))
    return pairs


ANY = pl.BlockSpec(memory_space=pl.ANY)
HBM = pl.BlockSpec(memory_space=pltpu.HBM)
WHOLE = pl.BlockSpec(memory_space=pltpu.VMEM)
SCALARS = pl.BlockSpec(memory_space=pltpu.SMEM)


def position():
    index = lax.axis_index("dir")
    return index % 2, (index // 2) % 4, index // 8


def phasor_rows(channel, freq, gain_of, uv, screen, lm, flux, direction, out, ready):
    stations, sources = screen.shape[1], lm.shape[1]
    ratio = freq[channel]
    along = lm[0:1, :] * ratio
    across = lm[1:2, :] * ratio
    amp = jnp.sqrt(flux[...])
    second = direction[...] > 0
    per_turn = 1.0 / (2.0 * math.pi * ratio)
    by_station = jnp.concatenate(
        [uv[0], uv[1], screen[...] * per_turn, jnp.zeros((2, stations), f32)], axis=0
    )
    cols = jnp.transpose(by_station)
    mask = jnp.broadcast_to(jnp.where(second, 1.0, 0.0), (16, sources)).astype(bf16)
    for moment in range(2):
        for start in range(0, stations, CHUNK):
            ready(moment, start)
            rows = slice(start, start + CHUNK)
            col = cols[rows]
            u = col[:, 2 * moment : 2 * moment + 1]
            v = col[:, 2 * moment + 1 : 2 * moment + 2]
            turns = u * along + v * across + jnp.where(second, col[:, 5:6], col[:, 4:5])
            turns = turns - ((turns + ROUNDER) - ROUNDER)
            z = turns * turns
            sin_half = SIN_COEF[4]
            cos_half = COS_COEF[4]
            for power in (3, 2, 1, 0):
                sin_half = sin_half * z + SIN_COEF[power]
                cos_half = cos_half * z + COS_COEF[power]
            sin_half = sin_half * turns
            sin_amp = sin_half * amp
            sine = sin_amp * cos_half
            cosine = amp - sin_amp * sin_half
            gain_re = gain_of(moment, 0, rows).astype(f32)
            gain_im = gain_of(moment, 1, rows).astype(f32)
            out[moment, rows, 0:sources] = (gain_re * cosine - gain_im * sine).astype(bf16)
            out[moment, rows, sources : 2 * sources] = (
                gain_re * sine + gain_im * cosine
            ).astype(bf16)
        out[moment, stations : stations + 16, 0:sources] = mask
        out[moment, stations : stations + 16, sources : 2 * sources] = mask


def phasor_send_kernel(
    freq, gain, uv, screen, lm, flux, direction, out_hbm, *rest
):
    out, out_sems, held, freq_held, uv_held, screen_held, lm_held, flux_held, direction_held, sems = rest
    core, _, _ = position()
    channel = 1 - core
    quarter = gain.shape[3] // 4
    loads = [
        pltpu.make_async_copy(source, target, sems.at[8 + index])
        for index, (source, target) in enumerate(
            (
                (freq, freq_held),
                (uv, uv_held),
                (screen, screen_held),
                (lm, lm_held),
                (flux, flux_held.at[0]),
                (direction, direction_held.at[0]),
            )
        )
    ]
    copies = []
    for moment in range(2):
        for part in range(4):
            rows = pl.ds(part * quarter, quarter)
            copies.append(
                pltpu.make_async_copy(
                    gain.at[channel, moment, :, rows, :],
                    held.at[moment, :, rows, :],
                    sems.at[moment * 4 + part],
                )
            )
    for copy in loads + copies:
        copy.start()
    for load in loads:
        load.wait()

    half = gain.shape[3] // 2
    writes = []

    def write(moment, start, size):
        rows = pl.ds(start, size)
        writes.append(
            pltpu.make_async_copy(
                out.at[moment, rows, :], out_hbm.at[moment, rows, :], out_sems.at[len(writes)]
            )
        )
        writes[-1].start()

    def ready(moment, start):
        if start % quarter == 0:
            copies[moment * 4 + start // quarter].wait()
        if start == half:
            write(moment, 0, half)
        if start == 0 and moment == 1:
            write(0, half, half + 16)

    def gain_of(moment, part, rows):
        return held[moment, part, rows, :]

    phasor_rows(
        channel, freq_held, gain_of, uv_held, screen_held, lm_held, flux_held, direction_held, out, ready
    )
    write(1, half, half + 16)
    for copy in writes:
        copy.wait()


def phasor_own_kernel(freq, gain, uv, screen, lm, flux, direction, out, flux_held, direction_held, sems):
    channel = position()[0]
    loads = [
        pltpu.make_async_copy(flux, flux_held.at[0], sems.at[0]),
        pltpu.make_async_copy(direction, direction_held.at[0], sems.at[1]),
    ]
    for load in loads:
        load.start()
    for load in loads:
        load.wait()

    def gain_of(moment, part, rows):
        return gain[channel, moment, part, rows, :]

    phasor_rows(
        channel, freq, gain_of, uv, screen, lm, flux_held, direction_held, out, lambda moment, start: None
    )


def phasor_send(*inputs):
    gain = inputs[1]
    stations, sources = gain.shape[3], gain.shape[4]
    return pl.pallas_call(
        phasor_send_kernel,
        in_specs=[HBM] * 7,
        out_specs=HBM,
        out_shape=jax.ShapeDtypeStruct((2, stations + 16, 2 * sources), bf16),
        scratch_shapes=[
            pltpu.VMEM((2, stations + 16, 2 * sources), bf16),
            pltpu.SemaphoreType.DMA((4,)),
            pltpu.VMEM((2, 2, stations, sources), bf16),
            pltpu.SMEM(inputs[0].shape, f32),
        ]
        + [pltpu.VMEM(array.shape, f32) for array in inputs[2:5]]
        + [pltpu.VMEM((1, sources), f32), pltpu.VMEM((1, sources), jnp.int32)]
        + [pltpu.SemaphoreType.DMA((14,))],
        compiler_params=pltpu.CompilerParams(vmem_limit_bytes=60 * MIB),
        cost_estimate=pl.CostEstimate(
            flops=40 * 2 * stations * sources, bytes_accessed=3200000, transcendentals=0
        ),
        name="phasor_send",
    )(*inputs)


def phasor_own(*inputs):
    gain = inputs[1]
    stations, sources = gain.shape[3], gain.shape[4]
    return pl.pallas_call(
        phasor_own_kernel,
        in_specs=[SCALARS] + [WHOLE] * 4 + [ANY] * 2,
        out_specs=WHOLE,
        out_shape=jax.ShapeDtypeStruct((2, stations + 16, 2 * sources), bf16),
        scratch_shapes=[
            pltpu.VMEM((1, sources), f32),
            pltpu.VMEM((1, sources), jnp.int32),
            pltpu.SemaphoreType.DMA((2,)),
        ],
        compiler_params=pltpu.CompilerParams(vmem_limit_bytes=16 * MIB),
        cost_estimate=pl.CostEstimate(
            flops=40 * 2 * stations * sources, bytes_accessed=3200000, transcendentals=0
        ),
        name="phasor_own",
    )(*inputs)


def upper_mask():
    row = lax.broadcasted_iota(jnp.int32, (64, 64), 0)
    col = lax.broadcasted_iota(jnp.int32, (64, 64), 1)
    return row < col, row > col


def pack(re, im, odd, keep_re):
    re = jnp.where(odd, pltpu.roll(re, 320, 1), re)
    im = jnp.where(odd, pltpu.roll(im, 320, 1), im)
    row = lax.broadcasted_iota(jnp.int32, (64, 128), 0)
    col = lax.broadcasted_iota(jnp.int32, (64, 128), 1)
    near = col < 64
    far = jnp.where(keep_re, re[:, 256:384], im[:, 256:384])
    return jnp.concatenate(
        [
            jnp.where(near & (row >= col), im[:, 0:128], re[:, 0:128]),
            re[:, 128:256],
            jnp.where(near, far, im[:, 0:128]),
            im[:, 128:256],
        ],
        axis=1,
    )


def skewed(q):
    half = q.shape[1] // 2
    return jnp.concatenate([q[:, half:], -q[:, :half]], axis=1)


def mm(a, b):
    return lax.dot_general(a, b, NT, preferred_element_type=f32)


def fill_wide(wide, part, top, bottom):
    wide[part, 0:256, 0:512] = top
    wide[part, 256:512, 256:512] = bottom
    corner = jnp.transpose(top[:, 256:512])
    wide[part, 256:512, 512:768] = corner if part == 0 else -corner


def fill_gram(wide, left, right, scaling):
    for part, rows in ((0, left), (1, skewed(left))):
        value = mm(rows, right) * scaling
        wide[part, :, 0:512] = value
        wide[part, :, 512:768] = value[:, 0:256]


def block_of(wide, part, chip):
    start = pl.multiple_of((chip // 2) * 128, 128)
    return wide[part, pl.ds(pl.multiple_of(chip * 64, 64), 64), pl.ds(start, 384)]


def model_kernel(scaling, own, other_hbm, stay, out11, out21, out31, out10, out20, out30, wides, tops, bottoms, other, sems):
    _, y, z = position()
    copies = [
        pltpu.make_async_copy(other_hbm.at[moment], other.at[moment], sems.at[moment])
        for moment in range(2)
    ]
    for copy in copies:
        copy.start()
    for moment in range(2):
        wide, top, bottom = wides.at[moment], tops.at[moment], bottoms.at[moment]
        q = own[moment, 0:512, :]
        for part, rows in ((0, q), (1, skewed(q))):
            top[part] = mm(rows[0:256], q) * scaling
            bottom[part] = mm(rows[256:512], q[256:512]) * scaling
        copies[moment].wait()
        q = other[moment, 0:512, :]
        for part, rows in ((0, q), (1, skewed(q))):
            fill_wide(
                wide,
                part,
                top[part] + mm(rows[0:256], q) * scaling,
                bottom[part] + mm(rows[256:512], q[256:512]) * scaling,
            )
        for flip, outs in ((1, (out11, out21, out31)), (0, (out10, out20, out30))):
            for rel in range(4):
                zz = 1 - z if flip else z
                chip = zz * 4 + y_partner(rel, y)
                value = pack(
                    block_of(wide, 0, chip), block_of(wide, 1, chip), chip % 2 == 1, zz == 0
                )
                if rel == 0:
                    stay[flip, moment] = value
                else:
                    outs[rel - 1][moment] = value.astype(bf16)


def model_parts(scaling, own, other):
    return pl.pallas_call(
        functools.partial(model_kernel, scaling),
        in_specs=[WHOLE, HBM],
        out_specs=[WHOLE] * 10,
        scratch_shapes=[pltpu.VMEM(own.shape, bf16), pltpu.SemaphoreType.DMA((2,))],
        out_shape=[jax.ShapeDtypeStruct((2, 2, 64, 512), f32)]
        + [jax.ShapeDtypeStruct((2, 64, 512), bf16)] * 6
        + [
            jax.ShapeDtypeStruct((2, 2, 512, 768), f32),
            jax.ShapeDtypeStruct((2, 2, 256, 512), f32),
            jax.ShapeDtypeStruct((2, 2, 256, 256), f32),
        ],
        compiler_params=pltpu.CompilerParams(vmem_limit_bytes=20 * MIB),
        cost_estimate=pl.CostEstimate(
            flops=2 * 2 * 4 * 512 * 512 * 768, bytes_accessed=5000000, transcendentals=0
        ),
        name="model_parts",
    )(own, other)


def direction_kernel(moment, scaling, own, other, totals, tops, bottoms, out, mine, first_own, first_other):
    core, y, z = position()
    total = totals.at[moment]
    for part in range(2):
        fill_wide(mine, part, tops[moment, part], bottoms[moment, part])
    for source, first in ((own, first_own), (other, first_other)):
        q = source[moment, 0:512, :]
        in_first = source[moment, 512:513, :] < 0.5
        fill_gram(first, jnp.where(in_first, q, jnp.zeros_like(q)), q, scaling)
    for rel in range(4):
        for flip in range(2):
            zz = 1 - z if flip else z
            chip = zz * 4 + y_partner(rel, y)
            whole, own_all, own_first, other_first = (
                pack(block_of(wide, 1, chip), -block_of(wide, 0, chip), chip % 2 == 1, zz == 0)
                for wide in (total, mine, first_own, first_other)
            )
            out[core * 2, rel, flip] = own_first.astype(bf16)
            out[core * 2 + 1, rel, flip] = (own_all - own_first).astype(bf16)
            out[2 - core * 2, rel, flip] = other_first.astype(bf16)
            out[3 - core * 2, rel, flip] = ((whole - own_all) - other_first).astype(bf16)


def direction_parts(moment, scaling, *arrays):
    return pl.pallas_call(
        functools.partial(direction_kernel, moment, scaling),
        in_specs=[WHOLE] * 5,
        out_specs=WHOLE,
        scratch_shapes=[pltpu.VMEM((2, 512, 768), f32)] * 3,
        out_shape=jax.ShapeDtypeStruct((4, 4, 2, 64, 512), bf16),
        compiler_params=pltpu.CompilerParams(vmem_limit_bytes=18 * MIB),
        cost_estimate=pl.CostEstimate(
            flops=2 * 4 * 512 * 512 * 768, bytes_accessed=5000000, transcendentals=0
        ),
        name="direction_parts%d" % moment,
    )(*arrays)


def send_kernel(own, one, two, three, send):
    send[...] = (
        own[1] + one[...].astype(f32) + two[...].astype(f32) + three[...].astype(f32)
    ).astype(bf16)


def send_parts(own, *parts):
    return pl.pallas_call(
        send_kernel,
        in_specs=[WHOLE] * 4,
        out_specs=WHOLE,
        out_shape=jax.ShapeDtypeStruct(own.shape[1:], bf16),
        compiler_params=pltpu.CompilerParams(vmem_limit_bytes=4 * MIB),
        cost_estimate=pl.CostEstimate(flops=300000, bytes_accessed=1500000, transcendentals=0),
        name="send_parts",
    )(own, *parts)


def residual_kernel(own, one, two, three, last, obs, kept, _, resid, half):
    total = own[0] + one[...].astype(f32) + two[...].astype(f32) + three[...].astype(f32)
    value = kept[...] * (obs[...] - (total + last[...].astype(f32)))
    resid[...] = value
    half[...] = value.astype(bf16)


def residual_parts(own, *parts):
    return pl.pallas_call(
        residual_kernel,
        in_specs=[WHOLE] * 7 + [ANY],
        out_specs=[WHOLE] * 2,
        out_shape=[
            jax.ShapeDtypeStruct(own.shape[1:], f32),
            jax.ShapeDtypeStruct(own.shape[1:], bf16),
        ],
        compiler_params=pltpu.CompilerParams(vmem_limit_bytes=4 * MIB),
        cost_estimate=pl.CostEstimate(flops=500000, bytes_accessed=2500000, transcendentals=0),
        name="residual_parts",
    )(own, *parts)


def observed_send_kernel(observed, flags, _, out, sem):
    core, _, _ = position()
    copy = pltpu.make_async_copy(observed.at[:, 1 - core], out.at[:, :, 0:2, :], sem)
    copy.start()
    for moment in range(2):
        keep = flags[:, moment, :].astype(f32)
        out[:, moment, 2, :] = keep
        out[:, moment, 3, :] = keep
    copy.wait()


def observed_send(observed, flags, after):
    rows, _, _, _, stations = observed.shape
    return pl.pallas_call(
        observed_send_kernel,
        in_specs=[HBM, WHOLE, ANY],
        out_specs=WHOLE,
        out_shape=jax.ShapeDtypeStruct((rows, 2, 4, stations), f32),
        scratch_shapes=[pltpu.SemaphoreType.DMA],
        cost_estimate=pl.CostEstimate(flops=100000, bytes_accessed=700000, transcendentals=0),
        compiler_params=pltpu.CompilerParams(vmem_limit_bytes=4 * MIB),
        name="observed_send",
    )(observed, flags, after)


def observed_kernel(observed, flags, other, obs_out, keep_out, own, wide, sem):
    core, y, z = position()
    copy = pltpu.make_async_copy(observed.at[:, core], own, sem)
    copy.start()
    copy.wait()
    chip = z * 4 + y
    start = pl.ds(pl.multiple_of((chip // 2) * 128, 128), 384)
    odd = chip % 2 == 1
    row = lax.broadcasted_iota(jnp.int32, (64, 512), 0)
    col = lax.broadcasted_iota(jnp.int32, (64, 512), 1)
    for moment in range(2):
        for rows, mine in ((core, True), (1 - core, False)):
            there = pl.ds(pl.multiple_of(rows * 32, 32), 32)
            for part in range(3):
                if not mine:
                    value = other[:, moment, part, :]
                elif part == 2:
                    value = flags[:, moment, :].astype(f32)
                else:
                    value = own[:, moment, part, :]
                wide[part, there, 0:512] = value
                wide[part, there, 512:768] = value[:, 0:256]
        obs_out[moment] = pack(wide[0, :, start], wide[1, :, start], odd, z == 0)
        keep = pack(wide[2, :, start], wide[2, :, start], odd, z == 0)
        keep_out[moment] = jnp.where(row == col, 0.0, keep)


def observed_parts(observed, flags, other):
    rows, _, _, _, stations = observed.shape
    return pl.pallas_call(
        observed_kernel,
        in_specs=[HBM] + [WHOLE] * 2,
        out_specs=[WHOLE] * 2,
        out_shape=[jax.ShapeDtypeStruct((2, 64, 512), f32)] * 2,
        scratch_shapes=[
            pltpu.VMEM((rows, 2, 2, stations), f32),
            pltpu.VMEM((3, 64, 768), f32),
            pltpu.SemaphoreType.DMA,
        ],
        cost_estimate=pl.CostEstimate(flops=1000000, bytes_accessed=1500000, transcendentals=0),
        compiler_params=pltpu.CompilerParams(vmem_limit_bytes=6 * MIB),
        name="observed_parts",
    )(observed, flags, other)


def gradient_kernel(flip, freq, *refs):
    sources = refs[0:4]
    parts0, parts1 = refs[4:6]
    out, rows_sum, cols_sum = refs[-3:]
    core, y, z = position()
    zz = 1 - z if flip else z
    for rel, source in enumerate(sources):
        chip = y_partner(rel, y)
        for start in range(0, 64, 32):
            rows = slice(start, start + 32)
            resid0 = source[0, rows, :]
            resid1 = source[1, rows, :]
            for which in range(4):
                product = (resid0 * parts0[which, rel, flip, rows, :]).astype(f32)
                product += (resid1 * parts1[which, rel, flip, rows, :]).astype(f32)
                rows_sum[which, pl.ds(pl.multiple_of(chip * 64 + start, 32), 32), :] = (
                    product[:, 0:128] + product[:, 128:256]
                ) + (product[:, 256:384] + product[:, 384:512])
                column = (product[0:8] + product[8:16]) + (product[16:24] + product[24:32])
                if start == 0:
                    cols_sum[which, chip] = column
                else:
                    cols_sum[which, chip] += column
    near = lax.broadcasted_iota(jnp.int32, (8, 256), 1) < 64
    factor = 2.0 / freq[core]
    pieces = []
    for which in range(4):
        placed = []
        for odd in range(2):
            total = None
            for chip in range(odd, 4, 2):
                low = cols_sum[which, chip, :, 0:256]
                high = cols_sum[which, chip, :, 256:512]
                folded = [low + jnp.where(near, 0.0, high), jnp.where(near, high, 0.0)]
                quarters = [part[:, at : at + 128] for part in folded for at in (0, 128)]
                turn = (4 - chip // 2) % 4
                quarters = quarters[turn:] + quarters[:turn]
                total = quarters if total is None else [a + b for a, b in zip(total, quarters)]
            placed.append(jnp.concatenate(total, axis=1))
        columns = jnp.sum(placed[0] + pltpu.roll(placed[1], 64, 1), axis=0, keepdims=True)
        along_rows = jnp.sum(jnp.transpose(rows_sum[which]), axis=0, keepdims=True)
        first = (along_rows - columns[:, 0:256]) * factor
        second = -columns[:, 256:512] * factor
        low = jnp.where(zz == 0, first, second)
        high = jnp.where(zz == 0, second, first)
        pieces.extend([low[:, 0:128], low[:, 128:256], high[:, 0:128], high[:, 128:256]])
    value = jnp.concatenate(pieces, axis=0)
    if flip == 0:
        out[...] = value
    else:
        value = (value + refs[6][...]).astype(bf16)

        def copy(index, carry):
            out[index] = value
            return carry

        lax.fori_loop(0, out.shape[0], copy, 0, unroll=8)


def gradient_parts(flip, devices, freq, *arrays):
    out = jax.ShapeDtypeStruct((16, 128), f32)
    if flip:
        out = jax.ShapeDtypeStruct((devices, 16, 128), bf16)
    return pl.pallas_call(
        functools.partial(gradient_kernel, flip),
        in_specs=[SCALARS] + [WHOLE] * len(arrays),
        out_specs=WHOLE,
        scratch_shapes=[pltpu.VMEM((4, 256, 128), f32), pltpu.VMEM((4, 4, 8, 512), f32)],
        out_shape=out,
        compiler_params=pltpu.CompilerParams(vmem_limit_bytes=10 * MIB),
        cost_estimate=pl.CostEstimate(flops=5000000, bytes_accessed=3000000, transcendentals=0),
        name="gradient_parts%d" % flip,
    )(freq, *arrays)


def rows_kernel(resid, *refs):
    resids = refs[0:8]
    _, own_out, other_out, rolled = refs[8:]
    core, y, z = position()
    chip = z * 4 + y
    upper, lower = upper_mask()
    even = y % 2 == 0
    flip5 = jnp.where(y < 3, 1, 0)
    flip6 = jnp.where(y < 2, 1, 0)
    flip7 = jnp.where(y < 1, 1, 0)
    for moment in range(2):
        own = resid[moment]
        near = own[:, 0:64]
        near_t = jnp.transpose(near)
        zero = jnp.zeros_like(near)
        near_re = jnp.where(upper, near, jnp.where(lower, near_t, zero))
        near_im = jnp.where(lower, near, jnp.where(upper, -near_t, zero))
        far = own[:, 256:320]
        far_t = jnp.transpose(resids[4][moment][:, 256:320].astype(f32))
        far_re = jnp.where(z == 0, far, far_t)
        far_im = jnp.where(z == 0, -far_t, far)
        one5, two5, block6, one7, two7 = (
            jnp.where(flip == 1, resids[4 + rel][moment], resids[rel][moment]).astype(f32)
            for rel, flip in ((1, flip5), (2, flip5), (3, flip6), (1, flip7), (2, flip7))
        )
        block5 = jnp.where(even, one5, two5)
        block7 = jnp.where(even, two7, one7)
        re = [near_re, own[:, 64:256], far_re]
        im = [near_im, own[:, 320:512], far_im]
        for block, offset in ((block5, 3), (block6, 2), (block7, 1)):
            re.append(jnp.transpose(block[:, 64 * offset : 64 * offset + 64]))
            im.append(-jnp.transpose(block[:, 256 + 64 * offset : 320 + 64 * offset]))
        for part, pieces in enumerate((re, im)):
            index = moment * 2 + part
            rolled[index] = pltpu.roll(jnp.concatenate(pieces, axis=1), chip * 64, 1)
            own_out[index] = rolled[index, pl.ds(pl.multiple_of(core * 32, 32), 32), :]
            other_out[index] = rolled[index, pl.ds(pl.multiple_of((1 - core) * 32, 32), 32), :]


def whole_rows(resid, resids, after):
    return pl.pallas_call(
        rows_kernel,
        in_specs=[WHOLE] * 9 + [ANY],
        out_specs=[WHOLE] * 2,
        out_shape=[jax.ShapeDtypeStruct((4, 32, 512), f32)] * 2,
        scratch_shapes=[pltpu.VMEM((4, 64, 512), f32)],
        cost_estimate=pl.CostEstimate(flops=0, bytes_accessed=0, transcendentals=0),
        compiler_params=pltpu.CompilerParams(vmem_limit_bytes=6 * MIB),
        name="whole_rows",
    )(resid, *resids, after)


def halves(value):
    high = value.astype(bf16)
    return high, (value - high.astype(f32)).astype(bf16)


def update_kernel(grads, kernel, screen, out, total, smooth):
    core, y, z = position()
    per_chip = grads.shape[0] // 8
    for chip in range(8):
        total[chip * 16 : chip * 16 + 16, :] = jnp.sum(
            grads[chip * per_chip : (chip + 1) * per_chip].astype(f32), axis=0
        )
    gradient = jnp.concatenate(
        [total[pl.ds(piece, 32, stride=4), :] for piece in range(4)], axis=1
    )
    grad_high, grad_low = halves(gradient)
    kern_high, kern_low = halves(kernel[...])
    both = jnp.dot(
        jnp.concatenate([grad_high, grad_low], axis=0), kern_high, preferred_element_type=f32
    )
    value = both[0:32] + (
        both[32:64] + jnp.dot(grad_high, kern_low, preferred_element_type=f32)
    )
    mean_sq = jnp.sum(value * value) / value.size
    smooth[...] = value * (step_size * lax.rsqrt(mean_sq + epsilon))
    row = (z * 4 + y) * 4 + core * 2
    for step in range(2):
        out[step : step + 1, :] = screen[step : step + 1, :] - smooth[pl.ds(row + step, 1), :]


def updated_rows(grads, kernel, screen):
    return pl.pallas_call(
        update_kernel,
        in_specs=[WHOLE] * 3,
        out_specs=WHOLE,
        out_shape=jax.ShapeDtypeStruct(screen.shape, f32),
        scratch_shapes=[pltpu.VMEM((128, 128), f32), pltpu.VMEM((32, 512), f32)],
        compiler_params=pltpu.CompilerParams(vmem_limit_bytes=8 * MIB),
        cost_estimate=pl.CostEstimate(flops=200000000, bytes_accessed=1500000, transcendentals=0),
        name="updated_rows",
    )(grads, kernel, screen)


def body(
    observed,
    flags,
    screen,
    screen_kernel,
    station_uv,
    source_lm,
    source_flux,
    station_gain,
    source_direction,
    freq_ratio,
):
    devices = lax.axis_size("dir") * lax.axis_size("freq")
    stations = screen.shape[1]
    scaling = 1.0 / math.sqrt(source_flux.shape[0] * lax.axis_size("dir"))
    core = position()[0]
    swap = functools.partial(lax.ppermute, axis_name="dir", perm=dir_perm(0, flip_core=True))

    inputs = (freq_ratio, station_gain, station_uv, screen, source_lm, source_flux, source_direction)
    other = swap(phasor_send(*inputs))
    own = phasor_own(*inputs)

    def across(rel, array):
        return lax.ppermute(array, "dir", dir_perm(rel))

    def across_z(array):
        return lax.ppermute(array, "dir", dir_perm(0, flip_z=True))

    parts = model_parts(scaling, own, other)
    far = [across(rel, parts[rel]) for rel in (3, 2, 1)]
    near = [across(rel, parts[rel + 3]) for rel in (3, 2, 1)]
    other_observed = swap(observed_send(observed, flags, parts[6]))
    obs, kept = observed_parts(observed, flags, other_observed)
    directions0 = direction_parts(0, scaling, own, other, *parts[7:])
    last = across_z(send_parts(parts[0], *far))
    resid, half = residual_parts(parts[0], *near, last, obs, kept, directions0)
    half_z = across_z(half)
    directions1 = direction_parts(1, scaling, own, other, *parts[7:])
    one, two = across(1, half), across(2, half)
    one_z, two_z = across(1, half_z), across(2, half_z)
    resids = [half, one, two, across(2, one), half_z, one_z, two_z, across(1, two_z)]

    grads = gradient_parts(0, devices, freq_ratio, *resids[:4], directions0, directions1)
    grads = gradient_parts(1, devices, freq_ratio, *resids[4:], directions0, directions1, grads)
    own_rows, sent_rows = whole_rows(resid, resids, grads)
    other_rows = swap(sent_rows)
    grads = lax.all_to_all(grads, ("dir", "freq"), 0, 0, tiled=True)
    updated = updated_rows(grads, screen_kernel, screen)

    first = jnp.where(core == 0, own_rows, other_rows)
    second = jnp.where(core == 0, other_rows, own_rows)
    residual = jnp.stack([first, second]).reshape(2, 2, 2, 32, stations)
    return jnp.transpose(residual, (3, 0, 1, 2, 4)), updated


def solution(mesh):
    placed = (
        P("dir", "freq", None, None, None),
        P("dir", None, None),
        P("dir", None),
        P(),
        P(),
        P(None, "dir"),
        P("dir"),
        P("freq", None, None, None, "dir"),
        P("dir"),
        P("freq"),
    )
    return jax.shard_map(
        body,
        mesh=mesh,
        in_specs=placed,
        out_specs=(P("dir", "freq", None, None, None), P("dir", None)),
        check_vma=False,
    )
```

```python
import functools
import math

import jax
import jax.numpy as jnp
from jax import lax
from jax.experimental import pallas as pl
from jax.experimental.pallas import tpu as pltpu
from jax.sharding import PartitionSpec as P

step_size = 0.3
epsilon = 1e-06
highest = lax.Precision.HIGHEST
bf16 = jnp.bfloat16
f32 = jnp.float32

SIN_COEF = (4.44288292, -7.3082457, 3.60635441, -0.84611289, 0.10982699)
COS_COEF = (1.4142135, -6.97885099, 5.73946117, -1.88356299, 0.31069819)
ROUNDER = 12582912.0
CHUNK = 32
MIB = 1024 * 1024
NT = (((1,), (1,)), ((), ()))


def y_partner(rel, y):
    if rel == 0:
        return y
    if rel == 1:
        return y + 1 - 2 * (y % 2)
    if rel == 2:
        return 3 - y
    return (y + 2) % 4


def dir_perm(rel, flip_z=False, flip_core=False):
    pairs = []
    for index in range(16):
        z, y, core = index // 8, (index // 2) % 4, index % 2
        z = 1 - z if flip_z else z
        core = 1 - core if flip_core else core
        pairs.append((index, z * 8 + y_partner(rel, y) * 2 + core))
    return pairs


ANY = pl.BlockSpec(memory_space=pl.ANY)
HBM = pl.BlockSpec(memory_space=pltpu.HBM)
WHOLE = pl.BlockSpec(memory_space=pltpu.VMEM)
SCALARS = pl.BlockSpec(memory_space=pltpu.SMEM)


def position():
    index = lax.axis_index("dir")
    return index % 2, (index // 2) % 4, index // 8


def phasor_rows(channel, freq, gain_of, uv, screen, lm, flux, direction, out, ready):
    stations, sources = screen.shape[1], lm.shape[1]
    ratio = freq[channel]
    along = lm[0:1, :] * ratio
    across = lm[1:2, :] * ratio
    amp = jnp.sqrt(flux[...])
    second = direction[...] > 0
    per_turn = 1.0 / (2.0 * math.pi * ratio)
    by_station = jnp.concatenate(
        [uv[0], uv[1], screen[...] * per_turn, jnp.zeros((2, stations), f32)], axis=0
    )
    cols = jnp.transpose(by_station)
    mask = jnp.broadcast_to(jnp.where(second, 1.0, 0.0), (16, sources)).astype(bf16)
    for moment in range(2):
        for start in range(0, stations, CHUNK):
            ready(moment, start)
            rows = slice(start, start + CHUNK)
            col = cols[rows]
            u = col[:, 2 * moment : 2 * moment + 1]
            v = col[:, 2 * moment + 1 : 2 * moment + 2]
            turns = u * along + v * across + jnp.where(second, col[:, 5:6], col[:, 4:5])
            turns = turns - ((turns + ROUNDER) - ROUNDER)
            z = turns * turns
            sin_half = SIN_COEF[4]
            cos_half = COS_COEF[4]
            for power in (3, 2, 1, 0):
                sin_half = sin_half * z + SIN_COEF[power]
                cos_half = cos_half * z + COS_COEF[power]
            sin_half = sin_half * turns
            sin_amp = sin_half * amp
            sine = sin_amp * cos_half
            cosine = amp - sin_amp * sin_half
            gain_re = gain_of(moment, 0, rows).astype(f32)
            gain_im = gain_of(moment, 1, rows).astype(f32)
            out[moment, rows, 0:sources] = (gain_re * cosine - gain_im * sine).astype(bf16)
            out[moment, rows, sources : 2 * sources] = (
                gain_re * sine + gain_im * cosine
            ).astype(bf16)
        out[moment, stations : stations + 16, 0:sources] = mask
        out[moment, stations : stations + 16, sources : 2 * sources] = mask


def phasor_send_kernel(
    freq, gain, uv, screen, lm, flux, direction, out_hbm, *rest
):
    out, out_sems, held, freq_held, uv_held, screen_held, lm_held, flux_held, direction_held, sems = rest
    core, _, _ = position()
    channel = 1 - core
    quarter = gain.shape[3] // 4
    loads = [
        pltpu.make_async_copy(source, target, sems.at[8 + index])
        for index, (source, target) in enumerate(
            (
                (freq, freq_held),
                (uv, uv_held),
                (screen, screen_held),
                (lm, lm_held),
                (flux, flux_held.at[0]),
                (direction, direction_held.at[0]),
            )
        )
    ]
    copies = []
    for moment in range(2):
        for part in range(4):
            rows = pl.ds(part * quarter, quarter)
            copies.append(
                pltpu.make_async_copy(
                    gain.at[channel, moment, :, rows, :],
                    held.at[moment, :, rows, :],
                    sems.at[moment * 4 + part],
                )
            )
    for copy in loads + copies:
        copy.start()
    for load in loads:
        load.wait()

    half = gain.shape[3] // 2
    writes = []

    def write(moment, start, size):
        rows = pl.ds(start, size)
        writes.append(
            pltpu.make_async_copy(
                out.at[moment, rows, :], out_hbm.at[moment, rows, :], out_sems.at[len(writes)]
            )
        )
        writes[-1].start()

    def ready(moment, start):
        if start % quarter == 0:
            copies[moment * 4 + start // quarter].wait()
        if start == half:
            write(moment, 0, half)
        if start == 0 and moment == 1:
            write(0, half, half + 16)

    def gain_of(moment, part, rows):
        return held[moment, part, rows, :]

    phasor_rows(
        channel, freq_held, gain_of, uv_held, screen_held, lm_held, flux_held, direction_held, out, ready
    )
    write(1, half, half + 16)
    for copy in writes:
        copy.wait()


def phasor_own_kernel(freq, gain, uv, screen, lm, flux, direction, out, flux_held, direction_held, sems):
    channel = position()[0]
    loads = [
        pltpu.make_async_copy(flux, flux_held.at[0], sems.at[0]),
        pltpu.make_async_copy(direction, direction_held.at[0], sems.at[1]),
    ]
    for load in loads:
        load.start()
    for load in loads:
        load.wait()

    def gain_of(moment, part, rows):
        return gain[channel, moment, part, rows, :]

    phasor_rows(
        channel, freq, gain_of, uv, screen, lm, flux_held, direction_held, out, lambda moment, start: None
    )


def phasor_send(*inputs):
    gain = inputs[1]
    stations, sources = gain.shape[3], gain.shape[4]
    return pl.pallas_call(
        phasor_send_kernel,
        in_specs=[HBM] * 7,
        out_specs=HBM,
        out_shape=jax.ShapeDtypeStruct((2, stations + 16, 2 * sources), bf16),
        scratch_shapes=[
            pltpu.VMEM((2, stations + 16, 2 * sources), bf16),
            pltpu.SemaphoreType.DMA((4,)),
            pltpu.VMEM((2, 2, stations, sources), bf16),
            pltpu.SMEM(inputs[0].shape, f32),
        ]
        + [pltpu.VMEM(array.shape, f32) for array in inputs[2:5]]
        + [pltpu.VMEM((1, sources), f32), pltpu.VMEM((1, sources), jnp.int32)]
        + [pltpu.SemaphoreType.DMA((14,))],
        compiler_params=pltpu.CompilerParams(vmem_limit_bytes=60 * MIB),
        cost_estimate=pl.CostEstimate(
            flops=40 * 2 * stations * sources, bytes_accessed=3200000, transcendentals=0
        ),
        name="phasor_send",
    )(*inputs)


def phasor_own(*inputs):
    gain = inputs[1]
    stations, sources = gain.shape[3], gain.shape[4]
    return pl.pallas_call(
        phasor_own_kernel,
        in_specs=[SCALARS] + [WHOLE] * 4 + [ANY] * 2,
        out_specs=WHOLE,
        out_shape=jax.ShapeDtypeStruct((2, stations + 16, 2 * sources), bf16),
        scratch_shapes=[
            pltpu.VMEM((1, sources), f32),
            pltpu.VMEM((1, sources), jnp.int32),
            pltpu.SemaphoreType.DMA((2,)),
        ],
        compiler_params=pltpu.CompilerParams(vmem_limit_bytes=16 * MIB),
        cost_estimate=pl.CostEstimate(
            flops=40 * 2 * stations * sources, bytes_accessed=3200000, transcendentals=0
        ),
        name="phasor_own",
    )(*inputs)


def upper_mask():
    row = lax.broadcasted_iota(jnp.int32, (64, 64), 0)
    col = lax.broadcasted_iota(jnp.int32, (64, 64), 1)
    return row < col, row > col


def pack(re, im, odd, keep_re):
    re = jnp.where(odd, pltpu.roll(re, 320, 1), re)
    im = jnp.where(odd, pltpu.roll(im, 320, 1), im)
    row = lax.broadcasted_iota(jnp.int32, (64, 128), 0)
    col = lax.broadcasted_iota(jnp.int32, (64, 128), 1)
    near = col < 64
    far = jnp.where(keep_re, re[:, 256:384], im[:, 256:384])
    return jnp.concatenate(
        [
            jnp.where(near & (row >= col), im[:, 0:128], re[:, 0:128]),
            re[:, 128:256],
            jnp.where(near, far, im[:, 0:128]),
            im[:, 128:256],
        ],
        axis=1,
    )


def skewed(q):
    half = q.shape[1] // 2
    return jnp.concatenate([q[:, half:], -q[:, :half]], axis=1)


def mm(a, b):
    return lax.dot_general(a, b, NT, preferred_element_type=f32)


def fill_wide(wide, part, top, bottom):
    wide[part, 0:256, 0:512] = top
    wide[part, 256:512, 256:512] = bottom
    corner = jnp.transpose(top[:, 256:512])
    wide[part, 256:512, 512:768] = corner if part == 0 else -corner


def fill_gram(wide, left, right, scaling):
    for part, rows in ((0, left), (1, skewed(left))):
        value = mm(rows, right) * scaling
        wide[part, :, 0:512] = value
        wide[part, :, 512:768] = value[:, 0:256]


def block_of(wide, part, chip):
    start = pl.multiple_of((chip // 2) * 128, 128)
    return wide[part, pl.ds(pl.multiple_of(chip * 64, 64), 64), pl.ds(start, 384)]


def model_kernel(scaling, own, other_hbm, stay, out11, out21, out31, out10, out20, out30, wides, tops, bottoms, other, sems):
    _, y, z = position()
    copies = [
        pltpu.make_async_copy(other_hbm.at[moment], other.at[moment], sems.at[moment])
        for moment in range(2)
    ]
    for copy in copies:
        copy.start()
    for moment in range(2):
        wide, top, bottom = wides.at[moment], tops.at[moment], bottoms.at[moment]
        q = own[moment, 0:512, :]
        for part, rows in ((0, q), (1, skewed(q))):
            top[part] = mm(rows[0:256], q) * scaling
            bottom[part] = mm(rows[256:512], q[256:512]) * scaling
        copies[moment].wait()
        q = other[moment, 0:512, :]
        for part, rows in ((0, q), (1, skewed(q))):
            fill_wide(
                wide,
                part,
                top[part] + mm(rows[0:256], q) * scaling,
                bottom[part] + mm(rows[256:512], q[256:512]) * scaling,
            )
        for flip, outs in ((1, (out11, out21, out31)), (0, (out10, out20, out30))):
            for rel in range(4):
                zz = 1 - z if flip else z
                chip = zz * 4 + y_partner(rel, y)
                value = pack(
                    block_of(wide, 0, chip), block_of(wide, 1, chip), chip % 2 == 1, zz == 0
                )
                if rel == 0:
                    stay[flip, moment] = value
                else:
                    outs[rel - 1][moment] = value.astype(bf16)


def model_parts(scaling, own, other):
    return pl.pallas_call(
        functools.partial(model_kernel, scaling),
        in_specs=[WHOLE, HBM],
        out_specs=[WHOLE] * 10,
        scratch_shapes=[pltpu.VMEM(own.shape, bf16), pltpu.SemaphoreType.DMA((2,))],
        out_shape=[jax.ShapeDtypeStruct((2, 2, 64, 512), f32)]
        + [jax.ShapeDtypeStruct((2, 64, 512), bf16)] * 6
        + [
            jax.ShapeDtypeStruct((2, 2, 512, 768), f32),
            jax.ShapeDtypeStruct((2, 2, 256, 512), f32),
            jax.ShapeDtypeStruct((2, 2, 256, 256), f32),
        ],
        compiler_params=pltpu.CompilerParams(vmem_limit_bytes=20 * MIB),
        cost_estimate=pl.CostEstimate(
            flops=2 * 2 * 4 * 512 * 512 * 768, bytes_accessed=5000000, transcendentals=0
        ),
        name="model_parts",
    )(own, other)


def direction_kernel(moment, scaling, own, other, totals, tops, bottoms, out, mine, first_own, first_other):
    core, y, z = position()
    total = totals.at[moment]
    for part in range(2):
        fill_wide(mine, part, tops[moment, part], bottoms[moment, part])
    for source, first in ((own, first_own), (other, first_other)):
        q = source[moment, 0:512, :]
        in_first = source[moment, 512:513, :] < 0.5
        fill_gram(first, jnp.where(in_first, q, jnp.zeros_like(q)), q, scaling)
    for rel in range(4):
        for flip in range(2):
            zz = 1 - z if flip else z
            chip = zz * 4 + y_partner(rel, y)
            whole, own_all, own_first, other_first = (
                pack(block_of(wide, 1, chip), -block_of(wide, 0, chip), chip % 2 == 1, zz == 0)
                for wide in (total, mine, first_own, first_other)
            )
            out[core * 2, rel, flip] = own_first.astype(bf16)
            out[core * 2 + 1, rel, flip] = (own_all - own_first).astype(bf16)
            out[2 - core * 2, rel, flip] = other_first.astype(bf16)
            out[3 - core * 2, rel, flip] = ((whole - own_all) - other_first).astype(bf16)


def direction_parts(moment, scaling, *arrays):
    return pl.pallas_call(
        functools.partial(direction_kernel, moment, scaling),
        in_specs=[WHOLE] * 5,
        out_specs=WHOLE,
        scratch_shapes=[pltpu.VMEM((2, 512, 768), f32)] * 3,
        out_shape=jax.ShapeDtypeStruct((4, 4, 2, 64, 512), bf16),
        compiler_params=pltpu.CompilerParams(vmem_limit_bytes=18 * MIB),
        cost_estimate=pl.CostEstimate(
            flops=2 * 4 * 512 * 512 * 768, bytes_accessed=5000000, transcendentals=0
        ),
        name="direction_parts%d" % moment,
    )(*arrays)


def send_kernel(own, one, two, three, send):
    send[...] = (
        own[1] + one[...].astype(f32) + two[...].astype(f32) + three[...].astype(f32)
    ).astype(bf16)


def send_parts(own, *parts):
    return pl.pallas_call(
        send_kernel,
        in_specs=[WHOLE] * 4,
        out_specs=WHOLE,
        out_shape=jax.ShapeDtypeStruct(own.shape[1:], bf16),
        compiler_params=pltpu.CompilerParams(vmem_limit_bytes=4 * MIB),
        cost_estimate=pl.CostEstimate(flops=300000, bytes_accessed=1500000, transcendentals=0),
        name="send_parts",
    )(own, *parts)


def residual_kernel(own, one, two, three, last, obs, kept, _, resid, half):
    total = own[0] + one[...].astype(f32) + two[...].astype(f32) + three[...].astype(f32)
    value = kept[...] * (obs[...] - (total + last[...].astype(f32)))
    resid[...] = value
    half[...] = value.astype(bf16)


def residual_parts(own, *parts):
    return pl.pallas_call(
        residual_kernel,
        in_specs=[WHOLE] * 7 + [ANY],
        out_specs=[WHOLE] * 2,
        out_shape=[
            jax.ShapeDtypeStruct(own.shape[1:], f32),
            jax.ShapeDtypeStruct(own.shape[1:], bf16),
        ],
        compiler_params=pltpu.CompilerParams(vmem_limit_bytes=4 * MIB),
        cost_estimate=pl.CostEstimate(flops=500000, bytes_accessed=2500000, transcendentals=0),
        name="residual_parts",
    )(own, *parts)


def observed_send_kernel(observed, flags, _, out, sem):
    core, _, _ = position()
    copy = pltpu.make_async_copy(observed.at[:, 1 - core], out.at[:, :, 0:2, :], sem)
    copy.start()
    for moment in range(2):
        keep = flags[:, moment, :].astype(f32)
        out[:, moment, 2, :] = keep
        out[:, moment, 3, :] = keep
    copy.wait()


def observed_send(observed, flags, after):
    rows, _, _, _, stations = observed.shape
    return pl.pallas_call(
        observed_send_kernel,
        in_specs=[HBM, WHOLE, ANY],
        out_specs=WHOLE,
        out_shape=jax.ShapeDtypeStruct((rows, 2, 4, stations), f32),
        scratch_shapes=[pltpu.SemaphoreType.DMA],
        cost_estimate=pl.CostEstimate(flops=100000, bytes_accessed=700000, transcendentals=0),
        compiler_params=pltpu.CompilerParams(vmem_limit_bytes=4 * MIB),
        name="observed_send",
    )(observed, flags, after)


def observed_kernel(observed, flags, other, obs_out, keep_out, own, wide, sem):
    core, y, z = position()
    copy = pltpu.make_async_copy(observed.at[:, core], own, sem)
    copy.start()
    copy.wait()
    chip = z * 4 + y
    start = pl.ds(pl.multiple_of((chip // 2) * 128, 128), 384)
    odd = chip % 2 == 1
    row = lax.broadcasted_iota(jnp.int32, (64, 512), 0)
    col = lax.broadcasted_iota(jnp.int32, (64, 512), 1)
    for moment in range(2):
        for rows, mine in ((core, True), (1 - core, False)):
            there = pl.ds(pl.multiple_of(rows * 32, 32), 32)
            for part in range(3):
                if not mine:
                    value = other[:, moment, part, :]
                elif part == 2:
                    value = flags[:, moment, :].astype(f32)
                else:
                    value = own[:, moment, part, :]
                wide[part, there, 0:512] = value
                wide[part, there, 512:768] = value[:, 0:256]
        obs_out[moment] = pack(wide[0, :, start], wide[1, :, start], odd, z == 0)
        keep = pack(wide[2, :, start], wide[2, :, start], odd, z == 0)
        keep_out[moment] = jnp.where(row == col, 0.0, keep)


def observed_parts(observed, flags, other):
    rows, _, _, _, stations = observed.shape
    return pl.pallas_call(
        observed_kernel,
        in_specs=[HBM] + [WHOLE] * 2,
        out_specs=[WHOLE] * 2,
        out_shape=[jax.ShapeDtypeStruct((2, 64, 512), f32)] * 2,
        scratch_shapes=[
            pltpu.VMEM((rows, 2, 2, stations), f32),
            pltpu.VMEM((3, 64, 768), f32),
            pltpu.SemaphoreType.DMA,
        ],
        cost_estimate=pl.CostEstimate(flops=1000000, bytes_accessed=1500000, transcendentals=0),
        compiler_params=pltpu.CompilerParams(vmem_limit_bytes=6 * MIB),
        name="observed_parts",
    )(observed, flags, other)


def gradient_kernel(flip, freq, *refs):
    sources = refs[0:4]
    parts0, parts1 = refs[4:6]
    out, rows_sum, cols_sum = refs[-3:]
    core, y, z = position()
    zz = 1 - z if flip else z
    for rel, source in enumerate(sources):
        chip = y_partner(rel, y)
        for start in range(0, 64, 32):
            rows = slice(start, start + 32)
            resid0 = source[0, rows, :]
            resid1 = source[1, rows, :]
            for which in range(4):
                product = (resid0 * parts0[which, rel, flip, rows, :]).astype(f32)
                product += (resid1 * parts1[which, rel, flip, rows, :]).astype(f32)
                rows_sum[which, pl.ds(pl.multiple_of(chip * 64 + start, 32), 32), :] = (
                    product[:, 0:128] + product[:, 128:256]
                ) + (product[:, 256:384] + product[:, 384:512])
                column = (product[0:8] + product[8:16]) + (product[16:24] + product[24:32])
                if start == 0:
                    cols_sum[which, chip] = column
                else:
                    cols_sum[which, chip] += column
    near = lax.broadcasted_iota(jnp.int32, (8, 256), 1) < 64
    factor = 2.0 / freq[core]
    pieces = []
    for which in range(4):
        placed = []
        for odd in range(2):
            total = None
            for chip in range(odd, 4, 2):
                low = cols_sum[which, chip, :, 0:256]
                high = cols_sum[which, chip, :, 256:512]
                folded = [low + jnp.where(near, 0.0, high), jnp.where(near, high, 0.0)]
                quarters = [part[:, at : at + 128] for part in folded for at in (0, 128)]
                turn = (4 - chip // 2) % 4
                quarters = quarters[turn:] + quarters[:turn]
                total = quarters if total is None else [a + b for a, b in zip(total, quarters)]
            placed.append(jnp.concatenate(total, axis=1))
        columns = jnp.sum(placed[0] + pltpu.roll(placed[1], 64, 1), axis=0, keepdims=True)
        along_rows = jnp.sum(jnp.transpose(rows_sum[which]), axis=0, keepdims=True)
        first = (along_rows - columns[:, 0:256]) * factor
        second = -columns[:, 256:512] * factor
        low = jnp.where(zz == 0, first, second)
        high = jnp.where(zz == 0, second, first)
        pieces.extend([low[:, 0:128], low[:, 128:256], high[:, 0:128], high[:, 128:256]])
    value = jnp.concatenate(pieces, axis=0)
    if flip == 0:
        out[...] = value
    else:
        value = (value + refs[6][...]).astype(bf16)

        def copy(index, carry):
            out[index] = value
            return carry

        lax.fori_loop(0, out.shape[0], copy, 0, unroll=8)


def gradient_parts(flip, devices, freq, *arrays):
    out = jax.ShapeDtypeStruct((16, 128), f32)
    if flip:
        out = jax.ShapeDtypeStruct((devices, 16, 128), bf16)
    return pl.pallas_call(
        functools.partial(gradient_kernel, flip),
        in_specs=[SCALARS] + [WHOLE] * len(arrays),
        out_specs=WHOLE,
        scratch_shapes=[pltpu.VMEM((4, 256, 128), f32), pltpu.VMEM((4, 4, 8, 512), f32)],
        out_shape=out,
        compiler_params=pltpu.CompilerParams(vmem_limit_bytes=10 * MIB),
        cost_estimate=pl.CostEstimate(flops=5000000, bytes_accessed=3000000, transcendentals=0),
        name="gradient_parts%d" % flip,
    )(freq, *arrays)


def rows_kernel(resid, *refs):
    resids = refs[0:8]
    _, own_out, other_out, rolled = refs[8:]
    core, y, z = position()
    chip = z * 4 + y
    upper, lower = upper_mask()
    even = y % 2 == 0
    flip5 = jnp.where(y < 3, 1, 0)
    flip6 = jnp.where(y < 2, 1, 0)
    flip7 = jnp.where(y < 1, 1, 0)
    for moment in range(2):
        own = resid[moment]
        near = own[:, 0:64]
        near_t = jnp.transpose(near)
        zero = jnp.zeros_like(near)
        near_re = jnp.where(upper, near, jnp.where(lower, near_t, zero))
        near_im = jnp.where(lower, near, jnp.where(upper, -near_t, zero))
        far = own[:, 256:320]
        far_t = jnp.transpose(resids[4][moment][:, 256:320].astype(f32))
        far_re = jnp.where(z == 0, far, far_t)
        far_im = jnp.where(z == 0, -far_t, far)
        one5, two5, block6, one7, two7 = (
            jnp.where(flip == 1, resids[4 + rel][moment], resids[rel][moment]).astype(f32)
            for rel, flip in ((1, flip5), (2, flip5), (3, flip6), (1, flip7), (2, flip7))
        )
        block5 = jnp.where(even, one5, two5)
        block7 = jnp.where(even, two7, one7)
        re = [near_re, own[:, 64:256], far_re]
        im = [near_im, own[:, 320:512], far_im]
        for block, offset in ((block5, 3), (block6, 2), (block7, 1)):
            re.append(jnp.transpose(block[:, 64 * offset : 64 * offset + 64]))
            im.append(-jnp.transpose(block[:, 256 + 64 * offset : 320 + 64 * offset]))
        for part, pieces in enumerate((re, im)):
            index = moment * 2 + part
            rolled[index] = pltpu.roll(jnp.concatenate(pieces, axis=1), chip * 64, 1)
            own_out[index] = rolled[index, pl.ds(pl.multiple_of(core * 32, 32), 32), :]
            other_out[index] = rolled[index, pl.ds(pl.multiple_of((1 - core) * 32, 32), 32), :]


def whole_rows(resid, resids, after):
    return pl.pallas_call(
        rows_kernel,
        in_specs=[WHOLE] * 9 + [ANY],
        out_specs=[WHOLE] * 2,
        out_shape=[jax.ShapeDtypeStruct((4, 32, 512), f32)] * 2,
        scratch_shapes=[pltpu.VMEM((4, 64, 512), f32)],
        cost_estimate=pl.CostEstimate(flops=0, bytes_accessed=0, transcendentals=0),
        compiler_params=pltpu.CompilerParams(vmem_limit_bytes=6 * MIB),
        name="whole_rows",
    )(resid, *resids, after)


def assemble_kernel(own, other, out):
    core = position()[0]
    for channel, source in ((core, own), (1 - core, other)):
        for moment in range(2):
            for part in range(2):
                out[:, channel, moment, part, :] = source[moment * 2 + part]


def assemble(own, other, like):
    return pl.pallas_call(
        assemble_kernel,
        in_specs=[WHOLE] * 2,
        out_specs=WHOLE,
        out_shape=jax.ShapeDtypeStruct(like.shape, f32),
        compiler_params=pltpu.CompilerParams(vmem_limit_bytes=4 * MIB),
        cost_estimate=pl.CostEstimate(flops=0, bytes_accessed=0, transcendentals=0),
        name="assemble",
    )(own, other)


def halves(value):
    high = value.astype(bf16)
    return high, (value - high.astype(f32)).astype(bf16)


def update_kernel(grads, kernel, screen, out, total, smooth):
    core, y, z = position()
    per_chip = grads.shape[0] // 8
    for chip in range(8):
        total[chip * 16 : chip * 16 + 16, :] = jnp.sum(
            grads[chip * per_chip : (chip + 1) * per_chip].astype(f32), axis=0
        )
    gradient = jnp.concatenate(
        [total[pl.ds(piece, 32, stride=4), :] for piece in range(4)], axis=1
    )
    grad_high, grad_low = halves(gradient)
    kern_high, kern_low = halves(kernel[...])
    both = jnp.dot(
        jnp.concatenate([grad_high, grad_low], axis=0), kern_high, preferred_element_type=f32
    )
    value = both[0:32] + (
        both[32:64] + jnp.dot(grad_high, kern_low, preferred_element_type=f32)
    )
    mean_sq = jnp.sum(value * value) / value.size
    smooth[...] = value * (step_size * lax.rsqrt(mean_sq + epsilon))
    row = (z * 4 + y) * 4 + core * 2
    for step in range(2):
        out[step : step + 1, :] = screen[step : step + 1, :] - smooth[pl.ds(row + step, 1), :]


def updated_rows(grads, kernel, screen):
    return pl.pallas_call(
        update_kernel,
        in_specs=[WHOLE] * 3,
        out_specs=WHOLE,
        out_shape=jax.ShapeDtypeStruct(screen.shape, f32),
        scratch_shapes=[pltpu.VMEM((128, 128), f32), pltpu.VMEM((32, 512), f32)],
        compiler_params=pltpu.CompilerParams(vmem_limit_bytes=8 * MIB),
        cost_estimate=pl.CostEstimate(flops=200000000, bytes_accessed=1500000, transcendentals=0),
        name="updated_rows",
    )(grads, kernel, screen)


def body(
    observed,
    flags,
    screen,
    screen_kernel,
    station_uv,
    source_lm,
    source_flux,
    station_gain,
    source_direction,
    freq_ratio,
):
    devices = lax.axis_size("dir") * lax.axis_size("freq")
    stations = screen.shape[1]
    scaling = 1.0 / math.sqrt(source_flux.shape[0] * lax.axis_size("dir"))
    core = position()[0]
    swap = functools.partial(lax.ppermute, axis_name="dir", perm=dir_perm(0, flip_core=True))

    inputs = (freq_ratio, station_gain, station_uv, screen, source_lm, source_flux, source_direction)
    other = swap(phasor_send(*inputs))
    own = phasor_own(*inputs)

    def across(rel, array):
        return lax.ppermute(array, "dir", dir_perm(rel))

    def across_z(array):
        return lax.ppermute(array, "dir", dir_perm(0, flip_z=True))

    parts = model_parts(scaling, own, other)
    far = [across(rel, parts[rel]) for rel in (3, 2, 1)]
    near = [across(rel, parts[rel + 3]) for rel in (3, 2, 1)]
    other_observed = swap(observed_send(observed, flags, parts[6]))
    obs, kept = observed_parts(observed, flags, other_observed)
    directions0 = direction_parts(0, scaling, own, other, *parts[7:])
    last = across_z(send_parts(parts[0], *far))
    resid, half = residual_parts(parts[0], *near, last, obs, kept, directions0)
    half_z = across_z(half)
    directions1 = direction_parts(1, scaling, own, other, *parts[7:])
    resids = [
        array if rel == 0 else across(rel, array) for array in (half, half_z) for rel in range(4)
    ]

    grads = gradient_parts(0, devices, freq_ratio, *resids[:4], directions0, directions1)
    grads = gradient_parts(1, devices, freq_ratio, *resids[4:], directions0, directions1, grads)
    own_rows, sent_rows = whole_rows(resid, resids, grads)
    other_rows = swap(sent_rows)
    grads = lax.all_to_all(grads, ("dir", "freq"), 0, 0, tiled=True)
    updated = updated_rows(grads, screen_kernel, screen)

    return assemble(own_rows, other_rows, observed), updated


def solution(mesh):
    placed = (
        P("dir", "freq", None, None, None),
        P("dir", None, None),
        P("dir", None),
        P(),
        P(),
        P(None, "dir"),
        P("dir"),
        P("freq", None, None, None, "dir"),
        P("dir"),
        P("freq"),
    )
    return jax.shard_map(
        body,
        mesh=mesh,
        in_specs=placed,
        out_specs=(P("dir", "freq", None, None, None), P("dir", None)),
        check_vma=False,
    )
```

```python
import functools
import math

import jax
import jax.numpy as jnp
from jax import lax
from jax.experimental import pallas as pl
from jax.experimental.pallas import tpu as pltpu
from jax.sharding import PartitionSpec as P

step_size = 0.3
epsilon = 1e-06
highest = lax.Precision.HIGHEST
bf16 = jnp.bfloat16
f32 = jnp.float32

SIN_COEF = (4.44288292, -7.3082457, 3.60635441, -0.84611289, 0.10982699)
COS_COEF = (1.4142135, -6.97885099, 5.73946117, -1.88356299, 0.31069819)
ROUNDER = 12582912.0
CHUNK = 32
MIB = 1024 * 1024
NT = (((1,), (1,)), ((), ()))


def y_partner(rel, y):
    if rel == 0:
        return y
    if rel == 1:
        return y + 1 - 2 * (y % 2)
    if rel == 2:
        return 3 - y
    return (y + 2) % 4


def dir_perm(rel, flip_z=False, flip_core=False):
    pairs = []
    for index in range(16):
        z, y, core = index // 8, (index // 2) % 4, index % 2
        z = 1 - z if flip_z else z
        core = 1 - core if flip_core else core
        pairs.append((index, z * 8 + y_partner(rel, y) * 2 + core))
    return pairs


ANY = pl.BlockSpec(memory_space=pl.ANY)
HBM = pl.BlockSpec(memory_space=pltpu.HBM)
WHOLE = pl.BlockSpec(memory_space=pltpu.VMEM)
SCALARS = pl.BlockSpec(memory_space=pltpu.SMEM)


def position():
    index = lax.axis_index("dir")
    return index % 2, (index // 2) % 4, index // 8


def phasor_rows(channel, freq, gain_of, uv, screen, lm, flux, direction, out, ready):
    stations, sources = screen.shape[1], lm.shape[1]
    ratio = freq[channel]
    along = lm[0:1, :] * ratio
    across = lm[1:2, :] * ratio
    amp = jnp.sqrt(flux[...])
    second = direction[...] > 0
    per_turn = 1.0 / (2.0 * math.pi * ratio)
    by_station = jnp.concatenate(
        [uv[0], uv[1], screen[...] * per_turn, jnp.zeros((2, stations), f32)], axis=0
    )
    cols = jnp.transpose(by_station)
    mask = jnp.broadcast_to(jnp.where(second, 1.0, 0.0), (16, sources)).astype(bf16)
    for moment in range(2):
        for start in range(0, stations, CHUNK):
            ready(moment, start)
            rows = slice(start, start + CHUNK)
            col = cols[rows]
            u = col[:, 2 * moment : 2 * moment + 1]
            v = col[:, 2 * moment + 1 : 2 * moment + 2]
            turns = u * along + v * across + jnp.where(second, col[:, 5:6], col[:, 4:5])
            turns = turns - ((turns + ROUNDER) - ROUNDER)
            z = turns * turns
            sin_half = SIN_COEF[4]
            cos_half = COS_COEF[4]
            for power in (3, 2, 1, 0):
                sin_half = sin_half * z + SIN_COEF[power]
                cos_half = cos_half * z + COS_COEF[power]
            sin_half = sin_half * turns
            sin_amp = sin_half * amp
            sine = sin_amp * cos_half
            cosine = amp - sin_amp * sin_half
            gain_re = gain_of(moment, 0, rows).astype(f32)
            gain_im = gain_of(moment, 1, rows).astype(f32)
            out[moment, rows, 0:sources] = (gain_re * cosine - gain_im * sine).astype(bf16)
            out[moment, rows, sources : 2 * sources] = (
                gain_re * sine + gain_im * cosine
            ).astype(bf16)
        out[moment, stations : stations + 16, 0:sources] = mask
        out[moment, stations : stations + 16, sources : 2 * sources] = mask


def phasor_send_kernel(
    freq, gain, uv, screen, lm, flux, direction, out_hbm, *rest
):
    out, out_sems, held, freq_held, uv_held, screen_held, lm_held, flux_held, direction_held, sems = rest
    core, _, _ = position()
    channel = 1 - core
    quarter = gain.shape[3] // 4
    loads = [
        pltpu.make_async_copy(source, target, sems.at[8 + index])
        for index, (source, target) in enumerate(
            (
                (freq, freq_held),
                (uv, uv_held),
                (screen, screen_held),
                (lm, lm_held),
                (flux, flux_held.at[0]),
                (direction, direction_held.at[0]),
            )
        )
    ]
    copies = []
    for moment in range(2):
        for part in range(4):
            rows = pl.ds(part * quarter, quarter)
            copies.append(
                pltpu.make_async_copy(
                    gain.at[channel, moment, :, rows, :],
                    held.at[moment, :, rows, :],
                    sems.at[moment * 4 + part],
                )
            )
    for copy in loads + copies:
        copy.start()
    for load in loads:
        load.wait()

    half = gain.shape[3] // 2
    writes = []

    def write(moment, start, size):
        rows = pl.ds(start, size)
        writes.append(
            pltpu.make_async_copy(
                out.at[moment, rows, :], out_hbm.at[moment, rows, :], out_sems.at[len(writes)]
            )
        )
        writes[-1].start()

    def ready(moment, start):
        if start % quarter == 0:
            copies[moment * 4 + start // quarter].wait()
        if start == half:
            write(moment, 0, half)
        if start == 0 and moment == 1:
            write(0, half, half + 16)

    def gain_of(moment, part, rows):
        return held[moment, part, rows, :]

    phasor_rows(
        channel, freq_held, gain_of, uv_held, screen_held, lm_held, flux_held, direction_held, out, ready
    )
    write(1, half, half + 16)
    for copy in writes:
        copy.wait()


def phasor_own_kernel(freq, gain, uv, screen, lm, flux, direction, out, flux_held, direction_held, sems):
    channel = position()[0]
    loads = [
        pltpu.make_async_copy(flux, flux_held.at[0], sems.at[0]),
        pltpu.make_async_copy(direction, direction_held.at[0], sems.at[1]),
    ]
    for load in loads:
        load.start()
    for load in loads:
        load.wait()

    def gain_of(moment, part, rows):
        return gain[channel, moment, part, rows, :]

    phasor_rows(
        channel, freq, gain_of, uv, screen, lm, flux_held, direction_held, out, lambda moment, start: None
    )


def phasor_send(*inputs):
    gain = inputs[1]
    stations, sources = gain.shape[3], gain.shape[4]
    return pl.pallas_call(
        phasor_send_kernel,
        in_specs=[HBM] * 7,
        out_specs=HBM,
        out_shape=jax.ShapeDtypeStruct((2, stations + 16, 2 * sources), bf16),
        scratch_shapes=[
            pltpu.VMEM((2, stations + 16, 2 * sources), bf16),
            pltpu.SemaphoreType.DMA((4,)),
            pltpu.VMEM((2, 2, stations, sources), bf16),
            pltpu.SMEM(inputs[0].shape, f32),
        ]
        + [pltpu.VMEM(array.shape, f32) for array in inputs[2:5]]
        + [pltpu.VMEM((1, sources), f32), pltpu.VMEM((1, sources), jnp.int32)]
        + [pltpu.SemaphoreType.DMA((14,))],
        compiler_params=pltpu.CompilerParams(vmem_limit_bytes=60 * MIB),
        cost_estimate=pl.CostEstimate(
            flops=40 * 2 * stations * sources, bytes_accessed=3200000, transcendentals=0
        ),
        name="phasor_send",
    )(*inputs)


def phasor_own(*inputs):
    gain = inputs[1]
    stations, sources = gain.shape[3], gain.shape[4]
    return pl.pallas_call(
        phasor_own_kernel,
        in_specs=[SCALARS] + [WHOLE] * 4 + [ANY] * 2,
        out_specs=WHOLE,
        out_shape=jax.ShapeDtypeStruct((2, stations + 16, 2 * sources), bf16),
        scratch_shapes=[
            pltpu.VMEM((1, sources), f32),
            pltpu.VMEM((1, sources), jnp.int32),
            pltpu.SemaphoreType.DMA((2,)),
        ],
        compiler_params=pltpu.CompilerParams(vmem_limit_bytes=16 * MIB),
        cost_estimate=pl.CostEstimate(
            flops=40 * 2 * stations * sources, bytes_accessed=3200000, transcendentals=0
        ),
        name="phasor_own",
    )(*inputs)


def upper_mask():
    row = lax.broadcasted_iota(jnp.int32, (64, 64), 0)
    col = lax.broadcasted_iota(jnp.int32, (64, 64), 1)
    return row < col, row > col


def pack(re, im, odd, keep_re):
    re = jnp.where(odd, pltpu.roll(re, 320, 1), re)
    im = jnp.where(odd, pltpu.roll(im, 320, 1), im)
    row = lax.broadcasted_iota(jnp.int32, (64, 128), 0)
    col = lax.broadcasted_iota(jnp.int32, (64, 128), 1)
    near = col < 64
    far = jnp.where(keep_re, re[:, 256:384], im[:, 256:384])
    return jnp.concatenate(
        [
            jnp.where(near & (row >= col), im[:, 0:128], re[:, 0:128]),
            re[:, 128:256],
            jnp.where(near, far, im[:, 0:128]),
            im[:, 128:256],
        ],
        axis=1,
    )


def skewed(q):
    half = q.shape[1] // 2
    return jnp.concatenate([q[:, half:], -q[:, :half]], axis=1)


def mm(a, b):
    return lax.dot_general(a, b, NT, preferred_element_type=f32)


def fill_wide(wide, part, top, bottom):
    wide[part, 0:256, 0:512] = top
    wide[part, 256:512, 256:512] = bottom
    corner = jnp.transpose(top[:, 256:512])
    wide[part, 256:512, 512:768] = corner if part == 0 else -corner


def fill_gram(wide, left, right, scaling):
    for part, rows in ((0, left), (1, skewed(left))):
        value = mm(rows, right) * scaling
        wide[part, :, 0:512] = value
        wide[part, :, 512:768] = value[:, 0:256]


def block_of(wide, part, chip):
    start = pl.multiple_of((chip // 2) * 128, 128)
    return wide[part, pl.ds(pl.multiple_of(chip * 64, 64), 64), pl.ds(start, 384)]


def model_kernel(scaling, own, other_hbm, stay, out11, out21, out31, out10, out20, out30, wides, tops, bottoms, other, sems):
    _, y, z = position()
    copies = [
        pltpu.make_async_copy(other_hbm.at[moment], other.at[moment], sems.at[moment])
        for moment in range(2)
    ]
    for copy in copies:
        copy.start()
    for moment in range(2):
        wide, top, bottom = wides.at[moment], tops.at[moment], bottoms.at[moment]
        q = own[moment, 0:512, :]
        for part, rows in ((0, q), (1, skewed(q))):
            top[part] = mm(rows[0:256], q) * scaling
            bottom[part] = mm(rows[256:512], q[256:512]) * scaling
        copies[moment].wait()
        q = other[moment, 0:512, :]
        for part, rows in ((0, q), (1, skewed(q))):
            fill_wide(
                wide,
                part,
                top[part] + mm(rows[0:256], q) * scaling,
                bottom[part] + mm(rows[256:512], q[256:512]) * scaling,
            )
        for flip, outs in ((1, (out11, out21, out31)), (0, (out10, out20, out30))):
            for rel in range(4):
                zz = 1 - z if flip else z
                chip = zz * 4 + y_partner(rel, y)
                value = pack(
                    block_of(wide, 0, chip), block_of(wide, 1, chip), chip % 2 == 1, zz == 0
                )
                if rel == 0:
                    stay[flip, moment] = value
                else:
                    outs[rel - 1][moment] = value.astype(bf16)


def model_parts(scaling, own, other):
    return pl.pallas_call(
        functools.partial(model_kernel, scaling),
        in_specs=[WHOLE, HBM],
        out_specs=[WHOLE] * 10,
        scratch_shapes=[pltpu.VMEM(own.shape, bf16), pltpu.SemaphoreType.DMA((2,))],
        out_shape=[jax.ShapeDtypeStruct((2, 2, 64, 512), f32)]
        + [jax.ShapeDtypeStruct((2, 64, 512), bf16)] * 6
        + [
            jax.ShapeDtypeStruct((2, 2, 512, 768), f32),
            jax.ShapeDtypeStruct((2, 2, 256, 512), f32),
            jax.ShapeDtypeStruct((2, 2, 256, 256), f32),
        ],
        compiler_params=pltpu.CompilerParams(vmem_limit_bytes=20 * MIB),
        cost_estimate=pl.CostEstimate(
            flops=2 * 2 * 4 * 512 * 512 * 768, bytes_accessed=5000000, transcendentals=0
        ),
        name="model_parts",
    )(own, other)


def direction_kernel(moment, scaling, own, other, totals, tops, bottoms, out, mine, first_own, first_other):
    core, y, z = position()
    total = totals.at[moment]
    for part in range(2):
        fill_wide(mine, part, tops[moment, part], bottoms[moment, part])
    for source, first in ((own, first_own), (other, first_other)):
        q = source[moment, 0:512, :]
        in_first = source[moment, 512:513, :] < 0.5
        fill_gram(first, jnp.where(in_first, q, jnp.zeros_like(q)), q, scaling)
    for rel in range(4):
        for flip in range(2):
            zz = 1 - z if flip else z
            chip = zz * 4 + y_partner(rel, y)
            whole, own_all, own_first, other_first = (
                pack(block_of(wide, 1, chip), -block_of(wide, 0, chip), chip % 2 == 1, zz == 0)
                for wide in (total, mine, first_own, first_other)
            )
            out[core * 2, rel, flip] = own_first.astype(bf16)
            out[core * 2 + 1, rel, flip] = (own_all - own_first).astype(bf16)
            out[2 - core * 2, rel, flip] = other_first.astype(bf16)
            out[3 - core * 2, rel, flip] = ((whole - own_all) - other_first).astype(bf16)


def direction_parts(moment, scaling, *arrays):
    return pl.pallas_call(
        functools.partial(direction_kernel, moment, scaling),
        in_specs=[WHOLE] * 5,
        out_specs=WHOLE,
        scratch_shapes=[pltpu.VMEM((2, 512, 768), f32)] * 3,
        out_shape=jax.ShapeDtypeStruct((4, 4, 2, 64, 512), bf16),
        compiler_params=pltpu.CompilerParams(vmem_limit_bytes=18 * MIB),
        cost_estimate=pl.CostEstimate(
            flops=2 * 4 * 512 * 512 * 768, bytes_accessed=5000000, transcendentals=0
        ),
        name="direction_parts%d" % moment,
    )(*arrays)


def send_kernel(own, one, two, three, send):
    send[...] = (
        own[1] + one[...].astype(f32) + two[...].astype(f32) + three[...].astype(f32)
    ).astype(bf16)


def send_parts(own, *parts):
    return pl.pallas_call(
        send_kernel,
        in_specs=[WHOLE] * 4,
        out_specs=WHOLE,
        out_shape=jax.ShapeDtypeStruct(own.shape[1:], bf16),
        compiler_params=pltpu.CompilerParams(vmem_limit_bytes=4 * MIB),
        cost_estimate=pl.CostEstimate(flops=300000, bytes_accessed=1500000, transcendentals=0),
        name="send_parts",
    )(own, *parts)


def residual_kernel(own, one, two, three, last, obs, kept, _, resid, half):
    total = own[0] + one[...].astype(f32) + two[...].astype(f32) + three[...].astype(f32)
    value = kept[...] * (obs[...] - (total + last[...].astype(f32)))
    resid[...] = value
    half[...] = value.astype(bf16)


def residual_parts(own, *parts):
    return pl.pallas_call(
        residual_kernel,
        in_specs=[WHOLE] * 7 + [ANY],
        out_specs=[WHOLE] * 2,
        out_shape=[
            jax.ShapeDtypeStruct(own.shape[1:], f32),
            jax.ShapeDtypeStruct(own.shape[1:], bf16),
        ],
        compiler_params=pltpu.CompilerParams(vmem_limit_bytes=4 * MIB),
        cost_estimate=pl.CostEstimate(flops=500000, bytes_accessed=2500000, transcendentals=0),
        name="residual_parts",
    )(own, *parts)


def observed_send_kernel(observed, flags, _, out, sem):
    core, _, _ = position()
    copy = pltpu.make_async_copy(observed.at[:, 1 - core], out.at[:, :, 0:2, :], sem)
    copy.start()
    for moment in range(2):
        keep = flags[:, moment, :].astype(f32)
        out[:, moment, 2, :] = keep
        out[:, moment, 3, :] = keep
    copy.wait()


def observed_send(observed, flags, after):
    rows, _, _, _, stations = observed.shape
    return pl.pallas_call(
        observed_send_kernel,
        in_specs=[HBM, WHOLE, ANY],
        out_specs=WHOLE,
        out_shape=jax.ShapeDtypeStruct((rows, 2, 4, stations), f32),
        scratch_shapes=[pltpu.SemaphoreType.DMA],
        cost_estimate=pl.CostEstimate(flops=100000, bytes_accessed=700000, transcendentals=0),
        compiler_params=pltpu.CompilerParams(vmem_limit_bytes=4 * MIB),
        name="observed_send",
    )(observed, flags, after)


def observed_kernel(observed, flags, other, obs_out, keep_out, own, wide, sem):
    core, y, z = position()
    copy = pltpu.make_async_copy(observed.at[:, core], own, sem)
    copy.start()
    copy.wait()
    chip = z * 4 + y
    start = pl.ds(pl.multiple_of((chip // 2) * 128, 128), 384)
    odd = chip % 2 == 1
    row = lax.broadcasted_iota(jnp.int32, (64, 512), 0)
    col = lax.broadcasted_iota(jnp.int32, (64, 512), 1)
    for moment in range(2):
        for rows, mine in ((core, True), (1 - core, False)):
            there = pl.ds(pl.multiple_of(rows * 32, 32), 32)
            for part in range(3):
                if not mine:
                    value = other[:, moment, part, :]
                elif part == 2:
                    value = flags[:, moment, :].astype(f32)
                else:
                    value = own[:, moment, part, :]
                wide[part, there, 0:512] = value
                wide[part, there, 512:768] = value[:, 0:256]
        obs_out[moment] = pack(wide[0, :, start], wide[1, :, start], odd, z == 0)
        keep = pack(wide[2, :, start], wide[2, :, start], odd, z == 0)
        keep_out[moment] = jnp.where(row == col, 0.0, keep)


def observed_parts(observed, flags, other):
    rows, _, _, _, stations = observed.shape
    return pl.pallas_call(
        observed_kernel,
        in_specs=[HBM] + [WHOLE] * 2,
        out_specs=[WHOLE] * 2,
        out_shape=[jax.ShapeDtypeStruct((2, 64, 512), f32)] * 2,
        scratch_shapes=[
            pltpu.VMEM((rows, 2, 2, stations), f32),
            pltpu.VMEM((3, 64, 768), f32),
            pltpu.SemaphoreType.DMA,
        ],
        cost_estimate=pl.CostEstimate(flops=1000000, bytes_accessed=1500000, transcendentals=0),
        compiler_params=pltpu.CompilerParams(vmem_limit_bytes=6 * MIB),
        name="observed_parts",
    )(observed, flags, other)


def gradient_kernel(flip, freq, *refs):
    sources = refs[0:4]
    parts0, parts1 = refs[4:6]
    out, rows_sum, cols_sum = refs[-3:]
    core, y, z = position()
    zz = 1 - z if flip else z
    for rel, source in enumerate(sources):
        chip = y_partner(rel, y)
        for start in range(0, 64, 32):
            rows = slice(start, start + 32)
            resid0 = source[0, rows, :]
            resid1 = source[1, rows, :]
            for which in range(4):
                product = (resid0 * parts0[which, rel, flip, rows, :]).astype(f32)
                product += (resid1 * parts1[which, rel, flip, rows, :]).astype(f32)
                rows_sum[which, pl.ds(pl.multiple_of(chip * 64 + start, 32), 32), :] = (
                    product[:, 0:128] + product[:, 128:256]
                ) + (product[:, 256:384] + product[:, 384:512])
                column = (product[0:8] + product[8:16]) + (product[16:24] + product[24:32])
                if start == 0:
                    cols_sum[which, chip] = column
                else:
                    cols_sum[which, chip] += column
    near = lax.broadcasted_iota(jnp.int32, (8, 256), 1) < 64
    factor = 2.0 / freq[core]
    pieces = []
    for which in range(4):
        placed = []
        for odd in range(2):
            total = None
            for chip in range(odd, 4, 2):
                low = cols_sum[which, chip, :, 0:256]
                high = cols_sum[which, chip, :, 256:512]
                folded = [low + jnp.where(near, 0.0, high), jnp.where(near, high, 0.0)]
                quarters = [part[:, at : at + 128] for part in folded for at in (0, 128)]
                turn = (4 - chip // 2) % 4
                quarters = quarters[turn:] + quarters[:turn]
                total = quarters if total is None else [a + b for a, b in zip(total, quarters)]
            placed.append(jnp.concatenate(total, axis=1))
        columns = jnp.sum(placed[0] + pltpu.roll(placed[1], 64, 1), axis=0, keepdims=True)
        along_rows = jnp.sum(jnp.transpose(rows_sum[which]), axis=0, keepdims=True)
        first = (along_rows - columns[:, 0:256]) * factor
        second = -columns[:, 256:512] * factor
        low = jnp.where(zz == 0, first, second)
        high = jnp.where(zz == 0, second, first)
        pieces.extend([low[:, 0:128], low[:, 128:256], high[:, 0:128], high[:, 128:256]])
    value = jnp.concatenate(pieces, axis=0)
    if flip == 0:
        out[...] = value
    else:
        value = (value + refs[6][...]).astype(bf16)

        def copy(index, carry):
            out[index] = value
            return carry

        lax.fori_loop(0, out.shape[0], copy, 0, unroll=8)


def gradient_parts(flip, devices, freq, *arrays):
    out = jax.ShapeDtypeStruct((16, 128), f32)
    if flip:
        out = jax.ShapeDtypeStruct((devices, 16, 128), bf16)
    return pl.pallas_call(
        functools.partial(gradient_kernel, flip),
        in_specs=[SCALARS] + [WHOLE] * len(arrays),
        out_specs=WHOLE,
        scratch_shapes=[pltpu.VMEM((4, 256, 128), f32), pltpu.VMEM((4, 4, 8, 512), f32)],
        out_shape=out,
        compiler_params=pltpu.CompilerParams(vmem_limit_bytes=10 * MIB),
        cost_estimate=pl.CostEstimate(flops=5000000, bytes_accessed=3000000, transcendentals=0),
        name="gradient_parts%d" % flip,
    )(freq, *arrays)


def rows_kernel(resid, *refs):
    resids = refs[0:8]
    _, own_out, other_out, rolled = refs[8:]
    core, y, z = position()
    chip = z * 4 + y
    upper, lower = upper_mask()
    even = y % 2 == 0
    flip5 = jnp.where(y < 3, 1, 0)
    flip6 = jnp.where(y < 2, 1, 0)
    flip7 = jnp.where(y < 1, 1, 0)
    for moment in range(2):
        own = resid[moment]
        near = own[:, 0:64]
        near_t = jnp.transpose(near)
        zero = jnp.zeros_like(near)
        near_re = jnp.where(upper, near, jnp.where(lower, near_t, zero))
        near_im = jnp.where(lower, near, jnp.where(upper, -near_t, zero))
        far = own[:, 256:320]
        far_t = jnp.transpose(resids[4][moment][:, 256:320].astype(f32))
        far_re = jnp.where(z == 0, far, far_t)
        far_im = jnp.where(z == 0, -far_t, far)
        one5, two5, block6, one7, two7 = (
            jnp.where(flip == 1, resids[4 + rel][moment], resids[rel][moment]).astype(f32)
            for rel, flip in ((1, flip5), (2, flip5), (3, flip6), (1, flip7), (2, flip7))
        )
        block5 = jnp.where(even, one5, two5)
        block7 = jnp.where(even, two7, one7)
        re = [near_re, own[:, 64:256], far_re]
        im = [near_im, own[:, 320:512], far_im]
        for block, offset in ((block5, 3), (block6, 2), (block7, 1)):
            re.append(jnp.transpose(block[:, 64 * offset : 64 * offset + 64]))
            im.append(-jnp.transpose(block[:, 256 + 64 * offset : 320 + 64 * offset]))
        for part, pieces in enumerate((re, im)):
            index = moment * 2 + part
            rolled[index] = pltpu.roll(jnp.concatenate(pieces, axis=1), chip * 64, 1)
            own_out[index] = rolled[index, pl.ds(pl.multiple_of(core * 32, 32), 32), :]
            other_out[index] = rolled[index, pl.ds(pl.multiple_of((1 - core) * 32, 32), 32), :]


def whole_rows(resid, resids, after):
    return pl.pallas_call(
        rows_kernel,
        in_specs=[WHOLE] * 9 + [ANY],
        out_specs=[WHOLE] * 2,
        out_shape=[jax.ShapeDtypeStruct((4, 32, 512), f32)] * 2,
        scratch_shapes=[pltpu.VMEM((4, 64, 512), f32)],
        cost_estimate=pl.CostEstimate(flops=0, bytes_accessed=0, transcendentals=0),
        compiler_params=pltpu.CompilerParams(vmem_limit_bytes=6 * MIB),
        name="whole_rows",
    )(resid, *resids, after)


def assemble_kernel(own, other, out):
    core = position()[0]
    for channel, source in ((core, own), (1 - core, other)):
        for moment in range(2):
            for part in range(2):
                out[:, channel, moment, part, :] = source[moment * 2 + part]


def assemble(own, other, like):
    return pl.pallas_call(
        assemble_kernel,
        in_specs=[WHOLE] * 2,
        out_specs=WHOLE,
        out_shape=jax.ShapeDtypeStruct(like.shape, f32),
        compiler_params=pltpu.CompilerParams(vmem_limit_bytes=4 * MIB),
        cost_estimate=pl.CostEstimate(flops=0, bytes_accessed=0, transcendentals=0),
        name="assemble",
    )(own, other)


def halves(value):
    high = value.astype(bf16)
    return high, (value - high.astype(f32)).astype(bf16)


def update_kernel(grads, kernel, screen, out, total, smooth):
    core, y, z = position()
    per_chip = grads.shape[0] // 8
    for chip in range(8):
        total[chip * 16 : chip * 16 + 16, :] = jnp.sum(
            grads[chip * per_chip : (chip + 1) * per_chip].astype(f32), axis=0
        )
    gradient = jnp.concatenate(
        [total[pl.ds(piece, 32, stride=4), :] for piece in range(4)], axis=1
    )
    grad_high, grad_low = halves(gradient)
    kern_high, kern_low = halves(kernel[...])
    both = jnp.dot(
        jnp.concatenate([grad_high, grad_low], axis=0), kern_high, preferred_element_type=f32
    )
    value = both[0:32] + (
        both[32:64] + jnp.dot(grad_high, kern_low, preferred_element_type=f32)
    )
    mean_sq = jnp.sum(value * value) / value.size
    smooth[...] = value * (step_size * lax.rsqrt(mean_sq + epsilon))
    row = (z * 4 + y) * 4 + core * 2
    for step in range(2):
        out[step : step + 1, :] = screen[step : step + 1, :] - smooth[pl.ds(row + step, 1), :]


def updated_rows(grads, kernel, screen):
    return pl.pallas_call(
        update_kernel,
        in_specs=[WHOLE] * 3,
        out_specs=WHOLE,
        out_shape=jax.ShapeDtypeStruct(screen.shape, f32),
        scratch_shapes=[pltpu.VMEM((128, 128), f32), pltpu.VMEM((32, 512), f32)],
        compiler_params=pltpu.CompilerParams(vmem_limit_bytes=8 * MIB),
        cost_estimate=pl.CostEstimate(flops=200000000, bytes_accessed=1500000, transcendentals=0),
        name="updated_rows",
    )(grads, kernel, screen)


def body(
    observed,
    flags,
    screen,
    screen_kernel,
    station_uv,
    source_lm,
    source_flux,
    station_gain,
    source_direction,
    freq_ratio,
):
    devices = lax.axis_size("dir") * lax.axis_size("freq")
    stations = screen.shape[1]
    scaling = 1.0 / math.sqrt(source_flux.shape[0] * lax.axis_size("dir"))
    core = position()[0]
    swap = functools.partial(lax.ppermute, axis_name="dir", perm=dir_perm(0, flip_core=True))

    inputs = (freq_ratio, station_gain, station_uv, screen, source_lm, source_flux, source_direction)
    other = swap(phasor_send(*inputs))
    own = phasor_own(*inputs)

    def across(rel, array):
        return lax.ppermute(array, "dir", dir_perm(rel))

    def across_z(array):
        return lax.ppermute(array, "dir", dir_perm(0, flip_z=True))

    parts = model_parts(scaling, own, other)
    far = [across(rel, parts[rel]) for rel in (3, 2, 1)]
    near = [across(rel, parts[rel + 3]) for rel in (3, 2, 1)]
    other_observed = swap(observed_send(observed, flags, parts[6]))
    obs, kept = observed_parts(observed, flags, other_observed)
    directions0 = direction_parts(0, scaling, own, other, *parts[7:])
    last = across_z(send_parts(parts[0], *far))
    resid, half = residual_parts(parts[0], *near, last, obs, kept, directions0)
    half_z = across_z(half)
    directions1 = direction_parts(1, scaling, own, other, *parts[7:])
    one, two = across(1, half), across(2, half)
    resids = [half, one, two, across(2, one)]
    resids += [half_z, across(1, half_z), across(2, half_z), across(3, half_z)]

    grads = gradient_parts(0, devices, freq_ratio, *resids[:4], directions0, directions1)
    grads = gradient_parts(1, devices, freq_ratio, *resids[4:], directions0, directions1, grads)
    own_rows, sent_rows = whole_rows(resid, resids, grads)
    other_rows = swap(sent_rows)
    grads = lax.all_to_all(grads, ("dir", "freq"), 0, 0, tiled=True)
    updated = updated_rows(grads, screen_kernel, screen)

    return assemble(own_rows, other_rows, observed), updated


def solution(mesh):
    placed = (
        P("dir", "freq", None, None, None),
        P("dir", None, None),
        P("dir", None),
        P(),
        P(),
        P(None, "dir"),
        P("dir"),
        P("freq", None, None, None, "dir"),
        P("dir"),
        P("freq"),
    )
    return jax.shard_map(
        body,
        mesh=mesh,
        in_specs=placed,
        out_specs=(P("dir", "freq", None, None, None), P("dir", None)),
        check_vma=False,
    )
```

```python
import functools
import math

import jax
import jax.numpy as jnp
from jax import lax
from jax.experimental import pallas as pl
from jax.experimental.pallas import tpu as pltpu
from jax.sharding import PartitionSpec as P

step_size = 0.3
epsilon = 1e-06
highest = lax.Precision.HIGHEST
bf16 = jnp.bfloat16
f32 = jnp.float32

SIN_COEF = (4.44288292, -7.3082457, 3.60635441, -0.84611289, 0.10982699)
COS_COEF = (1.4142135, -6.97885099, 5.73946117, -1.88356299, 0.31069819)
ROUNDER = 12582912.0
CHUNK = 32
MIB = 1024 * 1024
NT = (((1,), (1,)), ((), ()))


def y_partner(rel, y):
    if rel == 0:
        return y
    if rel == 1:
        return y + 1 - 2 * (y % 2)
    if rel == 2:
        return 3 - y
    return (y + 2) % 4


def dir_perm(rel, flip_z=False, flip_core=False):
    pairs = []
    for index in range(16):
        z, y, core = index // 8, (index // 2) % 4, index % 2
        z = 1 - z if flip_z else z
        core = 1 - core if flip_core else core
        pairs.append((index, z * 8 + y_partner(rel, y) * 2 + core))
    return pairs


ANY = pl.BlockSpec(memory_space=pl.ANY)
HBM = pl.BlockSpec(memory_space=pltpu.HBM)
WHOLE = pl.BlockSpec(memory_space=pltpu.VMEM)
SCALARS = pl.BlockSpec(memory_space=pltpu.SMEM)


def position():
    index = lax.axis_index("dir")
    return index % 2, (index // 2) % 4, index // 8


def phasor_rows(channel, freq, gain_of, uv, screen, lm, flux, direction, out, ready):
    stations, sources = screen.shape[1], lm.shape[1]
    ratio = freq[channel]
    along = lm[0:1, :] * ratio
    across = lm[1:2, :] * ratio
    amp = jnp.sqrt(flux[...])
    second = direction[...] > 0
    per_turn = 1.0 / (2.0 * math.pi * ratio)
    by_station = jnp.concatenate(
        [uv[0], uv[1], screen[...] * per_turn, jnp.zeros((2, stations), f32)], axis=0
    )
    cols = jnp.transpose(by_station)
    mask = jnp.broadcast_to(jnp.where(second, 1.0, 0.0), (16, sources)).astype(bf16)
    for moment in range(2):
        for start in range(0, stations, CHUNK):
            ready(moment, start)
            rows = slice(start, start + CHUNK)
            col = cols[rows]
            u = col[:, 2 * moment : 2 * moment + 1]
            v = col[:, 2 * moment + 1 : 2 * moment + 2]
            turns = u * along + v * across + jnp.where(second, col[:, 5:6], col[:, 4:5])
            turns = turns - ((turns + ROUNDER) - ROUNDER)
            z = turns * turns
            sin_half = SIN_COEF[4]
            cos_half = COS_COEF[4]
            for power in (3, 2, 1, 0):
                sin_half = sin_half * z + SIN_COEF[power]
                cos_half = cos_half * z + COS_COEF[power]
            sin_half = sin_half * turns
            sin_amp = sin_half * amp
            sine = sin_amp * cos_half
            cosine = amp - sin_amp * sin_half
            gain_re = gain_of(moment, 0, rows).astype(f32)
            gain_im = gain_of(moment, 1, rows).astype(f32)
            out[moment, rows, 0:sources] = (gain_re * cosine - gain_im * sine).astype(bf16)
            out[moment, rows, sources : 2 * sources] = (
                gain_re * sine + gain_im * cosine
            ).astype(bf16)
        out[moment, stations : stations + 16, 0:sources] = mask
        out[moment, stations : stations + 16, sources : 2 * sources] = mask


def phasor_send_kernel(
    freq, gain, uv, screen, lm, flux, direction, out_hbm, *rest
):
    out, out_sems, held, freq_held, uv_held, screen_held, lm_held, flux_held, direction_held, sems = rest
    core, _, _ = position()
    channel = 1 - core
    quarter = gain.shape[3] // 4
    loads = [
        pltpu.make_async_copy(source, target, sems.at[8 + index])
        for index, (source, target) in enumerate(
            (
                (freq, freq_held),
                (uv, uv_held),
                (screen, screen_held),
                (lm, lm_held),
                (flux, flux_held.at[0]),
                (direction, direction_held.at[0]),
            )
        )
    ]
    copies = []
    for moment in range(2):
        for part in range(4):
            rows = pl.ds(part * quarter, quarter)
            copies.append(
                pltpu.make_async_copy(
                    gain.at[channel, moment, :, rows, :],
                    held.at[moment, :, rows, :],
                    sems.at[moment * 4 + part],
                )
            )
    for copy in loads + copies:
        copy.start()
    for load in loads:
        load.wait()

    half = gain.shape[3] // 2
    writes = []

    def write(moment, start, size):
        rows = pl.ds(start, size)
        writes.append(
            pltpu.make_async_copy(
                out.at[moment, rows, :], out_hbm.at[moment, rows, :], out_sems.at[len(writes)]
            )
        )
        writes[-1].start()

    def ready(moment, start):
        if start % quarter == 0:
            copies[moment * 4 + start // quarter].wait()
        if start == half:
            write(moment, 0, half)
        if start == 0 and moment == 1:
            write(0, half, half + 16)

    def gain_of(moment, part, rows):
        return held[moment, part, rows, :]

    phasor_rows(
        channel, freq_held, gain_of, uv_held, screen_held, lm_held, flux_held, direction_held, out, ready
    )
    write(1, half, half + 16)
    for copy in writes:
        copy.wait()


def phasor_own_kernel(freq, gain, uv, screen, lm, flux, direction, out, flux_held, direction_held, sems):
    channel = position()[0]
    loads = [
        pltpu.make_async_copy(flux, flux_held.at[0], sems.at[0]),
        pltpu.make_async_copy(direction, direction_held.at[0], sems.at[1]),
    ]
    for load in loads:
        load.start()
    for load in loads:
        load.wait()

    def gain_of(moment, part, rows):
        return gain[channel, moment, part, rows, :]

    phasor_rows(
        channel, freq, gain_of, uv, screen, lm, flux_held, direction_held, out, lambda moment, start: None
    )


def phasor_send(*inputs):
    gain = inputs[1]
    stations, sources = gain.shape[3], gain.shape[4]
    return pl.pallas_call(
        phasor_send_kernel,
        in_specs=[HBM] * 7,
        out_specs=HBM,
        out_shape=jax.ShapeDtypeStruct((2, stations + 16, 2 * sources), bf16),
        scratch_shapes=[
            pltpu.VMEM((2, stations + 16, 2 * sources), bf16),
            pltpu.SemaphoreType.DMA((4,)),
            pltpu.VMEM((2, 2, stations, sources), bf16),
            pltpu.SMEM(inputs[0].shape, f32),
        ]
        + [pltpu.VMEM(array.shape, f32) for array in inputs[2:5]]
        + [pltpu.VMEM((1, sources), f32), pltpu.VMEM((1, sources), jnp.int32)]
        + [pltpu.SemaphoreType.DMA((14,))],
        compiler_params=pltpu.CompilerParams(vmem_limit_bytes=60 * MIB),
        cost_estimate=pl.CostEstimate(
            flops=40 * 2 * stations * sources, bytes_accessed=3200000, transcendentals=0
        ),
        name="phasor_send",
    )(*inputs)


def phasor_own(*inputs):
    gain = inputs[1]
    stations, sources = gain.shape[3], gain.shape[4]
    return pl.pallas_call(
        phasor_own_kernel,
        in_specs=[SCALARS] + [WHOLE] * 4 + [ANY] * 2,
        out_specs=WHOLE,
        out_shape=jax.ShapeDtypeStruct((2, stations + 16, 2 * sources), bf16),
        scratch_shapes=[
            pltpu.VMEM((1, sources), f32),
            pltpu.VMEM((1, sources), jnp.int32),
            pltpu.SemaphoreType.DMA((2,)),
        ],
        compiler_params=pltpu.CompilerParams(vmem_limit_bytes=16 * MIB),
        cost_estimate=pl.CostEstimate(
            flops=40 * 2 * stations * sources, bytes_accessed=3200000, transcendentals=0
        ),
        name="phasor_own",
    )(*inputs)


def upper_mask():
    row = lax.broadcasted_iota(jnp.int32, (64, 64), 0)
    col = lax.broadcasted_iota(jnp.int32, (64, 64), 1)
    return row < col, row > col


def pack(re, im, odd, keep_re):
    re = jnp.where(odd, pltpu.roll(re, 320, 1), re)
    im = jnp.where(odd, pltpu.roll(im, 320, 1), im)
    row = lax.broadcasted_iota(jnp.int32, (64, 128), 0)
    col = lax.broadcasted_iota(jnp.int32, (64, 128), 1)
    near = col < 64
    far = jnp.where(keep_re, re[:, 256:384], im[:, 256:384])
    return jnp.concatenate(
        [
            jnp.where(near & (row >= col), im[:, 0:128], re[:, 0:128]),
            re[:, 128:256],
            jnp.where(near, far, im[:, 0:128]),
            im[:, 128:256],
        ],
        axis=1,
    )


def skewed(q):
    half = q.shape[1] // 2
    return jnp.concatenate([q[:, half:], -q[:, :half]], axis=1)


def mm(a, b):
    return lax.dot_general(a, b, NT, preferred_element_type=f32)


def fill_wide(wide, part, top, bottom):
    wide[part, 0:256, 0:512] = top
    wide[part, 256:512, 256:512] = bottom
    corner = jnp.transpose(top[:, 256:512])
    wide[part, 256:512, 512:768] = corner if part == 0 else -corner


def fill_gram(wide, left, right, scaling):
    for part, rows in ((0, left), (1, skewed(left))):
        value = mm(rows, right) * scaling
        wide[part, :, 0:512] = value
        wide[part, :, 512:768] = value[:, 0:256]


def block_of(wide, part, chip):
    start = pl.multiple_of((chip // 2) * 128, 128)
    return wide[part, pl.ds(pl.multiple_of(chip * 64, 64), 64), pl.ds(start, 384)]


def model_kernel(scaling, own, other_hbm, stay, out11, out21, out31, out10, out20, out30, wides, tops, bottoms, other, sems):
    _, y, z = position()
    copies = [
        pltpu.make_async_copy(other_hbm.at[moment], other.at[moment], sems.at[moment])
        for moment in range(2)
    ]
    for copy in copies:
        copy.start()
    for moment in range(2):
        wide, top, bottom = wides.at[moment], tops.at[moment], bottoms.at[moment]
        q = own[moment, 0:512, :]
        for part, rows in ((0, q), (1, skewed(q))):
            top[part] = mm(rows[0:256], q) * scaling
            bottom[part] = mm(rows[256:512], q[256:512]) * scaling
        copies[moment].wait()
        q = other[moment, 0:512, :]
        for part, rows in ((0, q), (1, skewed(q))):
            fill_wide(
                wide,
                part,
                top[part] + mm(rows[0:256], q) * scaling,
                bottom[part] + mm(rows[256:512], q[256:512]) * scaling,
            )
        for flip, outs in ((1, (out11, out21, out31)), (0, (out10, out20, out30))):
            for rel in range(4):
                zz = 1 - z if flip else z
                chip = zz * 4 + y_partner(rel, y)
                value = pack(
                    block_of(wide, 0, chip), block_of(wide, 1, chip), chip % 2 == 1, zz == 0
                )
                if rel == 0:
                    stay[flip, moment] = value
                else:
                    outs[rel - 1][moment] = value.astype(bf16)


def model_parts(scaling, own, other):
    return pl.pallas_call(
        functools.partial(model_kernel, scaling),
        in_specs=[WHOLE, HBM],
        out_specs=[WHOLE] * 10,
        scratch_shapes=[pltpu.VMEM(own.shape, bf16), pltpu.SemaphoreType.DMA((2,))],
        out_shape=[jax.ShapeDtypeStruct((2, 2, 64, 512), f32)]
        + [jax.ShapeDtypeStruct((2, 64, 512), bf16)] * 6
        + [
            jax.ShapeDtypeStruct((2, 2, 512, 768), f32),
            jax.ShapeDtypeStruct((2, 2, 256, 512), f32),
            jax.ShapeDtypeStruct((2, 2, 256, 256), f32),
        ],
        compiler_params=pltpu.CompilerParams(vmem_limit_bytes=20 * MIB),
        cost_estimate=pl.CostEstimate(
            flops=2 * 2 * 4 * 512 * 512 * 768, bytes_accessed=5000000, transcendentals=0
        ),
        name="model_parts",
    )(own, other)


def direction_kernel(moment, scaling, own, other, totals, tops, bottoms, out, mine, first_own, first_other):
    core, y, z = position()
    total = totals.at[moment]
    for part in range(2):
        fill_wide(mine, part, tops[moment, part], bottoms[moment, part])
    for source, first in ((own, first_own), (other, first_other)):
        q = source[moment, 0:512, :]
        in_first = source[moment, 512:513, :] < 0.5
        fill_gram(first, jnp.where(in_first, q, jnp.zeros_like(q)), q, scaling)
    for rel in range(4):
        for flip in range(2):
            zz = 1 - z if flip else z
            chip = zz * 4 + y_partner(rel, y)
            whole, own_all, own_first, other_first = (
                pack(block_of(wide, 1, chip), -block_of(wide, 0, chip), chip % 2 == 1, zz == 0)
                for wide in (total, mine, first_own, first_other)
            )
            out[core * 2, rel, flip] = own_first.astype(bf16)
            out[core * 2 + 1, rel, flip] = (own_all - own_first).astype(bf16)
            out[2 - core * 2, rel, flip] = other_first.astype(bf16)
            out[3 - core * 2, rel, flip] = ((whole - own_all) - other_first).astype(bf16)


def direction_parts(moment, scaling, *arrays):
    return pl.pallas_call(
        functools.partial(direction_kernel, moment, scaling),
        in_specs=[WHOLE] * 5,
        out_specs=WHOLE,
        scratch_shapes=[pltpu.VMEM((2, 512, 768), f32)] * 3,
        out_shape=jax.ShapeDtypeStruct((4, 4, 2, 64, 512), bf16),
        compiler_params=pltpu.CompilerParams(vmem_limit_bytes=18 * MIB),
        cost_estimate=pl.CostEstimate(
            flops=2 * 4 * 512 * 512 * 768, bytes_accessed=5000000, transcendentals=0
        ),
        name="direction_parts%d" % moment,
    )(*arrays)


def send_kernel(own, one, two, three, send):
    send[...] = (
        own[1] + one[...].astype(f32) + two[...].astype(f32) + three[...].astype(f32)
    ).astype(bf16)


def send_parts(own, *parts):
    return pl.pallas_call(
        send_kernel,
        in_specs=[WHOLE] * 4,
        out_specs=WHOLE,
        out_shape=jax.ShapeDtypeStruct(own.shape[1:], bf16),
        compiler_params=pltpu.CompilerParams(vmem_limit_bytes=4 * MIB),
        cost_estimate=pl.CostEstimate(flops=300000, bytes_accessed=1500000, transcendentals=0),
        name="send_parts",
    )(own, *parts)


def residual_kernel(own, one, two, three, last, obs, kept, _, resid, half):
    total = own[0] + one[...].astype(f32) + two[...].astype(f32) + three[...].astype(f32)
    value = kept[...] * (obs[...] - (total + last[...].astype(f32)))
    resid[...] = value
    half[...] = value.astype(bf16)


def residual_parts(own, *parts):
    return pl.pallas_call(
        residual_kernel,
        in_specs=[WHOLE] * 7 + [ANY],
        out_specs=[WHOLE] * 2,
        out_shape=[
            jax.ShapeDtypeStruct(own.shape[1:], f32),
            jax.ShapeDtypeStruct(own.shape[1:], bf16),
        ],
        compiler_params=pltpu.CompilerParams(vmem_limit_bytes=4 * MIB),
        cost_estimate=pl.CostEstimate(flops=500000, bytes_accessed=2500000, transcendentals=0),
        name="residual_parts",
    )(own, *parts)


def observed_send_kernel(observed, flags, _, out, sem):
    core, _, _ = position()
    copy = pltpu.make_async_copy(observed.at[:, 1 - core], out.at[:, :, 0:2, :], sem)
    copy.start()
    for moment in range(2):
        keep = flags[:, moment, :].astype(f32)
        out[:, moment, 2, :] = keep
        out[:, moment, 3, :] = keep
    copy.wait()


def observed_send(observed, flags, after):
    rows, _, _, _, stations = observed.shape
    return pl.pallas_call(
        observed_send_kernel,
        in_specs=[HBM, WHOLE, ANY],
        out_specs=WHOLE,
        out_shape=jax.ShapeDtypeStruct((rows, 2, 4, stations), f32),
        scratch_shapes=[pltpu.SemaphoreType.DMA],
        cost_estimate=pl.CostEstimate(flops=100000, bytes_accessed=700000, transcendentals=0),
        compiler_params=pltpu.CompilerParams(vmem_limit_bytes=4 * MIB),
        name="observed_send",
    )(observed, flags, after)


def observed_kernel(observed, flags, other, obs_out, keep_out, own, wide, sem):
    core, y, z = position()
    copy = pltpu.make_async_copy(observed.at[:, core], own, sem)
    copy.start()
    copy.wait()
    chip = z * 4 + y
    start = pl.ds(pl.multiple_of((chip // 2) * 128, 128), 384)
    odd = chip % 2 == 1
    row = lax.broadcasted_iota(jnp.int32, (64, 512), 0)
    col = lax.broadcasted_iota(jnp.int32, (64, 512), 1)
    for moment in range(2):
        for rows, mine in ((core, True), (1 - core, False)):
            there = pl.ds(pl.multiple_of(rows * 32, 32), 32)
            for part in range(3):
                if not mine:
                    value = other[:, moment, part, :]
                elif part == 2:
                    value = flags[:, moment, :].astype(f32)
                else:
                    value = own[:, moment, part, :]
                wide[part, there, 0:512] = value
                wide[part, there, 512:768] = value[:, 0:256]
        obs_out[moment] = pack(wide[0, :, start], wide[1, :, start], odd, z == 0)
        keep = pack(wide[2, :, start], wide[2, :, start], odd, z == 0)
        keep_out[moment] = jnp.where(row == col, 0.0, keep)


def observed_parts(observed, flags, other):
    rows, _, _, _, stations = observed.shape
    return pl.pallas_call(
        observed_kernel,
        in_specs=[HBM] + [WHOLE] * 2,
        out_specs=[WHOLE] * 2,
        out_shape=[jax.ShapeDtypeStruct((2, 64, 512), f32)] * 2,
        scratch_shapes=[
            pltpu.VMEM((rows, 2, 2, stations), f32),
            pltpu.VMEM((3, 64, 768), f32),
            pltpu.SemaphoreType.DMA,
        ],
        cost_estimate=pl.CostEstimate(flops=1000000, bytes_accessed=1500000, transcendentals=0),
        compiler_params=pltpu.CompilerParams(vmem_limit_bytes=6 * MIB),
        name="observed_parts",
    )(observed, flags, other)


def gradient_kernel(flip, freq, *refs):
    sources = refs[0:4]
    parts0, parts1 = refs[4:6]
    out, rows_sum, cols_sum = refs[-3:]
    core, y, z = position()
    zz = 1 - z if flip else z
    for rel, source in enumerate(sources):
        chip = y_partner(rel, y)
        for start in range(0, 64, 32):
            rows = slice(start, start + 32)
            resid0 = source[0, rows, :]
            resid1 = source[1, rows, :]
            for which in range(4):
                product = (resid0 * parts0[which, rel, flip, rows, :]).astype(f32)
                product += (resid1 * parts1[which, rel, flip, rows, :]).astype(f32)
                rows_sum[which, pl.ds(pl.multiple_of(chip * 64 + start, 32), 32), :] = (
                    product[:, 0:128] + product[:, 128:256]
                ) + (product[:, 256:384] + product[:, 384:512])
                column = (product[0:8] + product[8:16]) + (product[16:24] + product[24:32])
                if start == 0:
                    cols_sum[which, chip] = column
                else:
                    cols_sum[which, chip] += column
    near = lax.broadcasted_iota(jnp.int32, (8, 256), 1) < 64
    factor = 2.0 / freq[core]
    pieces = []
    for which in range(4):
        placed = []
        for odd in range(2):
            total = None
            for chip in range(odd, 4, 2):
                low = cols_sum[which, chip, :, 0:256]
                high = cols_sum[which, chip, :, 256:512]
                folded = [low + jnp.where(near, 0.0, high), jnp.where(near, high, 0.0)]
                quarters = [part[:, at : at + 128] for part in folded for at in (0, 128)]
                turn = (4 - chip // 2) % 4
                quarters = quarters[turn:] + quarters[:turn]
                total = quarters if total is None else [a + b for a, b in zip(total, quarters)]
            placed.append(jnp.concatenate(total, axis=1))
        columns = jnp.sum(placed[0] + pltpu.roll(placed[1], 64, 1), axis=0, keepdims=True)
        along_rows = jnp.sum(jnp.transpose(rows_sum[which]), axis=0, keepdims=True)
        first = (along_rows - columns[:, 0:256]) * factor
        second = -columns[:, 256:512] * factor
        low = jnp.where(zz == 0, first, second)
        high = jnp.where(zz == 0, second, first)
        pieces.extend([low[:, 0:128], low[:, 128:256], high[:, 0:128], high[:, 128:256]])
    value = jnp.concatenate(pieces, axis=0)
    if flip == 0:
        out[...] = value
    else:
        value = (value + refs[6][...]).astype(bf16)

        def copy(index, carry):
            out[index] = value
            return carry

        lax.fori_loop(0, out.shape[0], copy, 0, unroll=8)


def gradient_parts(flip, devices, freq, *arrays):
    out = jax.ShapeDtypeStruct((16, 128), f32)
    if flip:
        out = jax.ShapeDtypeStruct((devices, 16, 128), bf16)
    return pl.pallas_call(
        functools.partial(gradient_kernel, flip),
        in_specs=[SCALARS] + [WHOLE] * len(arrays),
        out_specs=WHOLE,
        scratch_shapes=[pltpu.VMEM((4, 256, 128), f32), pltpu.VMEM((4, 4, 8, 512), f32)],
        out_shape=out,
        compiler_params=pltpu.CompilerParams(vmem_limit_bytes=10 * MIB),
        cost_estimate=pl.CostEstimate(flops=5000000, bytes_accessed=3000000, transcendentals=0),
        name="gradient_parts%d" % flip,
    )(freq, *arrays)


def rows_kernel(resid, *refs):
    resids = refs[0:8]
    _, own_out, other_out, rolled = refs[8:]
    core, y, z = position()
    chip = z * 4 + y
    upper, lower = upper_mask()
    even = y % 2 == 0
    flip5 = jnp.where(y < 3, 1, 0)
    flip6 = jnp.where(y < 2, 1, 0)
    flip7 = jnp.where(y < 1, 1, 0)
    for moment in range(2):
        own = resid[moment]
        near = own[:, 0:64]
        near_t = jnp.transpose(near)
        zero = jnp.zeros_like(near)
        near_re = jnp.where(upper, near, jnp.where(lower, near_t, zero))
        near_im = jnp.where(lower, near, jnp.where(upper, -near_t, zero))
        far = own[:, 256:320]
        far_t = jnp.transpose(resids[4][moment][:, 256:320].astype(f32))
        far_re = jnp.where(z == 0, far, far_t)
        far_im = jnp.where(z == 0, -far_t, far)
        one5, two5, block6, one7, two7 = (
            jnp.where(flip == 1, resids[4 + rel][moment], resids[rel][moment]).astype(f32)
            for rel, flip in ((1, flip5), (2, flip5), (3, flip6), (1, flip7), (2, flip7))
        )
        block5 = jnp.where(even, one5, two5)
        block7 = jnp.where(even, two7, one7)
        re = [near_re, own[:, 64:256], far_re]
        im = [near_im, own[:, 320:512], far_im]
        for block, offset in ((block5, 3), (block6, 2), (block7, 1)):
            re.append(jnp.transpose(block[:, 64 * offset : 64 * offset + 64]))
            im.append(-jnp.transpose(block[:, 256 + 64 * offset : 320 + 64 * offset]))
        for part, pieces in enumerate((re, im)):
            index = moment * 2 + part
            rolled[index] = pltpu.roll(jnp.concatenate(pieces, axis=1), chip * 64, 1)
            own_out[index] = rolled[index, pl.ds(pl.multiple_of(core * 32, 32), 32), :]
            other_out[index] = rolled[index, pl.ds(pl.multiple_of((1 - core) * 32, 32), 32), :]


def whole_rows(resid, resids, after):
    return pl.pallas_call(
        rows_kernel,
        in_specs=[WHOLE] * 9 + [ANY],
        out_specs=[WHOLE] * 2,
        out_shape=[jax.ShapeDtypeStruct((4, 32, 512), f32)] * 2,
        scratch_shapes=[pltpu.VMEM((4, 64, 512), f32)],
        cost_estimate=pl.CostEstimate(flops=0, bytes_accessed=0, transcendentals=0),
        compiler_params=pltpu.CompilerParams(vmem_limit_bytes=6 * MIB),
        name="whole_rows",
    )(resid, *resids, after)


def assemble_kernel(own, other, out):
    core = position()[0]
    for channel, source in ((core, own), (1 - core, other)):
        for moment in range(2):
            for part in range(2):
                out[:, channel, moment, part, :] = source[moment * 2 + part]


def assemble(own, other, like):
    return pl.pallas_call(
        assemble_kernel,
        in_specs=[WHOLE] * 2,
        out_specs=WHOLE,
        out_shape=jax.ShapeDtypeStruct(like.shape, f32),
        compiler_params=pltpu.CompilerParams(vmem_limit_bytes=4 * MIB),
        cost_estimate=pl.CostEstimate(flops=0, bytes_accessed=0, transcendentals=0),
        name="assemble",
    )(own, other)


def halves(value):
    high = value.astype(bf16)
    return high, (value - high.astype(f32)).astype(bf16)


def update_kernel(grads, kernel, screen, out, total, smooth):
    core, y, z = position()
    per_chip = grads.shape[0] // 8
    for chip in range(8):
        total[chip * 16 : chip * 16 + 16, :] = jnp.sum(
            grads[chip * per_chip : (chip + 1) * per_chip].astype(f32), axis=0
        )
    gradient = jnp.concatenate(
        [total[pl.ds(piece, 32, stride=4), :] for piece in range(4)], axis=1
    )
    grad_high, grad_low = halves(gradient)
    kern_high, kern_low = halves(kernel[...])
    both = jnp.dot(
        jnp.concatenate([grad_high, grad_low], axis=0), kern_high, preferred_element_type=f32
    )
    value = both[0:32] + (
        both[32:64] + jnp.dot(grad_high, kern_low, preferred_element_type=f32)
    )
    mean_sq = jnp.sum(value * value) / value.size
    smooth[...] = value * (step_size * lax.rsqrt(mean_sq + epsilon))
    row = (z * 4 + y) * 4 + core * 2
    for step in range(2):
        out[step : step + 1, :] = screen[step : step + 1, :] - smooth[pl.ds(row + step, 1), :]


def updated_rows(grads, kernel, screen):
    return pl.pallas_call(
        update_kernel,
        in_specs=[WHOLE] * 3,
        out_specs=WHOLE,
        out_shape=jax.ShapeDtypeStruct(screen.shape, f32),
        scratch_shapes=[pltpu.VMEM((128, 128), f32), pltpu.VMEM((32, 512), f32)],
        compiler_params=pltpu.CompilerParams(vmem_limit_bytes=8 * MIB),
        cost_estimate=pl.CostEstimate(flops=200000000, bytes_accessed=1500000, transcendentals=0),
        name="updated_rows",
    )(grads, kernel, screen)


def body(
    observed,
    flags,
    screen,
    screen_kernel,
    station_uv,
    source_lm,
    source_flux,
    station_gain,
    source_direction,
    freq_ratio,
):
    devices = lax.axis_size("dir") * lax.axis_size("freq")
    stations = screen.shape[1]
    scaling = 1.0 / math.sqrt(source_flux.shape[0] * lax.axis_size("dir"))
    core = position()[0]
    swap = functools.partial(lax.ppermute, axis_name="dir", perm=dir_perm(0, flip_core=True))

    inputs = (freq_ratio, station_gain, station_uv, screen, source_lm, source_flux, source_direction)
    other = swap(phasor_send(*inputs))
    own = phasor_own(*inputs)

    def across(rel, array):
        return lax.ppermute(array, "dir", dir_perm(rel))

    def across_z(array):
        return lax.ppermute(array, "dir", dir_perm(0, flip_z=True))

    parts = model_parts(scaling, own, other)
    far = [across(rel, parts[rel]) for rel in (3, 2, 1)]
    near = [across(rel, parts[rel + 3]) for rel in (3, 2, 1)]
    other_observed = swap(observed_send(observed, flags, parts[6]))
    obs, kept = observed_parts(observed, flags, other_observed)
    directions0 = direction_parts(0, scaling, own, other, *parts[7:])
    last = across_z(send_parts(parts[0], *far))
    resid, half = residual_parts(parts[0], *near, last, obs, kept, directions0)
    half_z = across_z(half)
    directions1 = direction_parts(1, scaling, own, other, *parts[7:])
    resids = []
    for array in (half, half_z):
        three, two, one = (across(rel, array) for rel in (3, 2, 1))
        resids += [array, one, two, three]

    grads = gradient_parts(0, devices, freq_ratio, *resids[:4], directions0, directions1)
    grads = gradient_parts(1, devices, freq_ratio, *resids[4:], directions0, directions1, grads)
    own_rows, sent_rows = whole_rows(resid, resids, grads)
    other_rows = swap(sent_rows)
    grads = lax.all_to_all(grads, ("dir", "freq"), 0, 0, tiled=True)
    updated = updated_rows(grads, screen_kernel, screen)

    return assemble(own_rows, other_rows, observed), updated


def solution(mesh):
    placed = (
        P("dir", "freq", None, None, None),
        P("dir", None, None),
        P("dir", None),
        P(),
        P(),
        P(None, "dir"),
        P("dir"),
        P("freq", None, None, None, "dir"),
        P("dir"),
        P("freq"),
    )
    return jax.shard_map(
        body,
        mesh=mesh,
        in_specs=placed,
        out_specs=(P("dir", "freq", None, None, None), P("dir", None)),
        check_vma=False,
    )
```
